32 devices in a mesh: dp: 4 (over x, core), fsdp: 8 (over z, y).
Axes of the slice: x: 2, y: 2, z: 4, core: 2. Of those that a mesh axis runs over, the one named last changes fastest.
Arguments:
- tokens: bfloat16 [8192, 1024], P(('dp', 'fsdp')), may hold values from -6 to 6
- seq_lengths: int32 [128], P(('dp', 'fsdp')), may hold values from 0 to 256, as said below
- cotangent: bfloat16 [8192, 1024], P(('dp', 'fsdp')), may hold values from -6 to 6
- w_query: bfloat16 [1024, 1024], P(('dp', 'fsdp')), may hold values from -0.1875 to 0.1875
- w_latent: bfloat16 [1024, 512], P(('dp', 'fsdp')), may hold values from -0.1875 to 0.1875
- w_keyup: bfloat16 [512, 512], P(('dp', 'fsdp')), may hold values from -0.375 to 0.375
- w_valup: bfloat16 [512, 512], P(('dp', 'fsdp')), may hold values from -0.375 to 0.375
- w_output: bfloat16 [1024, 1024], P(('dp', 'fsdp')), may hold values from -1 to 1
- norm_attn: bfloat16 [1024], P(('dp', 'fsdp')), may hold values from 0.5 to 1.5
- norm_ffn: bfloat16 [1024], P(('dp', 'fsdp')), may hold values from 0.5 to 1.5
- w_gate: bfloat16 [1024, 2816], P(('dp', 'fsdp')), may hold values from -0.1875 to 0.1875
- w_up: bfloat16 [1024, 2816], P(('dp', 'fsdp')), may hold values from -0.1875 to 0.1875
- w_down: bfloat16 [2816, 1024], P(('dp', 'fsdp')), may hold values from -0.109375 to 0.109375
Outputs:
- block_out: bfloat16 [8192, 1024], P(('dp', 'fsdp'))
- grad_tokens: float32 [8192, 1024], P(('dp', 'fsdp'))
- grad_query: float32 [1024, 1024], P(('dp', 'fsdp'))
- grad_latent: float32 [1024, 512], P(('dp', 'fsdp'))
- grad_keyup: float32 [512, 512], P(('dp', 'fsdp'))
- grad_valup: float32 [512, 512], P(('dp', 'fsdp'))
- grad_output: float32 [1024, 1024], P(('dp', 'fsdp'))
- grad_norm_attn: float32 [1024], P(('dp', 'fsdp'))
- grad_norm_ffn: float32 [1024], P(('dp', 'fsdp'))
- grad_gate: float32 [1024, 2816], P(('dp', 'fsdp'))
- grad_up: float32 [1024, 2816], P(('dp', 'fsdp'))
- grad_down: float32 [2816, 1024], P(('dp', 'fsdp'))
The draws below stay inside these ranges and needn't reach their ends.
Inputs may be any that keep to these rules, and one draw needn't show every extreme that they name: `seq_lengths`: each device's 4 entries are sequence lengths that sum to at most 256; unused slots hold 0; in every draw some device holds one sequence of 256.
All inputs are finite; a program needn't handle non-finite values.
Results may differ from the reference program's by a relative error of at most 0.014.
Values may be sent and summed in bfloat16 or wider, within the bound.
A program may use at most 192 MiB of HBM per device.

```python
import jax
import jax.numpy as jnp
from jax import lax

D = 1024
FF = 2816
HEADS = 16
HEAD_DIM = 64
GROUPS = 2
LATENT = 256
TOK_DEV = 256
SEQS = 4
MIN_LEN = 64
TOKENS = 8192
SLOTS_ALL = 128


def draw_seq_lengths(key, part):
    key = jax.random.fold_in(key, 7)
    key_expo, key_jitter, key_pick = jax.random.split(key, 3)
    devices_count = SLOTS_ALL // SEQS
    span = max(TOK_DEV // MIN_LEN, 1).bit_length() - 1
    expo = jax.random.randint(key_expo, (devices_count, SEQS), 0, span + 1)
    base = jnp.left_shift(jnp.full((devices_count, SEQS), MIN_LEN, jnp.int32), expo.astype(jnp.int32))
    jitter = jax.random.randint(key_jitter, (devices_count, SEQS), 0, 2 ** 30) % base
    wanted = jnp.minimum(base + jitter, TOK_DEV).astype(jnp.int32)
    ends = jnp.minimum(jnp.cumsum(wanted, axis=1), TOK_DEV).astype(jnp.int32)
    starts = jnp.concatenate([jnp.zeros((devices_count, 1), jnp.int32), ends[:, :-1]], axis=1)
    lengths = ends - starts
    chosen = jax.random.randint(key_pick, (), 0, devices_count)
    full_row = jnp.where(jnp.arange(SEQS) == 0, TOK_DEV, 0).astype(jnp.int32)
    lengths = jnp.where((jnp.arange(devices_count) == chosen)[:, None], full_row[None, :], lengths)
    return lengths.reshape(-1).astype(jnp.int32)


def block_scale(key, extent, cuts, smallest, high):
    def one(axis_at, shards_of):
        draws = jax.random.uniform(jax.random.fold_in(jax.random.fold_in(key, 6), axis_at), (shards_of,), jnp.float32, smallest / len(cuts), high / len(cuts))
        return jnp.repeat(jnp.exp(draws), extent[axis_at] // shards_of).reshape((-1,) + (1,) * (len(extent) - axis_at - 1))

    level = one(*cuts[0])
    for cut in cuts[1:]:
        level = level * one(*cut)
    return level


def gaussian(stream_key, dims, scale, bound, cuts=(), kind=jnp.bfloat16):
    values = scale * jax.random.normal(stream_key, dims, jnp.float32)
    if cuts:
        values = values * block_scale(stream_key, dims, cuts, -0.22, 0.18)
    return jnp.clip(values, -bound, bound).astype(kind)


def setup_inputs(seed: int = 0) -> dict:
    key_of = jax.random.split(jax.random.key(seed), 14)
    return {
        "tokens": gaussian(key_of[0], (TOKENS, D), 1.0, 6.0, ((0, 32),)),
        "seq_lengths": draw_seq_lengths(jax.random.fold_in(key_of[13], 71), 0),
        "cotangent": gaussian(key_of[2], (TOKENS, D), 1.0, 6.0, ((0, 32),)),
        "w_query": gaussian(key_of[3], (D, HEADS * HEAD_DIM), D ** -0.5, 0.1875, ((0, 32),)),
        "w_latent": gaussian(key_of[4], (D, GROUPS * LATENT), D ** -0.5, 0.1875, ((0, 32),)),
        "w_keyup": gaussian(key_of[5], (GROUPS * LATENT, HEADS // GROUPS * HEAD_DIM), LATENT ** -0.5, 0.375, ((0, 32),)),
        "w_valup": gaussian(key_of[6], (GROUPS * LATENT, HEADS // GROUPS * HEAD_DIM), LATENT ** -0.5, 0.375, ((0, 32),)),
        "w_output": gaussian(key_of[7], (HEADS * HEAD_DIM, D), (HEADS * HEAD_DIM // 32) ** -0.5, 1.0, ((0, 32),)),
        "norm_attn": jnp.clip(1.0 + 0.1 * jax.random.normal(key_of[8], (D,), jnp.float32), 0.5, 1.5).astype(jnp.bfloat16),
        "norm_ffn": jnp.clip(1.0 + 0.1 * jax.random.normal(key_of[9], (D,), jnp.float32), 0.5, 1.5).astype(jnp.bfloat16),
        "w_gate": gaussian(key_of[10], (D, FF), D ** -0.5, 0.1875, ((0, 32),)),
        "w_up": gaussian(key_of[11], (D, FF), D ** -0.5, 0.1875, ((0, 32),)),
        "w_down": gaussian(key_of[12], (FF, D), FF ** -0.5, 0.109375, ((0, 32),)),
    }


@jax.custom_vjp
def low(v):
    return lax.optimization_barrier(v.astype(jnp.bfloat16)).astype(jnp.float32)

@jax.custom_vjp
def low_back(v):
    return v

def low_keep(v):
    return (low(v), None)

def low_pass(kept, grad):
    return (grad,)

def back_keep(v):
    return (v, None)

def back_low(kept, grad):
    return (low(grad),)
low.defvjp(low_keep, low_pass)
low_back.defvjp(back_keep, back_low)
EPSILON = 1e-06

def dense(left, right):
    return jnp.dot(left, right, precision=lax.Precision.HIGHEST, preferred_element_type=jnp.float32)

def rounded_both(value):
    return low(low_back(value))

def bucket_layer(inputs, lengths, params):
    w_query, w_latent, w_keyup, w_valup, w_output, gain_one, gain_two, w_gate, w_up, w_down = params
    rows = inputs.shape[0]
    position = jnp.arange(rows, dtype=jnp.int32)
    ends = jnp.cumsum(lengths).astype(jnp.int32)
    segment = lax.optimization_barrier(jnp.sum((position[None, :] >= ends[:, None]).astype(jnp.int32), axis=0))
    allowed = (segment[:, None] == segment[None, :]) & (position[None, :] <= position[:, None])
    rstd_one = lax.rsqrt(lax.optimization_barrier(jnp.mean(inputs * inputs, axis=1, keepdims=True)) + EPSILON)
    normed = low(inputs * rstd_one * gain_one)
    query = rounded_both(dense(normed, w_query))
    latent = rounded_both(dense(normed, w_latent))
    lat3 = latent.reshape(rows, GROUPS, LATENT)
    keys = rounded_both(jnp.einsum('tgl,glf->tgf', lat3, w_keyup.reshape(GROUPS, LATENT, -1), precision=lax.Precision.HIGHEST))
    values = rounded_both(jnp.einsum('tgl,glf->tgf', lat3, w_valup.reshape(GROUPS, LATENT, -1), precision=lax.Precision.HIGHEST))
    query3 = query.reshape(rows, HEADS, HEAD_DIM)
    keys3 = keys.reshape(rows, HEADS, HEAD_DIM)
    values3 = values.reshape(rows, HEADS, HEAD_DIM)
    scores = jnp.einsum('qhd,khd->hqk', query3, keys3, precision=lax.Precision.HIGHEST) * HEAD_DIM ** (-0.5)
    scores = low_back(scores)
    scores = jnp.where(allowed[None, :, :], scores, -1e+30)
    peak = lax.optimization_barrier(jnp.max(scores, axis=2, keepdims=True))
    expo = jnp.exp(scores - peak)
    probs = low(expo / lax.optimization_barrier(jnp.sum(expo, axis=2, keepdims=True)))
    attended = jnp.einsum('hqk,khd->qhd', probs, values3, precision=lax.Precision.HIGHEST)
    merged = rounded_both(attended.reshape(rows, HEADS * HEAD_DIM))
    middle = inputs + low_back(dense(merged, w_output))
    rstd_two = lax.rsqrt(lax.optimization_barrier(jnp.mean(middle * middle, axis=1, keepdims=True)) + EPSILON)
    normed_two = low(middle * rstd_two * gain_two)
    gate = low_back(dense(normed_two, w_gate))
    upper = low_back(dense(normed_two, w_up))
    mixed = low(jax.nn.silu(gate) * upper)
    return middle + low_back(dense(mixed, w_down))

def reference(tokens, seq_lengths, cotangent, w_query, w_latent, w_keyup, w_valup, w_output, norm_attn, norm_ffn, w_gate, w_up, w_down):
    inputs = tokens.astype(jnp.float32)
    params = tuple((p.astype(jnp.float32) for p in (w_query, w_latent, w_keyup, w_valup, w_output, norm_attn, norm_ffn, w_gate, w_up, w_down)))
    lengths = seq_lengths.reshape(-1, SEQS).astype(jnp.int32)

    def forward(values, *weights):
        blocks = values.reshape(-1, TOK_DEV, D)

        def one_bucket(operands):
            return bucket_layer(operands[0], operands[1], weights)
        outs = lax.map(jax.checkpoint(one_bucket), (blocks, lengths))
        return outs.reshape(-1, D)
    result, pullback = jax.vjp(forward, inputs, *params)
    totals = lax.optimization_barrier(jnp.sum(lengths, axis=1)).astype(jnp.int32)
    valid = (jnp.arange(TOK_DEV, dtype=jnp.int32)[None, :] < totals[:, None]).reshape(-1)
    dout = cotangent.astype(jnp.float32) * valid[:, None].astype(jnp.float32)
    grads = pullback(dout)
    return (result.astype(jnp.bfloat16), grads[0], grads[1], grads[2], grads[3], grads[4], grads[5], grads[6], grads[7], grads[8], grads[9], grads[10])
```

```python
import jax
import jax.numpy as jnp
from jax import lax
from jax.sharding import PartitionSpec as P

HEADS = 16
HEAD_DIM = 64
GROUPS = 2
LATENT = 256


EPSILON = 1e-06


def matmul(left, right):
    return jnp.dot(left, right, preferred_element_type=jnp.float32)


def matmul_left(left, right):
    return lax.dot_general(
        left, right, (((0,), (0,)), ((), ())), preferred_element_type=jnp.float32
    )


def matmul_right(left, right):
    return lax.dot_general(
        left, right, (((1,), (1,)), ((), ())), preferred_element_type=jnp.float32
    )


def segment_mask(lengths, rows):
    position = jnp.arange(rows, dtype=jnp.int32)
    ends = jnp.cumsum(lengths)
    segment = jnp.sum((position[None, :] >= ends[:, None]).astype(jnp.int32), axis=0)
    allowed = (segment[:, None] == segment[None, :]) & (position[None, :] <= position[:, None])
    valid = (position < ends[-1]).astype(jnp.float32)
    return (allowed, valid)


def head_forward(allowed, scale):

    def one_head(operands):
        query, key_rows, value_rows = operands
        scores = jnp.where(allowed, matmul_right(query, key_rows) * scale, -1e30)
        peak = jnp.max(scores, axis=1, keepdims=True)
        expo = jnp.exp(scores - peak)
        total = jnp.sum(expo, axis=1, keepdims=True)
        weights = (expo / total).astype(jnp.bfloat16)
        result = matmul(weights, value_rows).astype(jnp.bfloat16)
        return (result, peak[:, 0] + jnp.log(total[:, 0]))

    return one_head


def head_backward(allowed, scale):

    def one_head(operands):
        query, key_rows, value_rows, grad_out, logsum = operands
        scores = jnp.where(allowed, matmul_right(query, key_rows) * scale, -1e30)
        probs = jnp.exp(scores - logsum[:, None])
        grad_value = matmul_left(probs.astype(jnp.bfloat16), grad_out)
        grad_probs = matmul_right(grad_out, value_rows)
        inner = jnp.sum(probs * grad_probs, axis=1, keepdims=True)
        grad_scores = (probs * (grad_probs - inner)).astype(jnp.bfloat16)
        grad_query = matmul(grad_scores, key_rows) * scale
        grad_key = matmul_left(grad_scores, query) * scale
        return (grad_query, grad_key, grad_value)

    return one_head


def norm_back(grad_normed, inputs, rstd, gain):
    scaled = grad_normed * gain
    grad_in = rstd * (
        scaled - inputs * rstd * rstd * jnp.mean(scaled * inputs, axis=1, keepdims=True)
    )
    grad_gain = jnp.sum(grad_normed * inputs * rstd, axis=0)
    return (grad_in, grad_gain)


def column_term(left, right):
    return matmul_left(left, right).astype(jnp.bfloat16)


def forward(tokens, allowed, attn_w, ffn_w):
    w_query, w_latent, w_keyup, w_valup, w_output, gain_one = attn_w
    gain_two, w_gate, w_up, w_down = ffn_w
    rows = tokens.shape[0]
    inputs = tokens.astype(jnp.float32)
    rstd_one = lax.rsqrt(jnp.mean(inputs * inputs, axis=1, keepdims=True) + EPSILON)
    normed = (inputs * rstd_one * gain_one.astype(jnp.float32)).astype(jnp.bfloat16)
    query = matmul(normed, w_query).astype(jnp.bfloat16)
    latent = matmul(normed, w_latent).astype(jnp.bfloat16)
    lat3 = latent.reshape(rows, GROUPS, LATENT)
    keys = jnp.einsum(
        "tgl,glf->tgf",
        lat3,
        w_keyup.reshape(GROUPS, LATENT, -1),
        preferred_element_type=jnp.float32,
    ).astype(jnp.bfloat16)
    values = jnp.einsum(
        "tgl,glf->tgf",
        lat3,
        w_valup.reshape(GROUPS, LATENT, -1),
        preferred_element_type=jnp.float32,
    ).astype(jnp.bfloat16)
    heads_query = query.reshape(rows, HEADS, HEAD_DIM).transpose(1, 0, 2)
    heads_key = keys.reshape(rows, HEADS, HEAD_DIM).transpose(1, 0, 2)
    heads_value = values.reshape(rows, HEADS, HEAD_DIM).transpose(1, 0, 2)
    attended, logsum = lax.map(
        head_forward(allowed, HEAD_DIM ** (-0.5)), (heads_query, heads_key, heads_value)
    )
    merged = attended.transpose(1, 0, 2).reshape(rows, HEADS * HEAD_DIM)
    middle = inputs + matmul(merged, w_output)
    rstd_two = lax.rsqrt(jnp.mean(middle * middle, axis=1, keepdims=True) + EPSILON)
    normed_two = (middle * rstd_two * gain_two.astype(jnp.float32)).astype(jnp.bfloat16)
    gate = matmul(normed_two, w_gate)
    upper = matmul(normed_two, w_up)
    mixed = (jax.nn.silu(gate) * upper).astype(jnp.bfloat16)
    result = middle + matmul(mixed, w_down)
    return (
        result,
        inputs,
        rstd_one,
        normed,
        lat3,
        heads_query,
        heads_key,
        heads_value,
        logsum,
        merged,
        middle,
        rstd_two,
        normed_two,
        gate,
        upper,
        mixed,
    )


def on_device(
    tokens,
    seq_lengths,
    cotangent,
    w_query,
    w_latent,
    w_keyup,
    w_valup,
    w_output,
    norm_attn,
    norm_ffn,
    w_gate,
    w_up,
    w_down,
):
    rows = tokens.shape[0]
    allowed, valid = segment_mask(seq_lengths, rows)
    attn_w = (
        lax.all_gather(w_query, ("dp", "fsdp"), axis=0, tiled=True),
        lax.all_gather(w_latent, ("dp", "fsdp"), axis=0, tiled=True),
        lax.all_gather(w_keyup, ("dp", "fsdp"), axis=0, tiled=True),
        lax.all_gather(w_valup, ("dp", "fsdp"), axis=0, tiled=True),
        lax.all_gather(w_output, ("dp", "fsdp"), axis=0, tiled=True),
        lax.all_gather(norm_attn, ("dp", "fsdp"), axis=0, tiled=True),
    )
    ffn_w = (
        lax.all_gather(norm_ffn, ("dp", "fsdp"), axis=0, tiled=True),
        lax.all_gather(w_gate, ("dp", "fsdp"), axis=0, tiled=True),
        lax.all_gather(w_up, ("dp", "fsdp"), axis=0, tiled=True),
        lax.all_gather(w_down, ("dp", "fsdp"), axis=0, tiled=True),
    )
    saved = forward(tokens, allowed, attn_w, ffn_w)
    block_out = saved[0].astype(jnp.bfloat16)
    (
        result,
        inputs,
        rstd_one,
        normed,
        lat3,
        heads_query,
        heads_key,
        heads_value,
        logsum,
        merged,
        middle,
        rstd_two,
        normed_two,
        gate,
        upper,
        mixed,
    ) = saved
    full_query, full_latent, full_keyup, full_valup, full_output, gain_one = attn_w
    gain_two, full_gate, full_up, full_down = ffn_w
    ff_width = full_gate.shape[1]
    grad_out = cotangent.astype(jnp.float32) * valid[:, None]
    grad_low = grad_out.astype(jnp.bfloat16)
    grad_mixed = matmul_right(grad_low, full_down)
    sigmoid_gate = jax.nn.sigmoid(gate)
    grad_gate_low = (
        grad_mixed * upper * sigmoid_gate * (1.0 + gate * (1.0 - sigmoid_gate))
    ).astype(jnp.bfloat16)
    grad_upper_low = (grad_mixed * jax.nn.silu(gate)).astype(jnp.bfloat16)
    grad_normed_two = matmul_right(grad_gate_low, full_gate) + matmul_right(grad_upper_low, full_up)
    grad_mid_norm, grad_gain_two = norm_back(
        grad_normed_two, middle, rstd_two, gain_two.astype(jnp.float32)
    )
    grad_middle = grad_out + grad_mid_norm
    down_own = lax.psum_scatter(
        column_term(mixed, grad_low), ("dp", "fsdp"), scatter_dimension=0, tiled=True
    )
    packed_ffn = jnp.concatenate([grad_gate_low, grad_upper_low], axis=1)
    ffn_own = lax.psum_scatter(
        column_term(normed_two, packed_ffn), ("dp", "fsdp"), scatter_dimension=0, tiled=True
    )
    grad_branch = grad_middle.astype(jnp.bfloat16)
    grad_merged = matmul_right(grad_branch, full_output).astype(jnp.bfloat16)
    output_own = lax.psum_scatter(
        column_term(merged, grad_branch), ("dp", "fsdp"), scatter_dimension=0, tiled=True
    )
    heads_grad = grad_merged.reshape(rows, HEADS, HEAD_DIM).transpose(1, 0, 2)
    grad_hq, grad_hk, grad_hv = lax.map(
        head_backward(allowed, HEAD_DIM ** (-0.5)),
        (heads_query, heads_key, heads_value, heads_grad, logsum),
    )
    grad_query_low = grad_hq.transpose(1, 0, 2).reshape(rows, HEADS * HEAD_DIM).astype(jnp.bfloat16)
    grad_keys_low = grad_hk.transpose(1, 0, 2).reshape(rows, GROUPS, -1).astype(jnp.bfloat16)
    grad_values_low = grad_hv.transpose(1, 0, 2).reshape(rows, GROUPS, -1).astype(jnp.bfloat16)
    head_cols = grad_keys_low.shape[2]
    keyup3 = full_keyup.reshape(GROUPS, LATENT, -1)
    valup3 = full_valup.reshape(GROUPS, LATENT, -1)
    grad_lat = jnp.einsum("tgf,glf->tgl", grad_keys_low, keyup3, preferred_element_type=jnp.float32)
    grad_lat = grad_lat + jnp.einsum(
        "tgf,glf->tgl", grad_values_low, valup3, preferred_element_type=jnp.float32
    )
    grad_latent_low = grad_lat.reshape(rows, GROUPS * LATENT).astype(jnp.bfloat16)
    latent_flat = lat3.reshape(rows, GROUPS * LATENT)
    paired = jnp.concatenate([grad_keys_low, grad_values_low], axis=2).reshape(
        rows, GROUPS * 2 * head_cols
    )
    count = w_keyup.shape[0] * lax.axis_size(("dp", "fsdp"))
    product = matmul_left(latent_flat, paired).reshape(count, GROUPS, 2 * head_cols)
    owner = jnp.arange(count, dtype=jnp.int32) // LATENT
    picker = (owner[:, None] == jnp.arange(GROUPS, dtype=jnp.int32)[None, :]).astype(jnp.float32)
    latent_own = lax.psum_scatter(
        jnp.sum(product * picker[:, :, None], axis=1).astype(jnp.bfloat16),
        ("dp", "fsdp"),
        scatter_dimension=0,
        tiled=True,
    )
    grad_normed = matmul_right(grad_query_low, full_query) + matmul_right(
        grad_latent_low, full_latent
    )
    packed_attn = jnp.concatenate([grad_query_low, grad_latent_low], axis=1)
    attn_own = lax.psum_scatter(
        column_term(normed, packed_attn), ("dp", "fsdp"), scatter_dimension=0, tiled=True
    )
    grad_in_norm, grad_gain_one = norm_back(
        grad_normed, inputs, rstd_one, gain_one.astype(jnp.float32)
    )
    grad_tokens = grad_middle + grad_in_norm
    gains_own = (
        lax.psum_scatter(grad_gain_one, ("dp", "fsdp"), scatter_dimension=0, tiled=True),
        lax.psum_scatter(grad_gain_two, ("dp", "fsdp"), scatter_dimension=0, tiled=True),
    )
    query_cols = HEADS * HEAD_DIM
    return (
        block_out,
        grad_tokens,
        attn_own[:, :query_cols].astype(jnp.float32),
        attn_own[:, query_cols:].astype(jnp.float32),
        latent_own[:, :head_cols].astype(jnp.float32),
        latent_own[:, head_cols:].astype(jnp.float32),
        output_own.astype(jnp.float32),
        gains_own[0],
        gains_own[1],
        ffn_own[:, :ff_width].astype(jnp.float32),
        ffn_own[:, ff_width:].astype(jnp.float32),
        down_own.astype(jnp.float32),
    )


def solution(mesh):
    return jax.shard_map(
        on_device,
        mesh=mesh,
        in_specs=(
            P(("dp", "fsdp"), None),
            P(("dp", "fsdp")),
            P(("dp", "fsdp"), None),
            P(("dp", "fsdp"), None),
            P(("dp", "fsdp"), None),
            P(("dp", "fsdp"), None),
            P(("dp", "fsdp"), None),
            P(("dp", "fsdp"), None),
            P(("dp", "fsdp")),
            P(("dp", "fsdp")),
            P(("dp", "fsdp"), None),
            P(("dp", "fsdp"), None),
            P(("dp", "fsdp"), None),
        ),
        out_specs=(
            P(("dp", "fsdp"), None),
            P(("dp", "fsdp"), None),
            P(("dp", "fsdp"), None),
            P(("dp", "fsdp"), None),
            P(("dp", "fsdp"), None),
            P(("dp", "fsdp"), None),
            P(("dp", "fsdp"), None),
            P(("dp", "fsdp")),
            P(("dp", "fsdp")),
            P(("dp", "fsdp"), None),
            P(("dp", "fsdp"), None),
            P(("dp", "fsdp"), None),
        ),
        check_vma=False,
    )
```

```python
import jax
import jax.numpy as jnp
from jax import lax
from jax.experimental import pallas as pl
from jax.experimental.pallas import tpu as pltpu
from jax.sharding import PartitionSpec as P

HEADS = 16
HEAD_DIM = 64
GROUPS = 2
LATENT = 256


EPSILON = 1e-06


def matmul(left, right):
    return jnp.dot(left, right, preferred_element_type=jnp.float32)


def matmul_left(left, right):
    return lax.dot_general(
        left, right, (((0,), (0,)), ((), ())), preferred_element_type=jnp.float32
    )


def matmul_right(left, right):
    return lax.dot_general(
        left, right, (((1,), (1,)), ((), ())), preferred_element_type=jnp.float32
    )


def segment_mask(lengths, rows):
    position = jnp.arange(rows, dtype=jnp.int32)
    ends = jnp.cumsum(lengths)
    segment = jnp.sum((position[None, :] >= ends[:, None]).astype(jnp.int32), axis=0)
    allowed = (segment[:, None] == segment[None, :]) & (position[None, :] <= position[:, None])
    valid = (position < ends[-1]).astype(jnp.float32)
    return (allowed, valid)


def head_forward(allowed, scale):

    def one_head(operands):
        query, key_rows, value_rows = operands
        scores = jnp.where(allowed, matmul_right(query, key_rows) * scale, -1e30)
        peak = jnp.max(scores, axis=1, keepdims=True)
        expo = jnp.exp(scores - peak)
        total = jnp.sum(expo, axis=1, keepdims=True)
        weights = (expo / total).astype(jnp.bfloat16)
        result = matmul(weights, value_rows).astype(jnp.bfloat16)
        return (result, peak[:, 0] + jnp.log(total[:, 0]))

    return one_head


def head_backward(allowed, scale):

    def one_head(operands):
        query, key_rows, value_rows, grad_out, logsum = operands
        scores = jnp.where(allowed, matmul_right(query, key_rows) * scale, -1e30)
        probs = jnp.exp(scores - logsum[:, None])
        grad_value = matmul_left(probs.astype(jnp.bfloat16), grad_out)
        grad_probs = matmul_right(grad_out, value_rows)
        inner = jnp.sum(probs * grad_probs, axis=1, keepdims=True)
        grad_scores = (probs * (grad_probs - inner)).astype(jnp.bfloat16)
        grad_query = matmul(grad_scores, key_rows) * scale
        grad_key = matmul_left(grad_scores, query) * scale
        return (grad_query, grad_key, grad_value)

    return one_head


def norm_back(grad_normed, inputs, rstd, gain):
    scaled = grad_normed * gain
    grad_in = rstd * (
        scaled - inputs * rstd * rstd * jnp.mean(scaled * inputs, axis=1, keepdims=True)
    )
    grad_gain = jnp.sum(grad_normed * inputs * rstd, axis=0)
    return (grad_in, grad_gain)


def column_term(left, right):
    return matmul_left(left, right).astype(jnp.bfloat16)


def forward(tokens, allowed, attn_w, ffn_w):
    w_query, w_latent, w_keyup, w_valup, w_output, gain_one = attn_w
    gain_two, w_gate, w_up, w_down = ffn_w
    rows = tokens.shape[0]
    inputs = tokens.astype(jnp.float32)
    rstd_one = lax.rsqrt(jnp.mean(inputs * inputs, axis=1, keepdims=True) + EPSILON)
    normed = (inputs * rstd_one * gain_one.astype(jnp.float32)).astype(jnp.bfloat16)
    query = matmul(normed, w_query).astype(jnp.bfloat16)
    latent = matmul(normed, w_latent).astype(jnp.bfloat16)
    lat3 = latent.reshape(rows, GROUPS, LATENT)
    keys = jnp.einsum(
        "tgl,glf->tgf",
        lat3,
        w_keyup.reshape(GROUPS, LATENT, -1),
        preferred_element_type=jnp.float32,
    ).astype(jnp.bfloat16)
    values = jnp.einsum(
        "tgl,glf->tgf",
        lat3,
        w_valup.reshape(GROUPS, LATENT, -1),
        preferred_element_type=jnp.float32,
    ).astype(jnp.bfloat16)
    heads_query = query.reshape(rows, HEADS, HEAD_DIM).transpose(1, 0, 2)
    heads_key = keys.reshape(rows, HEADS, HEAD_DIM).transpose(1, 0, 2)
    heads_value = values.reshape(rows, HEADS, HEAD_DIM).transpose(1, 0, 2)
    attended, logsum = lax.map(
        head_forward(allowed, HEAD_DIM ** (-0.5)), (heads_query, heads_key, heads_value)
    )
    merged = attended.transpose(1, 0, 2).reshape(rows, HEADS * HEAD_DIM)
    middle = inputs + matmul(merged, w_output)
    rstd_two = lax.rsqrt(jnp.mean(middle * middle, axis=1, keepdims=True) + EPSILON)
    normed_two = (middle * rstd_two * gain_two.astype(jnp.float32)).astype(jnp.bfloat16)
    gate = matmul(normed_two, w_gate)
    upper = matmul(normed_two, w_up)
    mixed = (jax.nn.silu(gate) * upper).astype(jnp.bfloat16)
    result = middle + matmul(mixed, w_down)
    return (
        result,
        inputs,
        rstd_one,
        normed,
        lat3,
        heads_query,
        heads_key,
        heads_value,
        logsum,
        merged,
        middle,
        rstd_two,
        normed_two,
        gate,
        upper,
        mixed,
    )


def on_device(
    tokens,
    seq_lengths,
    cotangent,
    w_query,
    w_latent,
    w_keyup,
    w_valup,
    w_output,
    norm_attn,
    norm_ffn,
    w_gate,
    w_up,
    w_down,
):
    rows = tokens.shape[0]
    allowed, valid = segment_mask(seq_lengths, rows)
    attn_w = (
        lax.all_gather(w_query, ("dp", "fsdp"), axis=0, tiled=True),
        lax.all_gather(w_latent, ("dp", "fsdp"), axis=0, tiled=True),
        lax.all_gather(w_keyup, ("dp", "fsdp"), axis=0, tiled=True),
        lax.all_gather(w_valup, ("dp", "fsdp"), axis=0, tiled=True),
        lax.all_gather(w_output, ("dp", "fsdp"), axis=0, tiled=True),
        lax.all_gather(norm_attn, ("dp", "fsdp"), axis=0, tiled=True),
    )
    ffn_w = (
        lax.all_gather(norm_ffn, ("dp", "fsdp"), axis=0, tiled=True),
        lax.all_gather(w_gate, ("dp", "fsdp"), axis=0, tiled=True),
        lax.all_gather(w_up, ("dp", "fsdp"), axis=0, tiled=True),
        lax.all_gather(w_down, ("dp", "fsdp"), axis=0, tiled=True),
    )
    saved = forward(tokens, allowed, attn_w, ffn_w)
    block_out = saved[0].astype(jnp.bfloat16)
    (
        result,
        inputs,
        rstd_one,
        normed,
        lat3,
        heads_query,
        heads_key,
        heads_value,
        logsum,
        merged,
        middle,
        rstd_two,
        normed_two,
        gate,
        upper,
        mixed,
    ) = saved
    full_query, full_latent, full_keyup, full_valup, full_output, gain_one = attn_w
    gain_two, full_gate, full_up, full_down = ffn_w
    ff_width = full_gate.shape[1]
    grad_out = cotangent.astype(jnp.float32) * valid[:, None]
    grad_low = grad_out.astype(jnp.bfloat16)
    grad_mixed = matmul_right(grad_low, full_down)
    sigmoid_gate = jax.nn.sigmoid(gate)
    grad_gate_low = (
        grad_mixed * upper * sigmoid_gate * (1.0 + gate * (1.0 - sigmoid_gate))
    ).astype(jnp.bfloat16)
    grad_upper_low = (grad_mixed * jax.nn.silu(gate)).astype(jnp.bfloat16)
    grad_normed_two = matmul_right(grad_gate_low, full_gate) + matmul_right(grad_upper_low, full_up)
    grad_mid_norm, grad_gain_two = norm_back(
        grad_normed_two, middle, rstd_two, gain_two.astype(jnp.float32)
    )
    grad_middle = grad_out + grad_mid_norm
    down_own = lax.psum_scatter(
        column_term(mixed, grad_low), ("dp", "fsdp"), scatter_dimension=0, tiled=True
    )
    packed_ffn = jnp.concatenate([grad_gate_low, grad_upper_low], axis=1)
    ffn_own = lax.psum_scatter(
        column_term(normed_two, packed_ffn), ("dp", "fsdp"), scatter_dimension=0, tiled=True
    )
    grad_branch = grad_middle.astype(jnp.bfloat16)
    grad_merged = matmul_right(grad_branch, full_output).astype(jnp.bfloat16)
    output_own = lax.psum_scatter(
        column_term(merged, grad_branch), ("dp", "fsdp"), scatter_dimension=0, tiled=True
    )
    heads_grad = grad_merged.reshape(rows, HEADS, HEAD_DIM).transpose(1, 0, 2)
    grad_hq, grad_hk, grad_hv = lax.map(
        head_backward(allowed, HEAD_DIM ** (-0.5)),
        (heads_query, heads_key, heads_value, heads_grad, logsum),
    )
    grad_query_low = grad_hq.transpose(1, 0, 2).reshape(rows, HEADS * HEAD_DIM).astype(jnp.bfloat16)
    grad_keys_low = grad_hk.transpose(1, 0, 2).reshape(rows, GROUPS, -1).astype(jnp.bfloat16)
    grad_values_low = grad_hv.transpose(1, 0, 2).reshape(rows, GROUPS, -1).astype(jnp.bfloat16)
    head_cols = grad_keys_low.shape[2]
    keyup3 = full_keyup.reshape(GROUPS, LATENT, -1)
    valup3 = full_valup.reshape(GROUPS, LATENT, -1)
    grad_lat = jnp.einsum("tgf,glf->tgl", grad_keys_low, keyup3, preferred_element_type=jnp.float32)
    grad_lat = grad_lat + jnp.einsum(
        "tgf,glf->tgl", grad_values_low, valup3, preferred_element_type=jnp.float32
    )
    grad_latent_low = grad_lat.reshape(rows, GROUPS * LATENT).astype(jnp.bfloat16)
    latent_flat = lat3.reshape(rows, GROUPS * LATENT)
    paired = jnp.concatenate([grad_keys_low, grad_values_low], axis=2).reshape(
        rows, GROUPS * 2 * head_cols
    )
    count = w_keyup.shape[0] * lax.axis_size(("dp", "fsdp"))
    product = matmul_left(latent_flat, paired).reshape(count, GROUPS, 2 * head_cols)
    owner = jnp.arange(count, dtype=jnp.int32) // LATENT
    picker = (owner[:, None] == jnp.arange(GROUPS, dtype=jnp.int32)[None, :]).astype(jnp.float32)
    latent_own = lax.psum_scatter(
        jnp.sum(product * picker[:, :, None], axis=1).astype(jnp.bfloat16),
        ("dp", "fsdp"),
        scatter_dimension=0,
        tiled=True,
    )
    grad_normed = matmul_right(grad_query_low, full_query) + matmul_right(
        grad_latent_low, full_latent
    )
    packed_attn = jnp.concatenate([grad_query_low, grad_latent_low], axis=1)
    attn_own = lax.psum_scatter(
        column_term(normed, packed_attn), ("dp", "fsdp"), scatter_dimension=0, tiled=True
    )
    grad_in_norm, grad_gain_one = norm_back(
        grad_normed, inputs, rstd_one, gain_one.astype(jnp.float32)
    )
    grad_tokens = grad_middle + grad_in_norm
    gains_own = (
        lax.psum_scatter(grad_gain_one, ("dp", "fsdp"), scatter_dimension=0, tiled=True),
        lax.psum_scatter(grad_gain_two, ("dp", "fsdp"), scatter_dimension=0, tiled=True),
    )
    query_cols = HEADS * HEAD_DIM
    return (
        block_out,
        grad_tokens,
        attn_own[:, :query_cols].astype(jnp.float32),
        attn_own[:, query_cols:].astype(jnp.float32),
        latent_own[:, :head_cols].astype(jnp.float32),
        latent_own[:, head_cols:].astype(jnp.float32),
        output_own.astype(jnp.float32),
        gains_own[0],
        gains_own[1],
        ffn_own[:, :ff_width].astype(jnp.float32),
        ffn_own[:, ff_width:].astype(jnp.float32),
        down_own.astype(jnp.float32),
    )


MESH = pl.DeviceIdType.MESH
F32 = jnp.float32
BF16 = jnp.bfloat16
SCALE = HEAD_DIM ** (-0.5)
ROWS = 256
WIDTH = 1024
HALF = 1408
DOWN = 88
PAD = 96
CHUNKS = ((0, 512), (512, 512), (1024, 384))


class Slots:
    def __init__(self):
        self.count = 0

    def take(self, number):
        first = self.count
        self.count += number
        return first


SLOTS = Slots()
S_GAIN = SLOTS.take(5)
S_AY = SLOTS.take(1)
S_AZ = SLOTS.take(12)
S_AX = SLOTS.take(8)
S_AS = SLOTS.take(16)
S_HALF = SLOTS.take(2)
S_FZ = [SLOTS.take(6) for _ in range(3)]
S_FY = [SLOTS.take(4) for _ in range(3)]
S_FS = [SLOTS.take(8) for _ in range(3)]
S_COT = SLOTS.take(1)
S_N2 = SLOTS.take(1)
S_DN2 = SLOTS.take(1)
S_OUT = SLOTS.take(1)
S_RS = [SLOTS.take(2) for _ in range(3)]
S_RY = [SLOTS.take(4) for _ in range(3)]
S_RZ = [SLOTS.take(8) for _ in range(3)]
S_RX = SLOTS.take(2)
S_BS = [SLOTS.take(2) for _ in range(2)]
S_BX = [SLOTS.take(4) for _ in range(2)]
S_BZ = [SLOTS.take(8) for _ in range(2)]
S_BY = [SLOTS.take(1) for _ in range(2)]
S_SUM = SLOTS.take(5)
S_LOCAL = 8


def nn(left, right):
    return jnp.dot(left, right, preferred_element_type=F32)


def nt(left, right):
    return lax.dot_general(left, right, (((1,), (1,)), ((), ())), preferred_element_type=F32)


def tn(left, right):
    return lax.dot_general(left, right, (((0,), (0,)), ((), ())), preferred_element_type=F32)


def layer_kernel(
    tok_hbm, len_ref, cot_hbm, wq_hbm, wl_hbm, wk_hbm, wv_hbm, wo_hbm, gain_ref, wg_hbm, wu_hbm, wd_ref,
    out_ref, gtok_ref, gq_ref, gl_ref, gk_ref, gv_ref, go_ref, gain_out, gg_ref, gu_ref, gd_ref,
    attn, gate_w, up_w, down_w, down_c, gains, gain_full,
    tok, bias, normed, query, latent, keys, values, merged, lse, middle, normed2, dout,
    mixed, dgate, dup, tmp, rcv_out,
    dmid_low, dmerged, dquery, dkeys, dvalues, dlatent,
    pattn, s_d, s_g, s_u, y_d, y_g, y_u, z_d, z_g, z_u, x_g, x_u,
    s_a, x_a, z_a, y_a, sum_own, sum_rcv,
    send_sem, recv_sem, local_sem,
):
    snd_dn2, snd_out, rcv_dn2 = dquery, dkeys, dvalues
    dmid = gtok_ref
    dp = lax.axis_index("dp")
    fs = lax.axis_index("fsdp")
    x, c, z, y = lax.div(dp, 2), lax.rem(dp, 2), lax.div(fs, 2), lax.rem(fs, 2)
    sib = (x * 2 + 1 - c, fs)
    xp = ((1 - x) * 2 + c, fs)
    yp = (dp, z * 2 + 1 - y)
    zr = (dp, (z + 1) * 2 + y)
    zl = (dp, (z - 1) * 2 + y)
    z_one = (dp, (z + 1 - 2 * lax.rem(z, 2)) * 2 + y)
    z_two = (dp, lax.rem(z + 2, 4) * 2 + y)

    sends = {}

    def copy(src, dst, slot, target):
        return pltpu.make_async_remote_copy(
            src_ref=src, dst_ref=dst, send_sem=send_sem.at[slot], recv_sem=recv_sem.at[slot],
            device_id=target, device_id_type=MESH,
        )

    def when(cond, fn):
        if cond is True:
            fn()
        else:
            pl.when(cond)(fn)

    def send(group, src, dst, slot, target, cond=True):
        when(cond, lambda: copy(src, dst, slot, target).start())
        sends.setdefault(group, []).append((cond, lambda: copy(src, dst, slot, target).wait_send()))

    def drain(group):
        for cond, fn in sends.pop(group, []):
            when(cond, fn)

    def arrive(dst, slot, target=None):
        copy(dst, dst, slot, sib).wait_recv()

    loads = [
        (wq_hbm, attn.at[0, x, c, z, y]),
        (wl_hbm, attn.at[2, x, c, z, y, :, pl.ds(0, 512)]),
        (wk_hbm, attn.at[2, x, c, z, y, pl.ds(0, 16), pl.ds(512, 512)]),
        (wv_hbm, attn.at[2, x, c, z, y, pl.ds(16, 16), pl.ds(512, 512)]),
        (wo_hbm, attn.at[1, x, c, z, y]),
        (wg_hbm.at[:, pl.ds(pl.multiple_of(x * HALF, 128), HALF)], gate_w.at[c, z, y, x]),
        (wu_hbm.at[:, pl.ds(pl.multiple_of(x * HALF, 128), HALF)], up_w.at[c, z, y, x]),
        (tok_hbm, tok),
        (cot_hbm, dout.at[x]),
    ]
    loads = [pltpu.make_async_copy(s, d, local_sem.at[i]) for i, (s, d) in enumerate(loads)]
    for load in loads:
        load.start()
    bar = pltpu.get_barrier_semaphore()
    for target, cond in ((sib, True), (xp, True), (yp, True), (z_two, True), (zr, z < 3), (zl, z > 0)):
        when(cond, lambda target=target: pl.semaphore_signal(bar, inc=1, device_id=target, device_id_type=MESH))
    down_w[c, z, y] = jnp.concatenate(
        [wd_ref[...].astype(F32), jnp.zeros((PAD - DOWN, WIDTH), F32)], axis=0
    ).astype(BF16)
    lane = lax.broadcasted_iota(jnp.int32, (16, 128), 1)
    mine = lax.div(lane, 32) == lax.rem(fs, 4)
    gains[x, c, z, y] = jnp.where(mine, gain_ref[...].astype(F32), 0.0).astype(BF16)
    pl.semaphore_wait(bar, 5 + jnp.where((z > 0) & (z < 3), 1, 0))

    def attn_blk(xx, zz, yy, cc=c):
        return attn.at[:, xx, cc, zz, yy]

    def attn_out(zz, yy):
        blk = attn_blk(x, zz, yy)
        send("attn", blk, blk, S_AX + zz * 2 + yy, xp)
        send("attn", blk, blk, S_AS + x * 8 + zz * 2 + yy, sib)

    def attn_z(s, k, yy):
        right, left = attn_blk(x, z - s, yy), attn_blk(x, z + s, yy)
        send("attn", right, right, S_AZ + k * 6 + s, zr, (z < 3) & (z - s >= 0))
        send("attn", left, left, S_AZ + k * 6 + 3 + s, zl, (z > 0) & (z + s <= 3))

    def attn_z_step(s, yy):
        def from_left():
            blk = attn_blk(x, z - 1 - s, yy)
            arrive(blk, S_AZ + yy * 6 + s)

        def from_right():
            blk = attn_blk(x, z + 1 + s, yy)
            arrive(blk, S_AZ + yy * 6 + 3 + s)

        for cond, fn, zz in ((z - 1 - s >= 0, from_left, z - 1 - s), (z + 1 + s <= 3, from_right, z + 1 + s)):
            pl.when(cond)(fn)
            blk = attn_blk(x, zz, yy)
            if s < 2:
                if fn is from_left:
                    send("attn", blk, blk, S_AZ + yy * 6 + s + 1, zr, cond & (z < 3))
                else:
                    send("attn", blk, blk, S_AZ + yy * 6 + 3 + s + 1, zl, cond & (z > 0))
            send("attn", blk, blk, S_AX + zz * 2 + yy, xp, cond)
            send("attn", blk, blk, S_AS + x * 8 + zz * 2 + yy, sib, cond)

    for load in loads[:5]:
        load.wait()
    own = attn_blk(x, z, y)
    send("attn", own, own, S_AY, yp)
    attn_z(0, y, y)
    attn_out(z, y)

    other_cols = pl.ds(pl.multiple_of((1 - x) * HALF, 128), HALF)
    send("half", wg_hbm.at[:, other_cols], gate_w.at[c, z, y, x], S_HALF, xp)
    send("half", wu_hbm.at[:, other_cols], up_w.at[c, z, y, x], S_HALF + 1, xp)

    gain_steps = (
        (gains.at[x, c, z, y], sib),
        (gains.at[x, :, z, y], yp),
        (gains.at[x, :, z], xp),
        (gains.at[:, :, z], z_one),
        (gains.at[:, :, pl.ds(lax.div(z, 2) * 2, 2)], z_two),
    )
    gain_from = (
        gains.at[x, 1 - c, z, y],
        gains.at[x, :, z, 1 - y],
        gains.at[1 - x, :, z],
        gains.at[:, :, z + 1 - 2 * lax.rem(z, 2)],
        gains.at[:, :, pl.ds(2 - lax.div(z, 2) * 2, 2)],
    )

    def gain_send(i):
        ref, target = gain_steps[i]
        send("gain", ref, ref, S_GAIN + i, target)

    def gain_recv(i):
        arrive(gain_from[i], S_GAIN + i)

    gain_send(0)

    ffn = (down_w, gate_w, up_w)

    def ffn_own(t):
        blk = ffn[t].at[c, z, y]
        send("ffn%d" % t, blk, blk, S_FY[t] + z, yp)
        send("ffn%d" % t, blk, blk, S_FS[t] + z * 2 + y, sib)

    def ffn_own_z(t):
        blk = ffn[t].at[c, z, y]
        send("ffn%d" % t, blk, blk, S_FZ[t], zr, z < 3)
        send("ffn%d" % t, blk, blk, S_FZ[t] + 3, zl, z > 0)

    def ffn_z_step(t, s):
        for right, cond, zz in ((True, z - 1 - s >= 0, z - 1 - s), (False, z + 1 + s <= 3, z + 1 + s)):
            blk = ffn[t].at[c, zz, y]
            slot = S_FZ[t] + (0 if right else 3) + s
            pl.when(cond)(lambda blk=blk, slot=slot: arrive(blk, slot))
            if s < 2:
                on = (z < 3) if right else (z > 0)
                send("ffn%d" % t, blk, blk, slot + 1, zr if right else zl, cond & on)
            send("ffn%d" % t, blk, blk, S_FY[t] + zz, yp, cond)
            send("ffn%d" % t, blk, blk, S_FS[t] + zz * 2 + y, sib, cond)

    def ffn_y_step(t, zz):
        blk = ffn[t].at[c, zz, 1 - y]
        arrive(blk, S_FY[t] + zz)
        send("ffn%d" % t, blk, blk, S_FS[t] + zz * 2 + 1 - y, sib)

    def ffn_sib(t):
        for k in range(8):
            arrive(ffn[t].at[1 - c, k // 2, k % 2], S_FS[t] + k)

    ffn_own(0)
    gain_recv(0)
    gain_send(1)

    e0 = len_ref[0]
    e1 = e0 + len_ref[1]
    e2 = e1 + len_ref[2]
    e3 = e2 + len_ref[3]

    def segment(position):
        return sum((position >= e).astype(jnp.int32) for e in (e0, e1, e2, e3))

    row = lax.broadcasted_iota(jnp.int32, (ROWS, ROWS), 0)
    col = lax.broadcasted_iota(jnp.int32, (ROWS, ROWS), 1)
    bias[...] = jnp.where((segment(row) == segment(col)) & (col <= row), 0.0, -1e30)

    for load in loads[5:]:
        load.wait()

    def mask_rows(k, carry):
        rows = pl.ds(pl.multiple_of(k * 64, 64), 64)
        position = lax.broadcasted_iota(jnp.int32, (64, WIDTH), 0) + k * 64
        dout[x, rows] = jnp.where(position < e3, dout[x, rows].astype(F32), 0.0).astype(BF16)
        return carry

    lax.fori_loop(0, 4, mask_rows, 0)

    arrive(attn_blk(x, z, 1 - y), S_AY)
    attn_z(0, 1 - y, 1 - y)
    attn_out(z, 1 - y)
    gain_recv(1)
    gain_send(2)
    attn_z_step(0, y)
    gain_recv(2)
    gain_send(3)
    attn_z_step(0, 1 - y)
    arrive(gate_w.at[c, z, y, 1 - x], S_HALF)
    arrive(up_w.at[c, z, y, 1 - x], S_HALF + 1)
    ffn_own(1)
    ffn_own(2)
    gain_recv(3)
    gain_send(4)
    attn_z_step(1, y)
    attn_z_step(1, 1 - y)
    attn_z_step(2, y)
    attn_z_step(2, 1 - y)
    for t in range(3):
        ffn_own_z(t)
    send("cot", dout.at[x], dout.at[x], S_COT, xp)
    gain_recv(4)

    def gain_rows(k, carry):
        g = gains.at[lax.div(k, 4), lax.div(lax.rem(k, 4), 2)]
        part = g[pl.ds(lax.rem(k, 2) * 2, 2)].astype(F32)
        gain_full[:, pl.ds(pl.multiple_of(k * 128, 128), 128)] = part[0, 0] + part[0, 1] + part[1, 0] + part[1, 1]
        return carry

    lax.fori_loop(0, 8, gain_rows, 0)

    def norm_rows(k, carry):
        rows = pl.ds(pl.multiple_of(k * 64, 64), 64)
        val = tok[rows].astype(F32)
        r1 = lax.rsqrt(jnp.mean(val * val, axis=1, keepdims=True) + EPSILON)
        normed[rows] = (val * r1 * gain_full[0:1, :]).astype(BF16)
        return carry

    lax.fori_loop(0, 4, norm_rows, 0)

    for zz in range(4):
        for yy in range(2):
            blk = attn_blk(1 - x, zz, yy)
            arrive(blk, S_AX + zz * 2 + yy)
            send("attn", blk, blk, S_AS + (1 - x) * 8 + zz * 2 + yy, sib)
    for k in range(16):
        arrive(attn_blk(k // 8, (k % 8) // 2, k % 2, 1 - c), S_AS + k)

    def cols(n, width=256):
        return pl.ds(pl.multiple_of(n * width, width), width)

    def query_cols(n, carry):
        w = attn[0, :, :, :, :, :, cols(n)].reshape(WIDTH, 256)
        query[:, cols(n)] = nn(normed[...], w).astype(BF16)
        return carry

    lax.fori_loop(0, 4, query_cols, 0)

    def latent_cols(n, carry):
        w = attn[2, :, :, :, :, :, cols(n)].reshape(WIDTH, 256)
        latent[:, cols(n)] = nn(normed[...], w).astype(BF16)
        return carry

    lax.fori_loop(0, 2, latent_cols, 0)

    def up_weight(g, first):
        return attn[2, g, :, :, :, pl.ds(first, 16), pl.ds(512, 512)].reshape(256, 512)

    def key_cols(g, carry):
        lat = latent[:, cols(g)]
        keys[:, cols(g, 512)] = nn(lat, up_weight(g, 0)).astype(BF16)
        values[:, cols(g, 512)] = nn(lat, up_weight(g, 16)).astype(BF16)
        return carry

    lax.fori_loop(0, GROUPS, key_cols, 0)
    ffn_z_step(0, 0)

    low_half = lax.broadcasted_iota(jnp.int32, (ROWS, 128), 1) < HEAD_DIM
    head_lane = lax.broadcasted_iota(jnp.int32, (ROWS, 128), 1)
    lse[...] = jnp.zeros((ROWS, 128), F32)

    def halves(v):
        zero = jnp.zeros_like(v)
        return (jnp.where(low_half, v, zero), jnp.where(low_half, zero, v))

    def attend(j, carry):
        pair = cols(j, 128)
        k_pair, v_pair = keys[:, pair], values[:, pair]
        res = []
        for h, q in enumerate(halves(query[:, pair])):
            s = nt(q, k_pair) * SCALE + bias[...]
            peak = jnp.max(s, axis=1, keepdims=True)
            expo = jnp.exp(s - peak)
            total = jnp.sum(expo, axis=1, keepdims=True)
            res.append(nn((expo / total).astype(BF16), v_pair))
            lse[...] = jnp.where(head_lane == j * 2 + h, peak + jnp.log(total), lse[...])
        merged[:, pair] = jnp.where(low_half, res[0], res[1]).astype(BF16)
        return carry

    lax.fori_loop(0, 4, attend, 0)
    ffn_z_step(0, 1)
    lax.fori_loop(4, 8, attend, 0)
    ffn_z_step(0, 2)

    def middle_cols(n, carry):
        w = attn[1, :, :, :, :, :, cols(n)].reshape(WIDTH, 256)
        middle[:, cols(n)] = tok[:, cols(n)].astype(F32) + nn(merged[...], w)
        return carry

    lax.fori_loop(0, 4, middle_cols, 0)

    def norm2_rows(k, carry):
        rows = pl.ds(pl.multiple_of(k * 64, 64), 64)
        val = middle[rows]
        r2 = lax.rsqrt(jnp.mean(val * val, axis=1, keepdims=True) + EPSILON)
        normed2[x, rows] = (val * r2 * gain_full[1:2, :]).astype(BF16)
        return carry

    lax.fori_loop(0, 4, norm2_rows, 0)
    send("n2", normed2.at[x], normed2.at[x], S_N2, xp)

    ffn_z_step(1, 0)
    for zz in range(4):
        ffn_y_step(0, zz)
    ffn_z_step(1, 1)
    ffn_z_step(1, 2)
    ffn_z_step(2, 0)
    ffn_sib(0)

    def compact(k, carry):
        pair = down_w.at[lax.div(k, 4), lax.rem(k, 4)]
        joined = jnp.concatenate([pair[0, 0:DOWN].astype(F32), pair[1, 0:DOWN].astype(F32)], axis=0)
        down_c[pl.ds(pl.multiple_of(k * 2 * DOWN, 16), 2 * DOWN)] = joined.astype(BF16)
        return carry

    lax.fori_loop(0, 8, compact, 0)
    for zz in range(4):
        ffn_y_step(1, zz)
    ffn_z_step(2, 1)
    ffn_z_step(2, 2)
    arrive(dout.at[1 - x], S_COT)
    arrive(normed2.at[1 - x], S_N2)
    ffn_sib(1)
    for zz in range(4):
        ffn_y_step(2, zz)
    ffn_sib(2)

    def ffn_w(ref, half, sl):
        return ref[:, :, :, half, :, sl].reshape(512, sl.size)

    for first, width in CHUNKS:
        sl = pl.ds(first, width)

        def hidden(m, carry, sl=sl):
            n2 = normed2[m]
            gate = nn(n2[:, 0:512], ffn_w(gate_w, 0, sl)) + nn(n2[:, 512:1024], ffn_w(gate_w, 1, sl))
            upper = nn(n2[:, 0:512], ffn_w(up_w, 0, sl)) + nn(n2[:, 512:1024], ffn_w(up_w, 1, sl))
            dmix = nt(dout[m], down_c[sl])
            sig = jax.nn.sigmoid(gate)
            silu = gate * sig
            rows = pl.ds(pl.multiple_of(m * ROWS, ROWS), ROWS)
            mixed[rows, sl] = (silu * upper).astype(BF16)
            dgate[rows, sl] = (dmix * upper * sig * (1.0 + gate * (1.0 - sig))).astype(BF16)
            dup[rows, sl] = (dmix * silu).astype(BF16)
            return carry

        lax.fori_loop(0, 2, hidden, 0)

    grads = (down_w, gate_w, up_w)
    s_bufs, y_bufs, z_bufs = (s_d, s_g, s_u), (y_d, y_g, y_u), (z_d, z_g, z_u)

    def add(dst, src):
        dst[...] = dst[...] + src[...]

    def rs_sib_send(t):
        for k, yy in enumerate((1 - y, y)):
            send("rs%d" % t, grads[t].at[1 - c, :, yy], s_bufs[t].at[yy], S_RS[t] + yy, sib)

    def rs_sib_recv(t, yy):
        arrive(s_bufs[t].at[yy], S_RS[t] + yy)

        def one(zz, carry):
            add(grads[t].at[c, zz, yy], s_bufs[t].at[yy, zz])
            return carry

        lax.fori_loop(0, 4, one, 0)

    def rs_y_send(t):
        for zz in (3, 0, 2, 1):
            send("rs%d" % t, grads[t].at[c, zz, 1 - y], y_bufs[t].at[zz], S_RY[t] + zz, yp)

    def rs_y_recv(t):
        for zz in (3, 0, 2, 1):
            arrive(y_bufs[t].at[zz], S_RY[t] + zz)
            add(grads[t].at[c, zz, y], y_bufs[t].at[zz])

    end = (z == 0) | (z == 3)
    inner = (z == 1) | (z == 2)
    lower = z < 2

    def real(m):
        return jnp.where(lower, m, 3 - m)

    far = (dp, jnp.where(lower, z + 1, z - 1) * 2 + y)
    near = (dp, jnp.where(lower, z - 1, z + 1) * 2 + y)
    far_way = jnp.where(lower, 0, 4)
    near_way = jnp.where(lower, 4, 0)

    def slot_at(way, dest, receiver):
        return jnp.where((way == 4) & (dest == receiver), 4, dest)

    def chain_send(group, blk, buf, base, m, to_far, cond):
        d = real(m)
        way = far_way if to_far else near_way
        receiver = jnp.where(lower == to_far, z + 1, z - 1)
        send(group, blk(d), buf(slot_at(way, d, receiver)), base + way + d, far if to_far else near, cond)

    def chain_take(blk, buf, base, m, from_far):
        d = real(m)
        way = near_way if from_far else far_way
        src = buf(slot_at(way, d, z))
        arrive(src, base + way + d)
        add(blk(d), src)

    def chain_start(group, blk, buf, base):
        for m in (3, 2, 1):
            chain_send(group, blk, buf, base, m, True, end)

    def chain_pass(group, blk, buf, base):
        for m in (3, 2):
            pl.when(inner)(lambda m=m: chain_take(blk, buf, base, m, False))
            chain_send(group, blk, buf, base, m, True, inner)

    def chain_back(group, blk, buf, base):
        pl.when(inner)(lambda: chain_take(blk, buf, base, 0, True))
        chain_send(group, blk, buf, base, 0, False, inner)

    def chain_end(blk, buf, base):
        pl.when(inner)(lambda: chain_take(blk, buf, base, 1, False))
        pl.when(inner)(lambda: chain_take(blk, buf, base, 1, True))
        pl.when(end)(lambda: chain_take(blk, buf, base, 0, True))

    def rs_chain(t):
        return ("rs%d" % t, lambda d: grads[t].at[c, d, y], lambda k: z_bufs[t].at[k], S_RZ[t])

    def dn_half(it, carry):
        m = jnp.where(it == 0, 1 - x, x)
        rows = pl.ds(pl.multiple_of(m * ROWS, ROWS), ROWS)
        for half in range(2):
            full = pl.ds(0, HALF)
            tmp[pl.ds(0, ROWS), pl.ds(half * 512, 512)] = nt(dgate[rows], ffn_w(gate_w, half, full)) + nt(
                dup[rows], ffn_w(up_w, half, full)
            )

        @pl.when(it == 0)
        def _():
            snd_dn2[...] = tmp[0:ROWS].astype(BF16)
            copy(snd_dn2, rcv_dn2, S_DN2, xp).start()

        return carry

    lax.fori_loop(0, 2, dn_half, 0)
    sends["dn2"] = [(True, lambda: copy(snd_dn2, rcv_dn2, S_DN2, xp).wait_send())]

    drain("ffn0")

    def grad_down(it, carry):
        cc = jnp.where(it == 0, 1 - c, c)
        wide = pl.ds(pl.multiple_of(cc * 640, 128), 768)
        mt = mixed[:, wide].T
        tmp[pl.ds(ROWS, 768)] = nn(mt[:, 0:256], dout[0]) + nn(mt[:, 256:512], dout[1])

        def split(k, inner_carry):
            rows = tmp[pl.ds(pl.multiple_of(ROWS + cc * 64 + k * DOWN, 8), DOWN)]
            down_w[cc, lax.div(k, 2), lax.rem(k, 2)] = jnp.concatenate(
                [rows, jnp.zeros((PAD - DOWN, WIDTH), F32)], axis=0
            ).astype(BF16)
            return inner_carry

        lax.fori_loop(0, 8, split, 0)
        return carry

    lax.fori_loop(0, 2, grad_down, 0)
    rs_sib_send(0)

    drain("ffn1")
    drain("ffn2")

    def grad_gate_up(it, carry):
        cc = jnp.where(it < 2, 1 - c, c)
        half = lax.rem(it, 2)
        sl = pl.ds(pl.multiple_of(half * 512 + cc * 256, 256), 256)
        for src, dst in ((dgate, gate_w), (dup, up_w)):
            g = nn(normed2[0, :, sl].T, src[pl.ds(0, ROWS)]) + nn(normed2[1, :, sl].T, src[pl.ds(ROWS, ROWS)])
            dst[cc, :, :, half] = g.astype(BF16).reshape(4, 2, 32, HALF)
        return carry

    lax.fori_loop(0, 4, grad_gate_up, 0)
    rs_sib_send(1)
    rs_sib_send(2)

    rs_sib_recv(0, 1 - y)
    rs_y_send(0)
    rs_sib_recv(0, y)

    def out_half(it, carry):
        m = jnp.where(it == 0, 1 - x, x)
        rows = pl.ds(pl.multiple_of(m * ROWS, ROWS), ROWS)
        part = nn(mixed[rows], down_c[...])
        tmp[pl.ds(ROWS, ROWS)] = part

        @pl.when(it == 0)
        def _():
            snd_out[...] = tmp[pl.ds(ROWS, ROWS)].astype(BF16)
            copy(snd_out, rcv_out, S_OUT, xp).start()

        return carry

    lax.fori_loop(0, 2, out_half, 0)
    sends["out"] = [(True, lambda: copy(snd_out, rcv_out, S_OUT, xp).wait_send())]

    for t in (1, 2):
        rs_sib_recv(t, 1 - y)
        rs_y_send(t)
        rs_sib_recv(t, y)

    sum_own[...] = jnp.zeros((8, WIDTH), F32)
    arrive(rcv_dn2, S_DN2)

    def back_two(k, carry):
        rows = pl.ds(pl.multiple_of(k * 32, 32), 32)
        mid = middle[rows]
        r2 = lax.rsqrt(jnp.mean(mid * mid, axis=1, keepdims=True) + EPSILON)
        grad = tmp[rows] + rcv_dn2[rows].astype(F32)
        sum_own[1:2] = sum_own[1:2] + jnp.sum(grad * mid * r2, axis=0, keepdims=True)
        s = grad * gain_full[1:2, :]
        res = dout[x, rows].astype(F32) + r2 * (s - mid * r2 * r2 * jnp.mean(s * mid, axis=1, keepdims=True))
        dmid[rows] = res
        dmid_low[rows] = res.astype(BF16)
        return carry

    lax.fori_loop(0, 8, back_two, 0)

    def dmerged_cols(k, carry):
        w = attn[1, lax.div(k, 2), lax.rem(k, 2)].reshape(256, WIDTH)
        dmerged[:, cols(k)] = nt(dmid_low[...], w).astype(BF16)
        return carry

    lax.fori_loop(0, 4, dmerged_cols, 0)

    def grad_output(it, carry):
        cc = jnp.where(it < 2, 1 - c, c)
        half = lax.rem(it, 2)
        g = nn(merged[:, cols(half * 2 + cc)].T, dmid_low[...])
        pattn[0, half, cc] = g.astype(BF16).reshape(4, 2, 32, WIDTH)
        return carry

    lax.fori_loop(0, 4, grad_output, 0)

    parts = (pl.ds(0, 1), pl.ds(1, 2))

    def at_sib_send(p):
        for xx in (1 - x, x):
            send("at", pattn.at[parts[p], xx, 1 - c], s_a.at[parts[p], xx], S_BS[p] + xx, sib)

    def at_sib_recv(p, xx):
        arrive(s_a.at[parts[p], xx], S_BS[p] + xx)

        def one(zz, carry):
            add(pattn.at[parts[p], xx, c, zz], s_a.at[parts[p], xx, zz])
            return carry

        lax.fori_loop(0, 4, one, 0)

    def at_x_send(p):
        for zz in (3, 0, 2, 1):
            send("at", pattn.at[parts[p], 1 - x, c, zz], x_a.at[parts[p], zz], S_BX[p] + zz, xp)

    def at_x_recv(p):
        for zz in (3, 0, 2, 1):
            arrive(x_a.at[parts[p], zz], S_BX[p] + zz)
            add(pattn.at[parts[p], x, c, zz], x_a.at[parts[p], zz])

    def at_chain(p):
        return ("at", lambda d: pattn.at[parts[p], x, c, d], lambda k: z_a.at[parts[p], k], S_BZ[p])

    def at_y_send(p):
        send("at", pattn.at[parts[p], x, c, z, 1 - y], y_a.at[parts[p]], S_BY[p], yp)

    def at_y_recv(p):
        arrive(y_a.at[parts[p]], S_BY[p])
        add(pattn.at[parts[p], x, c, z, y], y_a.at[parts[p]])

    at_sib_send(0)

    rs_y_recv(0)
    chain_start(*rs_chain(0))
    at_sib_recv(0, 1 - x)
    at_x_send(0)
    at_sib_recv(0, x)
    chain_pass(*rs_chain(0))

    drain("dn2")
    drain("out")

    def attend_back(j, carry):
        pair = cols(j, 128)
        q_pair, k_pair, v_pair, do_pair = query[:, pair], keys[:, pair], values[:, pair], dmerged[:, pair]
        dq, dk, dv = [], [], []
        for h, (q, do) in enumerate(zip(halves(q_pair), halves(do_pair))):
            logsum = jnp.sum(jnp.where(head_lane == j * 2 + h, lse[...], 0.0), axis=1, keepdims=True)
            probs = jnp.exp(nt(q, k_pair) * SCALE + bias[...] - logsum)
            dv.append(tn(probs.astype(BF16), do_pair))
            dprobs = nt(do, v_pair)
            row_sum = jnp.sum(probs * dprobs, axis=1, keepdims=True)
            dscores = (probs * (dprobs - row_sum)).astype(BF16)
            dq.append(nn(dscores, k_pair))
            dk.append(tn(dscores, q_pair))
        dquery[:, pair] = (jnp.where(low_half, dq[0], dq[1]) * SCALE).astype(BF16)
        dkeys[:, pair] = (jnp.where(low_half, dk[0], dk[1]) * SCALE).astype(BF16)
        dvalues[:, pair] = jnp.where(low_half, dv[0], dv[1]).astype(BF16)
        return carry

    lax.fori_loop(0, 4, attend_back, 0)
    rs_y_recv(1)
    chain_start(*rs_chain(1))
    chain_back(*rs_chain(0))
    lax.fori_loop(4, 8, attend_back, 0)
    chain_pass(*rs_chain(1))

    def latent_back(g, carry):
        dk, dv = dkeys[:, cols(g, 512)], dvalues[:, cols(g, 512)]
        dlatent[:, cols(g)] = (nt(dk, up_weight(g, 0)) + nt(dv, up_weight(g, 16))).astype(BF16)
        lat = latent[:, cols(g)].T
        pattn[2, g, :, :, :, pl.ds(0, 16), pl.ds(512, 512)] = nn(lat, dk).astype(BF16).reshape(2, 4, 2, 16, 512)
        pattn[2, g, :, :, :, pl.ds(16, 16), pl.ds(512, 512)] = nn(lat, dv).astype(BF16).reshape(2, 4, 2, 16, 512)
        return carry

    lax.fori_loop(0, GROUPS, latent_back, 0)

    def grad_proj(it, carry):
        cc = jnp.where(it < 2, 1 - c, c)
        half = lax.rem(it, 2)
        nt_ = normed[:, cols(half * 2 + cc)].T
        pattn[1, half, cc] = nn(nt_, dquery[...]).astype(BF16).reshape(4, 2, 32, WIDTH)
        pattn[2, half, cc, :, :, :, pl.ds(0, 512)] = nn(nt_, dlatent[...]).astype(BF16).reshape(4, 2, 32, 512)
        return carry

    lax.fori_loop(0, 4, grad_proj, 0)
    at_sib_send(1)
    at_sib_recv(1, 1 - x)
    at_x_send(1)
    at_sib_recv(1, x)

    rs_y_recv(2)
    chain_start(*rs_chain(2))
    at_x_recv(0)
    chain_start(*at_chain(0))

    def dnormed_cols(k, carry):
        xx, cc = lax.div(k, 2), lax.rem(k, 2)
        part = nt(dquery[...], attn[0, xx, cc].reshape(256, WIDTH))
        part = part + nt(dlatent[...], attn[2, xx, cc, :, :, :, pl.ds(0, 512)].reshape(256, 512))
        tmp[pl.ds(0, ROWS), cols(k)] = part
        return carry

    lax.fori_loop(0, 4, dnormed_cols, 0)

    def back_one(k, carry):
        rows = pl.ds(pl.multiple_of(k * 32, 32), 32)
        val = tok[rows].astype(F32)
        r1 = lax.rsqrt(jnp.mean(val * val, axis=1, keepdims=True) + EPSILON)
        grad = tmp[rows]
        sum_own[0:1] = sum_own[0:1] + jnp.sum(grad * val * r1, axis=0, keepdims=True)
        s = grad * gain_full[0:1, :]
        gtok_ref[rows] = dmid[rows] + r1 * (s - val * r1 * r1 * jnp.mean(s * val, axis=1, keepdims=True))
        return carry

    lax.fori_loop(0, 8, back_one, 0)

    sum_to = (sib, yp, xp, z_one, z_two)

    def sum_send(i):
        send("sum%d" % i, sum_own, sum_rcv.at[i], S_SUM + i, sum_to[i])

    def sum_recv(i):
        drain("sum%d" % i)
        arrive(sum_rcv.at[i], S_SUM + i)
        sum_own[...] = sum_own[...] + sum_rcv[i]

    sum_send(0)
    arrive(rcv_out, S_OUT)

    def out_rows(k, carry):
        rows = pl.ds(pl.multiple_of(k * 32, 32), 32)
        part = tmp[pl.ds(pl.multiple_of(ROWS + k * 32, 32), 32)]
        out_ref[rows] = (middle[rows] + (part + rcv_out[rows].astype(F32))).astype(BF16)
        return carry

    lax.fori_loop(0, 8, out_rows, 0)
    sum_recv(0)
    sum_send(1)

    chain_end(*rs_chain(0)[1:])
    gd_ref[...] = down_w[c, z, y].astype(F32)[0:DOWN]
    chain_back(*rs_chain(1))
    sum_recv(1)
    sum_send(2)
    chain_pass(*rs_chain(2))
    chain_pass(*at_chain(0))
    chain_end(*rs_chain(1)[1:])
    send("rx", gate_w.at[c, z, y, 1 - x], x_g, S_RX, xp)
    sum_recv(2)
    sum_send(3)
    chain_back(*rs_chain(2))
    chain_back(*at_chain(0))
    at_x_recv(1)
    chain_start(*at_chain(1))
    sum_recv(3)
    sum_send(4)
    chain_end(*rs_chain(2)[1:])
    send("rx", up_w.at[c, z, y, 1 - x], x_u, S_RX + 1, xp)
    chain_pass(*at_chain(1))
    chain_end(*at_chain(0)[1:])
    at_y_send(0)
    chain_back(*at_chain(1))
    sum_recv(4)
    own_cols = pl.ds(pl.multiple_of(x * HALF, 128), HALF)
    for w, ref, buf, k in ((gate_w, gg_ref, x_g, 0), (up_w, gu_ref, x_u, 1)):
        ref[:, own_cols] = w[c, z, y, x].astype(F32)
        arrive(buf, S_RX + k)
        ref[:, other_cols] = buf[...].astype(F32)
    gain_out[...] = sum_own[:, pl.ds(pl.multiple_of((dp * 2 + lax.div(fs, 4)) * 128, 128), 128)]
    at_y_recv(0)
    go_ref[...] = pattn[0, x, c, z, y].astype(F32)
    chain_end(*at_chain(1)[1:])
    at_y_send(1)
    at_y_recv(1)
    gq_ref[...] = pattn[1, x, c, z, y].astype(F32)
    last = pattn.at[2, x, c, z, y]
    gl_ref[...] = last[:, 0:512].astype(F32)
    gk_ref[...] = last[0:16, 512:1024].astype(F32)
    gv_ref[...] = last[16:32, 512:1024].astype(F32)
    for group in list(sends):
        drain(group)


def kernel_on_device(
    tokens, seq_lengths, cotangent, w_query, w_latent, w_keyup, w_valup, w_output, norm_attn, norm_ffn,
    w_gate, w_up, w_down,
):
    gain_rows = jnp.concatenate(
        [jnp.tile(norm_attn, 4)[None], jnp.tile(norm_ffn, 4)[None], jnp.zeros((14, 128), BF16)], axis=0
    )
    hbm, vmem = pl.BlockSpec(memory_space=pl.ANY), pl.BlockSpec(memory_space=pltpu.VMEM)
    smem = pl.BlockSpec(memory_space=pltpu.SMEM)
    shape = jax.ShapeDtypeStruct
    outs = [
        shape((ROWS, WIDTH), BF16), shape((ROWS, WIDTH), F32), shape((32, WIDTH), F32), shape((32, 512), F32),
        shape((16, 512), F32), shape((16, 512), F32), shape((32, WIDTH), F32), shape((8, 128), F32),
        shape((32, 2 * HALF), F32), shape((32, 2 * HALF), F32), shape((DOWN, WIDTH), F32),
    ]
    V = pltpu.VMEM
    act = V((ROWS, WIDTH), BF16)
    scratch = [
        V((3, 2, 2, 4, 2, 32, WIDTH), BF16), V((2, 4, 2, 2, 32, HALF), BF16), V((2, 4, 2, 2, 32, HALF), BF16),
        V((2, 4, 2, PAD, WIDTH), BF16), V((HALF, WIDTH), BF16), V((2, 2, 4, 2, 16, 128), BF16), V((16, WIDTH), F32),
        act, V((ROWS, ROWS), F32), act, act, V((ROWS, 512), BF16), act, act, act, V((ROWS, 128), F32),
        V((ROWS, WIDTH), F32), V((2, ROWS, WIDTH), BF16), V((2, ROWS, WIDTH), BF16),
        V((512, HALF), BF16), V((512, HALF), BF16), V((512, HALF), BF16), V((ROWS + 768, WIDTH), F32),
        act,
        act, act, act, act, act, V((ROWS, 512), BF16),
        V((3, 2, 2, 4, 2, 32, WIDTH), BF16),
        V((2, 4, PAD, WIDTH), BF16), V((2, 4, 2, 32, HALF), BF16), V((2, 4, 2, 32, HALF), BF16),
        V((4, PAD, WIDTH), BF16), V((4, 2, 32, HALF), BF16), V((4, 2, 32, HALF), BF16),
        V((5, PAD, WIDTH), BF16), V((5, 2, 32, HALF), BF16), V((5, 2, 32, HALF), BF16),
        V((32, HALF), BF16), V((32, HALF), BF16),
        V((3, 2, 4, 2, 32, WIDTH), BF16), V((3, 4, 2, 32, WIDTH), BF16), V((3, 5, 2, 32, WIDTH), BF16),
        V((3, 32, WIDTH), BF16), V((8, WIDTH), F32), V((5, 8, WIDTH), F32),
        pltpu.SemaphoreType.DMA((SLOTS.count,)), pltpu.SemaphoreType.DMA((SLOTS.count,)), pltpu.SemaphoreType.DMA((9,)),
    ]
    res = pl.pallas_call(
        layer_kernel,
        out_shape=outs,
        in_specs=[hbm, smem, hbm, hbm, hbm, hbm, hbm, hbm, vmem, hbm, hbm, vmem],
        out_specs=[vmem] * len(outs),
        scratch_shapes=scratch,
        compiler_params=pltpu.CompilerParams(
            collective_id=0, has_side_effects=True, vmem_limit_bytes=63 * 2**20
        ),
    )(tokens, seq_lengths, cotangent, w_query, w_latent, w_keyup, w_valup, w_output, gain_rows, w_gate, w_up, w_down)
    out, gtok, gq, gl, gk, gv, go, gain, gg, gu, gd = res
    first = lax.rem(lax.axis_index("fsdp"), 4) * 32
    own = lax.dynamic_slice(gain, (0, first), (2, 32))
    return (out, gtok, gq, gl, gk, gv, go, own[0], own[1], gg, gu, gd)


def solution(mesh):
    fits = dict(mesh.shape) == {"dp": 4, "fsdp": 8}
    return jax.shard_map(
        kernel_on_device if fits else on_device,
        mesh=mesh,
        in_specs=(
            P(("dp", "fsdp"), None),
            P(("dp", "fsdp")),
            P(("dp", "fsdp"), None),
            P(("dp", "fsdp"), None),
            P(("dp", "fsdp"), None),
            P(("dp", "fsdp"), None),
            P(("dp", "fsdp"), None),
            P(("dp", "fsdp"), None),
            P(("dp", "fsdp")),
            P(("dp", "fsdp")),
            P(("dp", "fsdp"), None),
            P(("dp", "fsdp"), None),
            P(("dp", "fsdp"), None),
        ),
        out_specs=(
            P(("dp", "fsdp"), None),
            P(("dp", "fsdp"), None),
            P(("dp", "fsdp"), None),
            P(("dp", "fsdp"), None),
            P(("dp", "fsdp"), None),
            P(("dp", "fsdp"), None),
            P(("dp", "fsdp"), None),
            P(("dp", "fsdp")),
            P(("dp", "fsdp")),
            P(("dp", "fsdp"), None),
            P(("dp", "fsdp"), None),
            P(("dp", "fsdp"), None),
        ),
        check_vma=False,
    )
```

```python
import jax
import jax.numpy as jnp
from jax import lax
from jax.experimental import pallas as pl
from jax.experimental.pallas import tpu as pltpu
from jax.sharding import PartitionSpec as P

HEADS = 16
HEAD_DIM = 64
GROUPS = 2
LATENT = 256


EPSILON = 1e-06


def matmul(left, right):
    return jnp.dot(left, right, preferred_element_type=jnp.float32)


def matmul_left(left, right):
    return lax.dot_general(
        left, right, (((0,), (0,)), ((), ())), preferred_element_type=jnp.float32
    )


def matmul_right(left, right):
    return lax.dot_general(
        left, right, (((1,), (1,)), ((), ())), preferred_element_type=jnp.float32
    )


def segment_mask(lengths, rows):
    position = jnp.arange(rows, dtype=jnp.int32)
    ends = jnp.cumsum(lengths)
    segment = jnp.sum((position[None, :] >= ends[:, None]).astype(jnp.int32), axis=0)
    allowed = (segment[:, None] == segment[None, :]) & (position[None, :] <= position[:, None])
    valid = (position < ends[-1]).astype(jnp.float32)
    return (allowed, valid)


def head_forward(allowed, scale):

    def one_head(operands):
        query, key_rows, value_rows = operands
        scores = jnp.where(allowed, matmul_right(query, key_rows) * scale, -1e30)
        peak = jnp.max(scores, axis=1, keepdims=True)
        expo = jnp.exp(scores - peak)
        total = jnp.sum(expo, axis=1, keepdims=True)
        weights = (expo / total).astype(jnp.bfloat16)
        result = matmul(weights, value_rows).astype(jnp.bfloat16)
        return (result, peak[:, 0] + jnp.log(total[:, 0]))

    return one_head


def head_backward(allowed, scale):

    def one_head(operands):
        query, key_rows, value_rows, grad_out, logsum = operands
        scores = jnp.where(allowed, matmul_right(query, key_rows) * scale, -1e30)
        probs = jnp.exp(scores - logsum[:, None])
        grad_value = matmul_left(probs.astype(jnp.bfloat16), grad_out)
        grad_probs = matmul_right(grad_out, value_rows)
        inner = jnp.sum(probs * grad_probs, axis=1, keepdims=True)
        grad_scores = (probs * (grad_probs - inner)).astype(jnp.bfloat16)
        grad_query = matmul(grad_scores, key_rows) * scale
        grad_key = matmul_left(grad_scores, query) * scale
        return (grad_query, grad_key, grad_value)

    return one_head


def norm_back(grad_normed, inputs, rstd, gain):
    scaled = grad_normed * gain
    grad_in = rstd * (
        scaled - inputs * rstd * rstd * jnp.mean(scaled * inputs, axis=1, keepdims=True)
    )
    grad_gain = jnp.sum(grad_normed * inputs * rstd, axis=0)
    return (grad_in, grad_gain)


def column_term(left, right):
    return matmul_left(left, right).astype(jnp.bfloat16)


def forward(tokens, allowed, attn_w, ffn_w):
    w_query, w_latent, w_keyup, w_valup, w_output, gain_one = attn_w
    gain_two, w_gate, w_up, w_down = ffn_w
    rows = tokens.shape[0]
    inputs = tokens.astype(jnp.float32)
    rstd_one = lax.rsqrt(jnp.mean(inputs * inputs, axis=1, keepdims=True) + EPSILON)
    normed = (inputs * rstd_one * gain_one.astype(jnp.float32)).astype(jnp.bfloat16)
    query = matmul(normed, w_query).astype(jnp.bfloat16)
    latent = matmul(normed, w_latent).astype(jnp.bfloat16)
    lat3 = latent.reshape(rows, GROUPS, LATENT)
    keys = jnp.einsum(
        "tgl,glf->tgf",
        lat3,
        w_keyup.reshape(GROUPS, LATENT, -1),
        preferred_element_type=jnp.float32,
    ).astype(jnp.bfloat16)
    values = jnp.einsum(
        "tgl,glf->tgf",
        lat3,
        w_valup.reshape(GROUPS, LATENT, -1),
        preferred_element_type=jnp.float32,
    ).astype(jnp.bfloat16)
    heads_query = query.reshape(rows, HEADS, HEAD_DIM).transpose(1, 0, 2)
    heads_key = keys.reshape(rows, HEADS, HEAD_DIM).transpose(1, 0, 2)
    heads_value = values.reshape(rows, HEADS, HEAD_DIM).transpose(1, 0, 2)
    attended, logsum = lax.map(
        head_forward(allowed, HEAD_DIM ** (-0.5)), (heads_query, heads_key, heads_value)
    )
    merged = attended.transpose(1, 0, 2).reshape(rows, HEADS * HEAD_DIM)
    middle = inputs + matmul(merged, w_output)
    rstd_two = lax.rsqrt(jnp.mean(middle * middle, axis=1, keepdims=True) + EPSILON)
    normed_two = (middle * rstd_two * gain_two.astype(jnp.float32)).astype(jnp.bfloat16)
    gate = matmul(normed_two, w_gate)
    upper = matmul(normed_two, w_up)
    mixed = (jax.nn.silu(gate) * upper).astype(jnp.bfloat16)
    result = middle + matmul(mixed, w_down)
    return (
        result,
        inputs,
        rstd_one,
        normed,
        lat3,
        heads_query,
        heads_key,
        heads_value,
        logsum,
        merged,
        middle,
        rstd_two,
        normed_two,
        gate,
        upper,
        mixed,
    )


def on_device(
    tokens,
    seq_lengths,
    cotangent,
    w_query,
    w_latent,
    w_keyup,
    w_valup,
    w_output,
    norm_attn,
    norm_ffn,
    w_gate,
    w_up,
    w_down,
):
    rows = tokens.shape[0]
    allowed, valid = segment_mask(seq_lengths, rows)
    attn_w = (
        lax.all_gather(w_query, ("dp", "fsdp"), axis=0, tiled=True),
        lax.all_gather(w_latent, ("dp", "fsdp"), axis=0, tiled=True),
        lax.all_gather(w_keyup, ("dp", "fsdp"), axis=0, tiled=True),
        lax.all_gather(w_valup, ("dp", "fsdp"), axis=0, tiled=True),
        lax.all_gather(w_output, ("dp", "fsdp"), axis=0, tiled=True),
        lax.all_gather(norm_attn, ("dp", "fsdp"), axis=0, tiled=True),
    )
    ffn_w = (
        lax.all_gather(norm_ffn, ("dp", "fsdp"), axis=0, tiled=True),
        lax.all_gather(w_gate, ("dp", "fsdp"), axis=0, tiled=True),
        lax.all_gather(w_up, ("dp", "fsdp"), axis=0, tiled=True),
        lax.all_gather(w_down, ("dp", "fsdp"), axis=0, tiled=True),
    )
    saved = forward(tokens, allowed, attn_w, ffn_w)
    block_out = saved[0].astype(jnp.bfloat16)
    (
        result,
        inputs,
        rstd_one,
        normed,
        lat3,
        heads_query,
        heads_key,
        heads_value,
        logsum,
        merged,
        middle,
        rstd_two,
        normed_two,
        gate,
        upper,
        mixed,
    ) = saved
    full_query, full_latent, full_keyup, full_valup, full_output, gain_one = attn_w
    gain_two, full_gate, full_up, full_down = ffn_w
    ff_width = full_gate.shape[1]
    grad_out = cotangent.astype(jnp.float32) * valid[:, None]
    grad_low = grad_out.astype(jnp.bfloat16)
    grad_mixed = matmul_right(grad_low, full_down)
    sigmoid_gate = jax.nn.sigmoid(gate)
    grad_gate_low = (
        grad_mixed * upper * sigmoid_gate * (1.0 + gate * (1.0 - sigmoid_gate))
    ).astype(jnp.bfloat16)
    grad_upper_low = (grad_mixed * jax.nn.silu(gate)).astype(jnp.bfloat16)
    grad_normed_two = matmul_right(grad_gate_low, full_gate) + matmul_right(grad_upper_low, full_up)
    grad_mid_norm, grad_gain_two = norm_back(
        grad_normed_two, middle, rstd_two, gain_two.astype(jnp.float32)
    )
    grad_middle = grad_out + grad_mid_norm
    down_own = lax.psum_scatter(
        column_term(mixed, grad_low), ("dp", "fsdp"), scatter_dimension=0, tiled=True
    )
    packed_ffn = jnp.concatenate([grad_gate_low, grad_upper_low], axis=1)
    ffn_own = lax.psum_scatter(
        column_term(normed_two, packed_ffn), ("dp", "fsdp"), scatter_dimension=0, tiled=True
    )
    grad_branch = grad_middle.astype(jnp.bfloat16)
    grad_merged = matmul_right(grad_branch, full_output).astype(jnp.bfloat16)
    output_own = lax.psum_scatter(
        column_term(merged, grad_branch), ("dp", "fsdp"), scatter_dimension=0, tiled=True
    )
    heads_grad = grad_merged.reshape(rows, HEADS, HEAD_DIM).transpose(1, 0, 2)
    grad_hq, grad_hk, grad_hv = lax.map(
        head_backward(allowed, HEAD_DIM ** (-0.5)),
        (heads_query, heads_key, heads_value, heads_grad, logsum),
    )
    grad_query_low = grad_hq.transpose(1, 0, 2).reshape(rows, HEADS * HEAD_DIM).astype(jnp.bfloat16)
    grad_keys_low = grad_hk.transpose(1, 0, 2).reshape(rows, GROUPS, -1).astype(jnp.bfloat16)
    grad_values_low = grad_hv.transpose(1, 0, 2).reshape(rows, GROUPS, -1).astype(jnp.bfloat16)
    head_cols = grad_keys_low.shape[2]
    keyup3 = full_keyup.reshape(GROUPS, LATENT, -1)
    valup3 = full_valup.reshape(GROUPS, LATENT, -1)
    grad_lat = jnp.einsum("tgf,glf->tgl", grad_keys_low, keyup3, preferred_element_type=jnp.float32)
    grad_lat = grad_lat + jnp.einsum(
        "tgf,glf->tgl", grad_values_low, valup3, preferred_element_type=jnp.float32
    )
    grad_latent_low = grad_lat.reshape(rows, GROUPS * LATENT).astype(jnp.bfloat16)
    latent_flat = lat3.reshape(rows, GROUPS * LATENT)
    paired = jnp.concatenate([grad_keys_low, grad_values_low], axis=2).reshape(
        rows, GROUPS * 2 * head_cols
    )
    count = w_keyup.shape[0] * lax.axis_size(("dp", "fsdp"))
    product = matmul_left(latent_flat, paired).reshape(count, GROUPS, 2 * head_cols)
    owner = jnp.arange(count, dtype=jnp.int32) // LATENT
    picker = (owner[:, None] == jnp.arange(GROUPS, dtype=jnp.int32)[None, :]).astype(jnp.float32)
    latent_own = lax.psum_scatter(
        jnp.sum(product * picker[:, :, None], axis=1).astype(jnp.bfloat16),
        ("dp", "fsdp"),
        scatter_dimension=0,
        tiled=True,
    )
    grad_normed = matmul_right(grad_query_low, full_query) + matmul_right(
        grad_latent_low, full_latent
    )
    packed_attn = jnp.concatenate([grad_query_low, grad_latent_low], axis=1)
    attn_own = lax.psum_scatter(
        column_term(normed, packed_attn), ("dp", "fsdp"), scatter_dimension=0, tiled=True
    )
    grad_in_norm, grad_gain_one = norm_back(
        grad_normed, inputs, rstd_one, gain_one.astype(jnp.float32)
    )
    grad_tokens = grad_middle + grad_in_norm
    gains_own = (
        lax.psum_scatter(grad_gain_one, ("dp", "fsdp"), scatter_dimension=0, tiled=True),
        lax.psum_scatter(grad_gain_two, ("dp", "fsdp"), scatter_dimension=0, tiled=True),
    )
    query_cols = HEADS * HEAD_DIM
    return (
        block_out,
        grad_tokens,
        attn_own[:, :query_cols].astype(jnp.float32),
        attn_own[:, query_cols:].astype(jnp.float32),
        latent_own[:, :head_cols].astype(jnp.float32),
        latent_own[:, head_cols:].astype(jnp.float32),
        output_own.astype(jnp.float32),
        gains_own[0],
        gains_own[1],
        ffn_own[:, :ff_width].astype(jnp.float32),
        ffn_own[:, ff_width:].astype(jnp.float32),
        down_own.astype(jnp.float32),
    )


MESH = pl.DeviceIdType.MESH
F32 = jnp.float32
BF16 = jnp.bfloat16
SCALE = HEAD_DIM ** (-0.5)
ROWS = 256
WIDTH = 1024
HALF = 1408
PARTS = (768, 640)
FFN = 1 + 2 * len(PARTS)
PUT = 20
DOWN = 88


ROUTE = ("y21xs", "y21xs", "21xys", "21yxs")
SUM_X_FIRST = (True, False, True, True)


class Slots:
    def __init__(self):
        self.count = 0

    def take(self, number):
        first = self.count
        self.count += number
        return first


SLOTS = Slots()
S_A = [SLOTS.take(32) for _ in range(4)]
S_HALF = SLOTS.take(FFN)
S_F = [SLOTS.take(16) for _ in range(FFN)]
S_COT, S_TOK, S_DN2, S_OUT, S_END = (SLOTS.take(n) for n in (4, 4, 1, 4, 1))
S_R = [SLOTS.take(10) for _ in range(FFN + 4)]
S_SUM = SLOTS.take(5)


def nn(left, right):
    return jnp.dot(left, right, preferred_element_type=F32)


def nt(left, right):
    return lax.dot_general(left, right, (((1,), (1,)), ((), ())), preferred_element_type=F32)


def tn(left, right):
    return lax.dot_general(left, right, (((0,), (0,)), ((), ())), preferred_element_type=F32)


(
    AA, AG, AT, H_S, H_R, FA, FG, FT, COT_S, COT_R, TOK_S, TOK_R, END_S, END_R, DN2_S, DN2_R, OUT_S,
    OUT_R, R_GO, R_S, R_B, R_A, R_1, R_2, R_L, R_E, SUM_S, SUM_R,
) = range(28)
(
    G_START, G_WEIGHTS, G_ACROSS, G_DOWN_W, G_QUERY, G_OUTPUT_W, G_FFN_A, G_FFN_B, G_BACK, G_RESULT,
    G_TAIL, G_MASK, G_NORM, G_LATENT, G_KEYS, G_NORM_P, G_LATENT_P, G_KEYS_P, G_COMPACT, G_ATTEND,
    G_QUERY_P, G_ATTEND_P, G_MIDDLE, G_NORM2, G_MIDDLE_P, G_NORM2_P, G_HIDDEN_A, G_DN_A, G_GATEUP_A,
    G_DN_B, G_HIDDEN_B, G_DOWN, G_GATEUP_B, G_OUT, G_OUTPUT, G_ATTENDB, G_PROJQ, G_PROJL, G_DNORMED,
    G_NORM1B, G_GAIN, G_NORM2B, G_DMERGED, G_LATENTB,
) = range(44)
PLAN = {
    G_START: (
        (H_S, 2), (AA, 2, 0), (AG, 2, 0, 1), (H_S, 1), (H_S, 4), (H_S, 3), (FA, 0, 0), (AA, 0, 0),
    ),
    (G_MASK, 3): (
        (TOK_S, 2), (AA, 1, 0), (FG, 0, 0, 0), (FG, 0, 0, 1),
    ),
    G_WEIGHTS: (
        (AG, 1, 0, 0), (AG, 0, 0, 1), (H_R, 4), (AG, 0, 0, 2), (TOK_S, 1), (TOK_S, 0), (AA, 3, 0),
        (FA, 4, 0), (AG, 0, 0, 0), (AA, 0, 1), (AG, 2, 0, 0), (AA, 1, 1), (AG, 3, 0, 1), (H_R, 2),
        (H_R, 1), (TOK_S, 3), (FG, 0, 0, 2), (AG, 0, 1, 1), (FA, 0, 1), (FG, 0, 1, 2), (AG, 0, 1, 2),
        (FA, 0, 2), (H_R, 3), (AG, 3, 0, 0), (AG, 0, 1, 3), (AA, 2, 1), (FA, 1, 0), (AA, 0, 2),
        (AG, 0, 2, 2), (AG, 0, 0, 3), (AG, 2, 1, 2), (AG, 2, 1, 1), (FG, 1, 0, 2), (AA, 0, 3),
        (FA, 2, 0), (AA, 3, 2), (AG, 1, 0, 1), (AG, 1, 0, 3), (FG, 2, 0, 2), (AG, 2, 1, 3),
        (AG, 0, 2, 3), (AG, 3, 0, 2), (AA, 0, 4), (AG, 1, 0, 2), (AA, 2, 5), (FG, 4, 0, 2),
        (AG, 0, 3, 2), (AA, 2, 2), (FA, 3, 0), (AG, 0, 3, 3), (AG, 1, 1, 1), (FA, 2, 4),
        (FG, 0, 1, 1), (AG, 2, 5, 3), (AA, 1, 8), (FG, 1, 0, 0), (AA, 3, 1), (AA, 0, 8), (AA, 2, 3),
        (AG, 2, 0, 2), (AG, 0, 4, 3), (FA, 0, 5), (AG, 1, 1, 2), (FG, 0, 2, 2), (AA, 0, 6),
        (AA, 0, 5), (AG, 3, 1, 2), (AG, 0, 6, 3), (AA, 0, 7), (FA, 0, 4), (AA, 0, 11), (AG, 0, 5, 3),
        (AG, 2, 3, 2), (AA, 0, 9), (AA, 3, 4), (AA, 1, 2), (AG, 3, 2, 2), (FA, 1, 4), (AA, 1, 3),
        (AG, 3, 1, 1), (AG, 0, 7, 3), (AA, 0, 13), (AG, 2, 2, 3), (AG, 1, 1, 3), (AA, 1, 4),
        (AA, 2, 9), (AA, 2, 4), (AG, 1, 2, 3), (AG, 1, 2, 2), (AG, 2, 2, 2), (AA, 2, 7), (AA, 2, 13),
        (END_S,), (AA, 0, 10), (FA, 0, 3), (FG, 0, 3, 2), (AA, 0, 12), (AG, 1, 3, 2), (FA, 4, 4),
        (AA, 0, 15), (FG, 2, 0, 0), (AA, 0, 14), (AG, 1, 3, 3), (TOK_R,), (AT, 0), (FG, 3, 0, 2),
        (AA, 2, 10), (AA, 1, 5), (FA, 1, 1), (AG, 1, 4, 3), (FG, 1, 0, 1),
    ),
    (G_NORM, 3): (
        (AA, 3, 3), (AA, 3, 5), (AG, 2, 3, 3), (AG, 2, 4, 3),
    ),
    (G_LATENT, 1): (
        (FG, 4, 0, 0), (AA, 1, 6), (AG, 1, 5, 3), (AA, 3, 6),
    ),
    (G_KEYS, 1): (
        (AG, 3, 3, 2), (FA, 0, 6), (AG, 2, 7, 3),
    ),
    G_ACROSS: (
        (AA, 2, 6), (FA, 0, 7), (AA, 1, 7), (AG, 1, 6, 3), (FG, 2, 0, 1), (FG, 1, 1, 1),
        (FG, 1, 1, 2), (END_R,), (AA, 1, 9),
    ),
    (G_NORM_P, 3): (
        (AG, 1, 7, 3), (FT, 0),
    ),
    (G_LATENT_P, 1): (
        (AA, 1, 12), (AA, 3, 7), (AG, 2, 0, 3), (AG, 3, 0, 3),
    ),
    (G_KEYS_P, 1): (
        (AG, 3, 5, 3), (FA, 2, 1), (AA, 1, 14),
    ),
    G_DOWN_W: (
        (AA, 1, 11), (AG, 3, 4, 3), (AG, 3, 3, 3), (FG, 3, 0, 0), (FG, 2, 1, 2), (FG, 2, 1, 1),
        (AA, 1, 13), (AG, 2, 6, 3),
    ),
    (G_COMPACT, 7): (
        (FG, 3, 0, 1), (AG, 3, 7, 3),
    ),
    G_QUERY: (
        (AG, 3, 6, 3), (AA, 1, 15), (AA, 1, 10), (FA, 1, 5), (AG, 3, 2, 3), (FA, 1, 2),
        (FG, 1, 2, 2), (AG, 3, 1, 3), (AA, 2, 8), (COT_S, 2), (COT_S, 1), (AT, 1), (FA, 4, 1),
        (AA, 2, 15), (AA, 2, 11),
    ),
    (G_QUERY, 3): (
        (AA, 2, 12),
    ),
    (G_ATTEND, 3): (
        (AA, 2, 14), (FG, 4, 1, 2), (AA, 3, 8), (AA, 3, 13),
    ),
    (G_ATTEND, 7): (
        (FA, 1, 3), (FG, 1, 3, 2), (FG, 4, 0, 1), (AA, 3, 12), (AA, 3, 10), (FA, 2, 2),
    ),
    (G_QUERY_P, 3): (
        (FA, 1, 6), (AT, 2), (FG, 4, 1, 1), (AA, 3, 14), (FA, 2, 5), (AA, 3, 15), (COT_S, 3),
        (AA, 3, 11), (FG, 2, 2, 2), (FA, 3, 1), (AA, 3, 9), (FG, 3, 1, 1),
    ),
    (G_ATTEND_P, 3): (
        (FA, 2, 3), (AT, 3), (FG, 2, 3, 2),
    ),
    G_OUTPUT_W: (
        (COT_S, 0), (FA, 1, 7),
    ),
    (G_MIDDLE, 3): (
        (FA, 3, 2), (FG, 3, 2, 2),
    ),
    (G_NORM2, 3): (
        (FG, 3, 1, 2), (FA, 4, 5), (FA, 2, 6), (FA, 4, 2),
    ),
    (G_MIDDLE_P, 3): (
        (FA, 2, 7), (FG, 4, 2, 2),
    ),
    (G_NORM2_P, 3): (
        (FA, 3, 4), (FT, 1),
    ),
    G_FFN_A: (
        (FT, 2),
    ),
    (G_HIDDEN_A, 0): (
        (FA, 3, 3), (FA, 4, 3), (FG, 3, 3, 2), (COT_R,),
    ),
    (G_DN_A, 0): (
        (FG, 4, 3, 2),
    ),
    (G_GATEUP_A, 1): (
        (R_GO, 1), (FA, 3, 5),
    ),
    (G_GATEUP_A, 3): (
        (FA, 4, 6), (FA, 3, 7), (FA, 3, 6), (R_S, 1, 1), (R_B, 1, 3),
    ),
    G_FFN_B: (
        (R_B, 1, 1), (FA, 4, 7), (R_B, 1, 2), (R_S, 1, 0), (R_GO, 2), (FT, 3), (FT, 4),
    ),
    (G_DN_B, 1): (
        (DN2_S,), (R_S, 2, 1),
    ),
    (G_HIDDEN_B, 0): (
        (R_B, 2, 3),
    ),
    (G_DN_B, 0): (
        (R_B, 2, 1), (R_A, 1, 3),
    ),
    (G_DOWN, 0): (
        (R_GO, 0), (R_A, 1, 1), (R_S, 2, 0),
    ),
    (G_GATEUP_B, 1): (
        (R_S, 0, 1), (R_GO, 3), (R_B, 0, 3), (R_A, 2, 3), (R_A, 1, 2), (R_GO, 4), (R_S, 0, 0),
    ),
    (G_GATEUP_B, 3): (
        (R_S, 3, 1), (R_A, 2, 1),
    ),
    (G_OUT, 0): (
        (R_B, 2, 2), (OUT_S, 1), (OUT_S, 2), (R_S, 4, 1), (R_1, 1, 1), (R_B, 3, 1), (R_S, 3, 0),
    ),
    (G_OUT, 1): (
        (R_B, 3, 3), (R_B, 0, 2), (OUT_S, 0), (R_B, 4, 3), (R_A, 0, 3), (R_B, 1, 0),
    ),
    G_BACK: (
        (DN2_R,),
    ),
    (G_OUTPUT, 1): (
        (R_A, 2, 2), (R_1, 2, 1), (OUT_S, 3),
    ),
    (G_OUTPUT, 3): (
        (R_GO, 5),
    ),
    (G_ATTENDB, 3): (
        (R_A, 3, 1), (R_A, 3, 3),
    ),
    (G_PROJQ, 1): (
        (R_S, 5, 1), (R_A, 0, 2),
    ),
    (G_PROJQ, 3): (
        (R_B, 5, 1), (R_1, 0, 1), (R_S, 4, 0), (R_A, 4, 3), (R_B, 4, 1),
    ),
    (G_PROJL, 1): (
        (R_B, 5, 3), (R_B, 4, 2), (R_S, 5, 0), (R_GO, 6), (R_B, 3, 2),
    ),
    (G_PROJL, 3): (
        (R_GO, 7), (R_B, 2, 0), (OUT_R,), (R_A, 5, 1), (R_B, 5, 0),
    ),
    (G_DNORMED, 3): (
        (R_S, 6, 1),
    ),
    (G_NORM1B, 7): (
        (R_B, 4, 0), (R_B, 3, 0), (R_A, 4, 2), (R_A, 5, 3), (R_GO, 8), (R_S, 7, 1), (R_S, 8, 0),
        (R_B, 6, 3), (R_A, 1, 0),
    ),
    G_RESULT: (
        (R_1, 4, 1), (R_1, 1, 0), (R_A, 4, 1), (R_B, 5, 2), (R_B, 6, 2), (R_B, 7, 1), (R_A, 2, 0),
    ),
    (G_RESULT, 7): (
        (R_A, 3, 2), (SUM_S, 0), (R_B, 0, 0), (SUM_R, 0), (R_1, 3, 1), (R_A, 3, 0), (R_A, 4, 0),
        (R_S, 8, 1), (R_S, 7, 0), (R_A, 5, 0), (R_B, 8, 3), (R_A, 5, 2), (SUM_S, 1), (R_B, 7, 2),
        (R_B, 8, 0), (R_1, 3, 0), (R_S, 6, 0), (R_2, 1), (R_A, 6, 3), (R_1, 2, 0), (R_B, 6, 1),
        (R_B, 8, 1), (R_B, 7, 0), (R_1, 5, 1), (R_A, 8, 3), (R_1, 5, 0), (R_A, 8, 0), (R_A, 6, 2),
        (R_B, 0, 1), (R_B, 6, 0), (R_B, 8, 2), (R_B, 7, 3), (R_A, 8, 1), (R_2, 2),
    ),
    G_TAIL: (
        (R_1, 6, 1), (R_A, 7, 1), (R_2, 3), (R_A, 8, 2), (R_1, 8, 0), (SUM_R, 1), (R_1, 4, 0),
        (R_A, 7, 3), (SUM_S, 2), (R_1, 8, 1), (R_A, 6, 1), (R_L, 3), (R_A, 6, 0), (R_A, 7, 2),
        (R_2, 4), (SUM_R, 2), (SUM_S, 3), (R_L, 1), (R_1, 7, 1), (R_2, 8), (R_A, 7, 0), (R_2, 5),
        (R_L, 4), (R_L, 5), (R_L, 8), (R_E, 3), (R_A, 0, 0), (R_A, 0, 1), (R_L, 2), (SUM_R, 3),
        (R_1, 7, 0), (R_E, 1), (R_1, 6, 0), (SUM_S, 4), (R_2, 6), (R_E, 2), (R_L, 6), (R_2, 7),
        (R_L, 7), (R_1, 0, 0), (R_E, 4), (R_E, 5), (R_E, 8), (R_2, 0), (R_E, 7), (R_E, 6),
        (SUM_R, 4), (R_L, 0),
    ),
}


def layer_kernel(
    tok_hbm, len_ref, cot_hbm, wq_hbm, wl_hbm, wk_hbm, wv_hbm, wo_hbm, gain_one, gain_two, wg_hbm, wu_hbm, wd_ref,
    out_hbm, gtok_hbm, at_hbm, gain_hbm, gg_hbm, gu_hbm, gd_hbm,
    attn, latw, gate_a, up_a, gate_b, up_b, down_w, down_c, gain_full,
    tok, ends, bias, normed, query, latent, keys, values, merged, lse, middle, normed2, dout,
    mixed, dgate, dup, tmp, rcv_dn2, snd_out, rcv_out,
    dmid, dmid_low, dmerged, dquery, dkeys, dvalues, dlatent,
    pattn,
    s_d, s_ga, s_ua, s_gb, s_ub,
    y_d, y_ga, y_ua, y_gb, y_ub,
    z_d, z_ga, z_ua, z_gb, z_ub,
    x_ga, x_ua, x_gb, x_ub,
    s_a, x_a, z_a, y_a, sum_own, sum_rcv,
    send_sem, recv_sem, local_sem,
):
    snd_dn2 = dquery
    dp = lax.axis_index("dp")
    fs = lax.axis_index("fsdp")
    x, c, z, y = lax.div(dp, 2), lax.rem(dp, 2), lax.div(fs, 2), lax.rem(fs, 2)
    zh, zl = lax.div(z, 2), lax.rem(z, 2)
    sib = (x * 2 + 1 - c, fs)
    xp = ((1 - x) * 2 + c, fs)
    yp = (dp, z * 2 + 1 - y)
    z1 = (dp, (zh * 2 + 1 - zl) * 2 + y)
    z2 = (dp, ((1 - zh) * 2 + zl) * 2 + y)

    def rel(v, other):
        return 1 - v if other else v

    def line(dh, dl):
        return rel(zh, dh) * 2 + rel(zl, dl)

    sent = {}
    now = {"op": None, "wait": None}

    def copy(src, dst, slot, target):
        return pltpu.make_async_remote_copy(
            src_ref=src, dst_ref=dst, send_sem=send_sem.at[slot], recv_sem=recv_sem.at[slot],
            device_id=target, device_id_type=MESH,
        )

    def send(group, src, dst, slot, target):
        if now["wait"] is None:
            copy(src, dst, slot, target).start()
            users = sent.setdefault(group, [])
            if now["op"] not in users:
                users.append(now["op"])
        elif now["wait"] == group:
            copy(src, dst, slot, target).wait_send()

    def arrive(dst, slot):
        if now["wait"] is None:
            copy(dst, dst, slot, sib).wait_recv()

    def local(src, dst, k):
        return pltpu.make_async_copy(src, dst, local_sem.at[k])

    def put(src, dst, k):
        if now["wait"] is None:
            local(src, dst, k).start()

    def add(dst, src):
        if now["wait"] is None:
            dst[...] = dst[...] + src[...]

    def cols(n, width=256):
        return pl.ds(pl.multiple_of(n * width, width), width)

    ops = {}

    def op(code):
        def enter(fn):
            ops[code] = fn
            return fn

        return enter

    def run(items, wait=None):
        now["wait"] = wait
        for name, *rest in items:
            now["op"] = (name, *rest)
            ops[name](*rest)
        now["wait"] = None

    def drain(group):
        run(sent.pop(group, []), group)

    def gap(name):
        run(PLAN.get(name, ()))

    def loop(count, *stages, at=(), unroll=1):
        ends = [*at, count]
        for first, last in zip([0, *at], ends):

            def step(k, carry):
                for _, body in stages:
                    body(k)
                return carry

            if last - first == 1:
                for name, body in stages:
                    body(first)
                    gap((name, first))
            else:
                lax.fori_loop(first, last, step, 0, unroll=unroll)
                gap((stages[-1][0], last - 1))

    ways = {"y": yp, "x": xp, "1": z1, "2": z2, "s": sib}

    def a_blk(w, bits):
        route = ROUTE[w]
        across = {way: bits >> k & 1 for k, way in enumerate(route)}
        xx, cc, yy = rel(x, across["x"]), rel(c, across["s"]), rel(y, across["y"])
        zz = line(across["2"], across["1"])
        if w == 0:
            return latw.at[xx, cc, zz, yy]
        if w == 1:
            return attn.at[0, xx, cc, zz, yy]
        return attn.at[1, xx, cc, zz, yy, :, pl.ds(512 * (w - 2), 512)]

    def a_send(w, bits, k):
        blk = a_blk(w, bits)
        send("attn", blk, blk, S_A[w] + bits + (1 << k), ways[ROUTE[w][k]])

    @op(AA)
    def aa(w, bits):
        if bits:
            arrive(a_blk(w, bits), S_A[w] + bits)
        a_send(w, bits, 4)

    @op(AG)
    def ag(w, bits, k):
        a_send(w, bits, k)

    @op(AT)
    def at(w):
        for bits in range(16, 32):
            arrive(a_blk(w, bits), S_A[w] + bits)

    ffn = (down_w, gate_a, up_a, gate_b, up_b)
    ffn_hbm = (None, wg_hbm, wu_hbm, wg_hbm, wu_hbm)
    starts = (None, 0, 0, 768, 768)

    def half_cols(xx, t):
        return pl.ds(pl.multiple_of(xx * HALF + starts[t], 128), ffn[t].shape[-1])

    @op(H_S)
    def h_s(t):
        send("half", ffn_hbm[t].at[:, half_cols(1 - x, t)], ffn[t].at[c, z, y, x], S_HALF + t, xp)

    @op(H_R)
    def h_r(t):
        arrive(ffn[t].at[c, z, y, 1 - x], S_HALF + t)

    def f_blk(t, bits):
        return ffn[t].at[rel(c, bits >> 3 & 1), line(bits & 1, bits >> 1 & 1), rel(y, bits >> 2 & 1)]

    def f_send(t, bits, k):
        blk = f_blk(t, bits)
        send("ffn%d" % t, blk, blk, S_F[t] + bits + (1 << k), (z2, z1, yp, sib)[k])

    @op(FA)
    def fa(t, bits):
        if bits:
            arrive(f_blk(t, bits), S_F[t] + bits)
        f_send(t, bits, 3)

    @op(FG)
    def fg(t, bits, k):
        f_send(t, bits, k)

    @op(FT)
    def ft(t):
        for bits in range(8, 16):
            arrive(f_blk(t, bits), S_F[t] + bits)

    def quarter(ref, k):
        return ref.at[pl.ds(k * 64, 64)]

    @op(COT_S)
    def cot_s(k):
        send("cot", quarter(dout.at[x], k), quarter(dout.at[x], k), S_COT + k, xp)

    @op(COT_R)
    def cot_r():
        for k in range(4):
            arrive(quarter(dout.at[1 - x], k), S_COT + k)

    @op(TOK_S)
    def tok_s(k):
        send("tok", quarter(tok.at[x], k), quarter(tok.at[x], k), S_TOK + k, xp)

    @op(TOK_R)
    def tok_r():
        for k in range(4):
            arrive(quarter(tok.at[1 - x], k), S_TOK + k)

    @op(END_S)
    def end_s():
        send("tok", ends.at[x], ends.at[x], S_END, xp)

    @op(END_R)
    def end_r():
        arrive(ends.at[1 - x], S_END)

    @op(DN2_S)
    def dn2_s():
        send("dn2", snd_dn2, rcv_dn2, S_DN2, xp)

    @op(DN2_R)
    def dn2_r():
        arrive(rcv_dn2, S_DN2)

    @op(OUT_S)
    def out_s(k):
        send("out", quarter(snd_out, k), quarter(rcv_out, k), S_OUT + k, xp)

    @op(OUT_R)
    def out_r():
        for k in range(4):
            arrive(quarter(rcv_out, k), S_OUT + k)

    ffn_s = (s_d, s_ga, s_ua, s_gb, s_ub)
    ffn_y = (y_d, y_ga, y_ua, y_gb, y_ub)
    ffn_zb = (z_d, z_ga, z_ua, z_gb, z_ub)
    ffn_x = (None, x_ga, x_ua, x_gb, x_ub)
    out_cols = (None, *[pl.ds(starts[t], ffn[t].shape[-1]) for t in range(1, FFN)])
    ffn_out = (None, *[gg_hbm, gu_hbm] * 2)

    def pick(i):
        return ((0, pl.ds(0, WIDTH)), (1, pl.ds(0, WIDTH)), (2, pl.ds(0, 512)), (2, pl.ds(512, 512)))[i - FFN]

    def sib_part(i, other):
        if i < FFN:
            yy = rel(y, other)
            return yy, ffn[i].at[1 - c, :, yy], ffn_s[i].at[yy], lambda zz: (ffn[i].at[c, zz, yy], ffn_s[i].at[yy, zz])
        k, cl = pick(i)
        if SUM_X_FIRST[i - FFN]:
            xx = rel(x, other)
            return (
                xx,
                pattn.at[k, xx, 1 - c, :, :, :, cl],
                s_a.at[k, xx, :, :, :, cl],
                lambda zz: (pattn.at[k, xx, c, zz, :, :, cl], s_a.at[k, xx, zz, :, :, cl]),
            )
        yy = rel(y, other)
        return (
            yy,
            pattn.at[k, :, 1 - c, :, yy, :, cl],
            s_a.at[k, :, :, yy, :, cl],
            lambda zz: (pattn.at[k, :, c, zz, yy, :, cl], s_a.at[k, :, zz, yy, :, cl]),
        )

    def first_hop(i, d):
        if i < FFN:
            return yp, ffn[i].at[c, d, 1 - y], ffn_y[i].at[d]
        k, cl = pick(i)
        if SUM_X_FIRST[i - FFN]:
            return xp, pattn.at[k, 1 - x, c, d, :, :, cl], x_a.at[k, d, :, :, cl]
        return yp, pattn.at[k, :, c, d, 1 - y, :, cl], x_a.at[k, d, :, :, cl]

    def line_blk(i, d):
        if i < FFN:
            return ffn[i].at[c, d, y]
        k, cl = pick(i)
        if SUM_X_FIRST[i - FFN]:
            return pattn.at[k, x, c, d, :, :, cl]
        return pattn.at[k, :, c, d, y, :, cl]

    def line_buf(i, b):
        if i < FFN:
            return ffn_zb[i].at[b]
        k, cl = pick(i)
        return z_a.at[k, b, :, :, cl]

    def last_hop(i):
        if i < FFN:
            return xp, ffn[i].at[c, z, y, 1 - x], ffn_x[i]
        k, cl = pick(i)
        if SUM_X_FIRST[i - FFN]:
            return yp, pattn.at[k, x, c, z, 1 - y, :, cl], y_a.at[k, :, cl]
        return xp, pattn.at[k, 1 - x, c, z, y, :, cl], y_a.at[k, :, cl]

    @op(R_GO)
    def r_go(i):
        for other in (1, 0):
            k, src, dst, _ = sib_part(i, other)
            send("r", src, dst, S_R[i] + k, sib)

    @op(R_S)
    def r_s(i, other):
        k, _, dst, pairs = sib_part(i, other)
        arrive(dst, S_R[i] + k)
        if not other:
            for zz in range(4):
                add(*pairs(zz))

    @op(R_B)
    def r_b(i, bits):
        d = line(bits >> 1, bits & 1)
        add(*sib_part(i, 1)[3](d))
        target, src, buf = first_hop(i, d)
        send("r", src, buf, S_R[i] + 2 + bits, target)

    @op(R_A)
    def r_a(i, bits):
        d = line(bits >> 1, bits & 1)
        _, _, buf = first_hop(i, d)
        arrive(buf, S_R[i] + 2 + bits)
        add(line_blk(i, d), buf)
        if bits & 1:
            send("r", line_blk(i, d), line_buf(i, bits >> 1), S_R[i] + 6 + (bits >> 1), z1)

    @op(R_1)
    def r_1(i, dh):
        d = line(dh, 0)
        arrive(line_buf(i, dh), S_R[i] + 6 + dh)
        add(line_blk(i, d), line_buf(i, dh))
        if dh:
            send("r", line_blk(i, d), line_buf(i, 2), S_R[i] + 8, z2)

    @op(R_2)
    def r_2(i):
        arrive(line_buf(i, 2), S_R[i] + 8)
        add(line_blk(i, z), line_buf(i, 2))

    @op(R_L)
    def r_l(i):
        if i == 0:
            put(down_w.at[c, z, y], gd_hbm, PUT)
            return
        target, src, buf = last_hop(i)
        send("r", src, buf, S_R[i] + 9, target)
        if i < FFN:
            put(ffn[i].at[c, z, y, x], ffn_out[i].at[x, :, out_cols[i]], PUT + i * 2)

    @op(R_E)
    def r_e(i):
        _, _, buf = last_hop(i)
        arrive(buf, S_R[i] + 9)
        if i < FFN:
            put(buf, ffn_out[i].at[1 - x, :, out_cols[i]], PUT + 1 + i * 2)
        else:
            k, cl = pick(i)
            blk = pattn.at[k, x, c, z, y, :, cl]
            add(blk, buf)
            put(blk, at_hbm.at[k, :, cl], PUT + 4 + FFN + i)

    def wait_out():
        local(down_w.at[c, z, y], gd_hbm, PUT).wait()
        for i in range(1, FFN):
            local(ffn[i].at[c, z, y, x], ffn_out[i].at[x, :, out_cols[i]], PUT + i * 2).wait()
            local(ffn_x[i], ffn_out[i].at[1 - x, :, out_cols[i]], PUT + 1 + i * 2).wait()
        for i in range(FFN, FFN + 4):
            k, cl = pick(i)
            local(pattn.at[k, x, c, z, y, :, cl], at_hbm.at[k, :, cl], PUT + 4 + FFN + i).wait()

    sum_to = (sib, yp, xp, z1, z2)

    @op(SUM_S)
    def sum_s(i):
        copy(sum_own, sum_rcv.at[i], S_SUM + i, sum_to[i]).start()

    @op(SUM_R)
    def sum_r(i):
        copy(sum_own, sum_rcv.at[i], S_SUM + i, sum_to[i]).wait_send()
        arrive(sum_rcv.at[i], S_SUM + i)
        add(sum_own, sum_rcv.at[i])

    loads = [
        (wq_hbm, attn.at[0, x, c, z, y]),
        (wl_hbm, latw.at[x, c, z, y, :, pl.ds(0, 512)]),
        (wk_hbm, latw.at[x, c, z, y, pl.ds(0, 16), pl.ds(512, 512)]),
        (wv_hbm, latw.at[x, c, z, y, pl.ds(16, 16), pl.ds(512, 512)]),
        (wo_hbm, attn.at[1, x, c, z, y]),
        (tok_hbm, tok.at[x]),
        (cot_hbm, dout.at[x]),
        *[(ffn_hbm[t].at[:, half_cols(x, t)], ffn[t].at[c, z, y, x]) for t in range(1, FFN)],
    ]
    loads = [local(src, dst, k) for k, (src, dst) in enumerate(loads)]
    for load in loads:
        load.start()
    bar = pltpu.get_barrier_semaphore()

    def hello(target):
        pl.semaphore_signal(bar, inc=1, device_id=target, device_id_type=MESH)

    for target in (sib, xp, yp, z1, z2):
        hello(target)

    def piled(rows):
        return jnp.concatenate([rows[:, 0:512], rows[:, 512:WIDTH]], axis=0).astype(BF16)

    def stage_own():
        down_w[c, z, y] = piled(wd_ref[...].astype(F32))
        lane = lax.broadcasted_iota(jnp.int32, (16, 128), 1)
        mine = lax.div(lane, 32) == lax.rem(fs, 4)
        two = [ref[...].astype(F32).reshape(1, 32) for ref in (gain_one, gain_two)]
        two = jnp.concatenate([*two, jnp.zeros((14, 32), F32)], axis=0)
        two = jnp.where(mine, jnp.concatenate([two] * 4, axis=1), 0.0)
        latw[x, c, z, y, pl.ds(0, 16), pl.ds(WIDTH, 128)] = two.astype(BF16)
        latw[x, c, z, y, pl.ds(16, 16), pl.ds(WIDTH, 128)] = jnp.zeros((16, 128), BF16)

    e0 = len_ref[0]
    e1 = e0 + len_ref[1]
    e2 = e1 + len_ref[2]
    e3 = e2 + len_ref[3]

    def stage_ends():
        place = lax.broadcasted_iota(jnp.int32, (8, 128), 0)
        ends[x] = sum(jnp.where(place == k, e, 0) for k, e in enumerate((e0, e1, e2, e3))).astype(F32)

    stage_own()
    stage_ends()
    for load in loads[:5]:
        load.wait()
    pl.semaphore_wait(bar, 5)
    gap(G_START)

    for load in loads[5:]:
        load.wait()

    def mask_rows(k):
        rows = pl.ds(pl.multiple_of(k * 64, 64), 64)
        position = lax.broadcasted_iota(jnp.int32, (64, WIDTH), 0) + k * 64
        dout[x, rows] = jnp.where(position < e3, dout[x, rows].astype(F32), 0.0).astype(BF16)

    loop(4, (G_MASK, mask_rows))
    gap(G_WEIGHTS)

    def gain_rows(k):
        g = latw.at[lax.div(k, 4), lax.div(lax.rem(k, 4), 2)]
        part = g[pl.ds(lax.rem(k, 2) * 2, 2), :, 0:16, WIDTH : WIDTH + 128].astype(F32)
        gain_full[:, pl.ds(pl.multiple_of(k * 128, 128), 128)] = part[0, 0] + part[0, 1] + part[1, 0] + part[1, 1]

    loop(8, (G_GAIN, gain_rows))

    low_half = lax.broadcasted_iota(jnp.int32, (ROWS, 128), 1) < HEAD_DIM
    head_lane = lax.broadcasted_iota(jnp.int32, (ROWS, 128), 1)

    def halves(v):
        zero = jnp.zeros_like(v)
        return (jnp.where(low_half, v, zero), jnp.where(low_half, zero, v))

    def both(v):
        return jnp.concatenate(halves(v), axis=0)

    def scaled(v):
        return (v.astype(F32) * SCALE).astype(BF16)

    def up_weight(g, first):
        return latw[g, :, :, :, pl.ds(first, 16), pl.ds(512, 512)].reshape(256, 512)

    def segment(m, shape, axis):
        position = lax.broadcasted_iota(jnp.int32, shape, axis).astype(F32)
        return sum((position >= ends[m, pl.ds(k, 1), pl.ds(0, 1)]).astype(F32) for k in range(4))

    def stage_masks(m):
        row = lax.broadcasted_iota(jnp.int32, (ROWS, ROWS), 0)
        col = lax.broadcasted_iota(jnp.int32, (ROWS, ROWS), 1)
        same = segment(m, (ROWS, 1), 0) == segment(m, (1, ROWS), 1)
        bias[m] = jnp.where(same & (col <= row), 0.0, -1e30)

    def attention(m, own, at, normed, query, latent, keys, values, merged, middle):
        at_norm, at_latent, at_keys, at_query, at_attend, at_middle, at_norm2 = at

        def norm_rows(k):
            rows = pl.ds(pl.multiple_of(k * 64, 64), 64)
            val = tok[m, rows].astype(F32)
            r1 = lax.rsqrt(jnp.mean(val * val, axis=1, keepdims=True) + EPSILON)
            normed[rows] = (val * r1 * gain_full[0:1, :]).astype(BF16)

        def latent_cols(n):
            w = latw[:, :, :, :, :, cols(n)].reshape(WIDTH, 256)
            latent[:, cols(n)] = nn(normed[...], w).astype(BF16)

        def key_cols(g):
            lat = latent[:, cols(g)]
            keys[:, cols(g, 512)] = nn(lat, up_weight(g, 0)).astype(BF16)
            values[:, cols(g, 512)] = nn(lat, up_weight(g, 16)).astype(BF16)

        def query_cols(n):
            w = attn[0, :, :, :, :, :, cols(n)].reshape(WIDTH, 256)
            query[:, cols(n)] = nn(normed[...], w).astype(BF16)

        def attend(j):
            pair = cols(j, 128)
            s = nt(both(scaled(query[:, pair])), keys[:, pair]) + jnp.concatenate([bias[m]] * 2, axis=0)
            peak = jnp.max(s, axis=1, keepdims=True)
            expo = jnp.exp(s - peak)
            total = jnp.sum(expo, axis=1, keepdims=True)
            res = nn((expo / total).astype(BF16), values[:, pair])
            merged[:, pair] = jnp.where(low_half, res[0:ROWS], res[ROWS : 2 * ROWS]).astype(BF16)
            if own:
                logsum = peak + jnp.log(total)
                lse[...] = jnp.where(
                    head_lane == j * 2,
                    logsum[0:ROWS],
                    jnp.where(head_lane == j * 2 + 1, logsum[ROWS : 2 * ROWS], lse[...]),
                )

        def middle_cols(n):
            w = attn[1, :, :, :, :, :, cols(n)].reshape(WIDTH, 256)
            middle[:, cols(n)] = tok[m, :, cols(n)].astype(F32) + nn(merged[...], w)

        def norm2_rows(k):
            rows = pl.ds(pl.multiple_of(k * 64, 64), 64)
            val = middle[rows]
            r2 = lax.rsqrt(jnp.mean(val * val, axis=1, keepdims=True) + EPSILON)
            normed2[m, rows] = (val * r2 * gain_full[1:2, :]).astype(BF16)

        def first():
            stage_masks(m)
            loop(4, (at_norm, norm_rows))
            loop(2, (at_latent, latent_cols), unroll=2)
            loop(GROUPS, (at_keys, key_cols), unroll=2)

        def second():
            loop(4, (at_query, query_cols), unroll=2)
            loop(8, (at_attend, attend), at=(4,), unroll=4)

        def third():
            loop(4, (at_middle, middle_cols), unroll=2)
            loop(4, (at_norm2, norm2_rows))

        return first, second, third

    def compact(k):
        pair = down_w.at[lax.div(k, 4), lax.rem(k, 4)]
        one, two = pair[0].astype(F32), pair[1].astype(F32)
        rows = pl.ds(pl.multiple_of(k * 2 * DOWN, 16), 2 * DOWN)
        for half in range(2):
            part = slice(half * DOWN, (half + 1) * DOWN)
            down_c[rows, pl.ds(half * 512, 512)] = jnp.concatenate([one[part], two[part]], axis=0).astype(BF16)

    at = (G_NORM, G_LATENT, G_KEYS, G_QUERY, G_ATTEND, G_MIDDLE, G_NORM2)
    own = attention(x, True, at, normed, query, latent, keys, values, merged, middle)
    at = (G_NORM_P, G_LATENT_P, G_KEYS_P, G_QUERY_P, G_ATTEND_P, G_MIDDLE_P, G_NORM2_P)
    across = attention(1 - x, False, at, dmid_low, dquery, dlatent, dkeys, dvalues, dmerged, dmid)
    own[0]()
    gap(G_ACROSS)
    across[0]()
    gap(G_DOWN_W)
    loop(8, (G_COMPACT, compact))
    gap(G_QUERY)
    own[1]()
    across[1]()
    gap(G_OUTPUT_W)
    own[2]()
    across[2]()
    gap(G_FFN_A)

    def ffn_w(ref, half, sl=slice(None)):
        w = ref[:, :, :, half, :, sl]
        return w.reshape(512, w.shape[-1])

    def hidden(it, gate_w, up_w, base, widths):
        m = rel(x, it)
        rows = pl.ds(pl.multiple_of(m * ROWS, ROWS), ROWS)
        for first, width in widths:
            sl, at = pl.ds(first, width), pl.ds(base + first, width)
            n2 = normed2[m]
            gate = nn(n2[:, 0:512], ffn_w(gate_w, 0, sl)) + nn(n2[:, 512:1024], ffn_w(gate_w, 1, sl))
            upper = nn(n2[:, 0:512], ffn_w(up_w, 0, sl)) + nn(n2[:, 512:1024], ffn_w(up_w, 1, sl))
            dmix = nt(dout[m], down_c[at])
            sig = jax.nn.sigmoid(gate)
            silu = gate * sig
            mixed[rows, at] = (silu * upper).astype(BF16)
            dgate[rows, at] = (dmix * upper * sig * (1.0 + gate * (1.0 - sig))).astype(BF16)
            dup[rows, at] = (dmix * silu).astype(BF16)

    def dn_half(it, gate_w, up_w, at, more):
        m = rel(x, it)
        rows = pl.ds(pl.multiple_of(m * ROWS, ROWS), ROWS)
        for half in range(2):
            part = nt(dgate[rows, at], ffn_w(gate_w, half)) + nt(dup[rows, at], ffn_w(up_w, half))
            to = (pl.ds(ROWS * it, ROWS), pl.ds(half * 512, 512))
            if more:
                part = part + tmp[to]
            if more == 2 and it:
                snd_dn2[:, pl.ds(half * 512, 512)] = part.astype(BF16)
            else:
                tmp[to] = part

    def grad_gate_up(it, gate_w, up_w, at):
        cc = jnp.where(it < 2, 1 - c, c)
        half = lax.rem(it, 2)
        sl = pl.ds(pl.multiple_of(half * 512 + cc * 256, 256), 256)
        width = gate_w.shape[-1]
        for src, dst in ((dgate, gate_w), (dup, up_w)):
            g = nn(normed2[0, :, sl].T, src[pl.ds(0, ROWS), at]) + nn(normed2[1, :, sl].T, src[pl.ds(ROWS, ROWS), at])
            dst[cc, :, :, half] = g.astype(BF16).reshape(4, 2, 32, width)

    def grad_down(it):
        cc = rel(c, it == 0)
        wide = pl.ds(pl.multiple_of(cc * 640, 128), 768)
        mt = mixed[:, wide].T
        tmp[pl.ds(ROWS, 768)] = nn(mt[:, 0:256], dout[0]) + nn(mt[:, 256:512], dout[1])

        def split(k, carry):
            rows = tmp[pl.ds(pl.multiple_of(ROWS + cc * 64 + k * DOWN, 8), DOWN)]
            down_w[cc, lax.div(k, 2), lax.rem(k, 2)] = piled(rows)
            return carry

        lax.fori_loop(0, 8, split, 0)

    def hidden_a(it):
        hidden(it, gate_a, up_a, 0, ((0, 512), (512, 256)))

    def dn_a(it):
        dn_half(it, gate_a, up_a, pl.ds(0, 768), 0)

    def gateup_a(it):
        grad_gate_up(it, gate_a, up_a, pl.ds(0, 768))

    def hidden_b(it):
        hidden(it, gate_b, up_b, 768, ((0, 512), (512, 128)))

    def dn_b(it):
        dn_half(it, gate_b, up_b, pl.ds(768, 640), 2)

    def gateup_b(it):
        grad_gate_up(it, gate_b, up_b, pl.ds(768, 640))

    def out_half(it):
        m = rel(x, it == 0)
        rows = pl.ds(pl.multiple_of(m * ROWS, ROWS), ROWS)
        part = nn(mixed[rows], down_c[...])
        if it == 0:
            snd_out[...] = part.astype(BF16)
        else:
            tmp[pl.ds(ROWS, ROWS)] = part

    loop(2, (G_HIDDEN_A, hidden_a), at=(1,))
    loop(2, (G_DN_A, dn_a), at=(1,))
    drain("ffn1")
    drain("ffn2")
    loop(4, (G_GATEUP_A, gateup_a), at=(2,))
    gap(G_FFN_B)
    hidden_b(1)
    gap((G_HIDDEN_B, 1))
    dn_b(1)
    gap((G_DN_B, 1))
    hidden_b(0)
    gap((G_HIDDEN_B, 0))
    dn_b(0)
    gap((G_DN_B, 0))
    drain("ffn0")
    loop(2, (G_DOWN, grad_down), at=(1,))
    drain("ffn3")
    drain("ffn4")
    loop(4, (G_GATEUP_B, gateup_b), at=(2,))
    loop(2, (G_OUT, out_half), at=(1,))
    gap(G_BACK)

    sum_own[...] = jnp.zeros((8, WIDTH), F32)

    def back_two(k):
        rows = pl.ds(pl.multiple_of(k * 32, 32), 32)
        mid = middle[rows]
        r2 = lax.rsqrt(jnp.mean(mid * mid, axis=1, keepdims=True) + EPSILON)
        grad = tmp[rows] + rcv_dn2[rows].astype(F32)
        sum_own[1:2] = sum_own[1:2] + jnp.sum(grad * mid * r2, axis=0, keepdims=True)
        s = grad * gain_full[1:2, :]
        res = dout[x, rows].astype(F32) + r2 * (s - mid * r2 * r2 * jnp.mean(s * mid, axis=1, keepdims=True))
        dmid[rows] = res
        dmid_low[rows] = res.astype(BF16)

    loop(8, (G_NORM2B, back_two), unroll=2)

    def dmerged_cols(k):
        w = attn[1, lax.div(k, 2), lax.rem(k, 2)].reshape(256, WIDTH)
        dmerged[:, cols(k)] = nt(dmid_low[...], w).astype(BF16)

    loop(4, (G_DMERGED, dmerged_cols), unroll=2)

    def grad_output(it):
        cc = jnp.where(it < 2, 1 - c, c)
        half = lax.rem(it, 2)
        g = nn(merged[:, cols(half * 2 + cc)].T, dmid_low[...])
        pattn[0, half, cc] = g.astype(BF16).reshape(4, 2, 32, WIDTH)

    loop(4, (G_OUTPUT, grad_output), at=(2,), unroll=2)

    drain("dn2")

    def attend_back(j):
        pair = cols(j, 128)
        k_pair, v_pair = keys[:, pair], values[:, pair]
        q, do = both(scaled(query[:, pair])), both(dmerged[:, pair])
        logsum = jnp.concatenate(
            [jnp.sum(jnp.where(head_lane == j * 2 + h, lse[...], 0.0), axis=1, keepdims=True) for h in (0, 1)], axis=0
        )
        probs = jnp.exp(nt(q, k_pair) + jnp.concatenate([bias[x]] * 2, axis=0) - logsum)
        dprobs = nt(do, v_pair)
        dvalues[:, pair] = tn(probs.astype(BF16), do).astype(BF16)
        row_sum = jnp.sum(probs * dprobs, axis=1, keepdims=True)
        dscores = (probs * (dprobs - row_sum)).astype(BF16)
        dq = nn(dscores, k_pair)
        dkeys[:, pair] = tn(dscores, q).astype(BF16)
        dquery[:, pair] = (jnp.where(low_half, dq[0:ROWS], dq[ROWS : 2 * ROWS]) * SCALE).astype(BF16)

    loop(8, (G_ATTENDB, attend_back), at=(4,), unroll=2)

    def other_first(it):
        cc = jnp.where(it < 2, 1 - c, c)
        return lax.rem(it, 2), cc

    def grad_query(it):
        half, cc = other_first(it)
        g = nn(normed[:, cols(half * 2 + cc)].T, dquery[...])
        pattn[1, half, cc] = g.astype(BF16).reshape(4, 2, 32, WIDTH)

    loop(4, (G_PROJQ, grad_query), at=(2,), unroll=2)

    def latent_back(g):
        dk, dv = dkeys[:, cols(g, 512)], dvalues[:, cols(g, 512)]
        dlatent[:, cols(g)] = (nt(dk, up_weight(g, 0)) + nt(dv, up_weight(g, 16))).astype(BF16)
        lat = latent[:, cols(g)].T
        pattn[2, g, :, :, :, pl.ds(0, 16), pl.ds(512, 512)] = nn(lat, dk).astype(BF16).reshape(2, 4, 2, 16, 512)
        pattn[2, g, :, :, :, pl.ds(16, 16), pl.ds(512, 512)] = nn(lat, dv).astype(BF16).reshape(2, 4, 2, 16, 512)

    loop(GROUPS, (G_LATENTB, latent_back))

    def grad_latent(it):
        half, cc = other_first(it)
        g = nn(normed[:, cols(half * 2 + cc)].T, dlatent[...])
        pattn[2, half, cc, :, :, :, pl.ds(0, 512)] = g.astype(BF16).reshape(4, 2, 32, 512)

    loop(4, (G_PROJL, grad_latent), at=(2,), unroll=2)

    def dnormed_cols(k):
        xx, cc = lax.div(k, 2), lax.rem(k, 2)
        part = nt(dquery[...], attn[0, xx, cc].reshape(256, WIDTH))
        part = part + nt(dlatent[...], latw[xx, cc, :, :, :, pl.ds(0, 512)].reshape(256, 512))
        tmp[pl.ds(0, ROWS), cols(k)] = part

    loop(4, (G_DNORMED, dnormed_cols), unroll=2)

    def back_one(k):
        rows = pl.ds(pl.multiple_of(k * 32, 32), 32)
        val = tok[x, rows].astype(F32)
        r1 = lax.rsqrt(jnp.mean(val * val, axis=1, keepdims=True) + EPSILON)
        grad = tmp[rows]
        sum_own[0:1] = sum_own[0:1] + jnp.sum(grad * val * r1, axis=0, keepdims=True)
        s = grad * gain_full[0:1, :]
        dmid[rows] = dmid[rows] + r1 * (s - val * r1 * r1 * jnp.mean(s * val, axis=1, keepdims=True))

    loop(8, (G_NORM1B, back_one), unroll=2)
    to_gtok = local(dmid, gtok_hbm, 0)
    to_gtok.start()
    gap(G_RESULT)

    def out_rows(k):
        rows = pl.ds(pl.multiple_of(k * 32, 32), 32)
        part = tmp[pl.ds(pl.multiple_of(ROWS + k * 32, 32), 32)]
        tok[x, rows] = (middle[rows] + (part + rcv_out[rows].astype(F32))).astype(BF16)

    drain("tok")
    loop(8, (G_RESULT, out_rows))
    to_out = local(tok.at[x], out_hbm, 1)
    to_out.start()
    gap(G_TAIL)
    to_gain = local(sum_own.at[:, pl.ds(pl.multiple_of((dp * 2 + lax.div(fs, 4)) * 128, 128), 128)], gain_hbm, 2)
    to_gain.start()
    for group in list(sent):
        drain(group)
    to_gtok.wait()
    to_out.wait()
    to_gain.wait()
    wait_out()


def finish_kernel(*refs):
    given, outs, bufs, casts = refs[:7], refs[7:19], refs[19:26], refs[26:36]
    in_sem, out_sem = refs[36:]
    takes = [pltpu.make_async_copy(src, dst, in_sem.at[k]) for k, (src, dst) in enumerate(zip(given, bufs))]
    gives = [pltpu.make_async_copy(src, dst, out_sem.at[k]) for k, (src, dst) in enumerate(zip([*bufs[:2], *casts], outs))]
    for k in (1, 0, 4, 5, 6, 2, 3):
        takes[k].start()
    for k in (1, 0):
        takes[k].wait()
        gives[k].start()
    _, _, at_ref, gain_ref, gg_ref, gu_ref, gd_ref = bufs
    gq_o, gl_o, gk_o, gv_o, go_o, ga_o, gf_o, gg_o, gu_o, gd_o = casts
    for k, src, dst in ((4, gg_ref, gg_o), (5, gu_ref, gu_o)):
        takes[k].wait()
        dst[:, 0:HALF] = src[0].astype(F32)
        dst[:, HALF : 2 * HALF] = src[1].astype(F32)
        gives[k + 5].start()
    takes[6].wait()
    gd = gd_ref[...].astype(F32)
    gd_o[:, 0:512] = gd[0:DOWN]
    gd_o[:, 512:WIDTH] = gd[DOWN : 2 * DOWN]
    gives[11].start()
    takes[2].wait()
    go_o[...] = at_ref[0].astype(F32)
    gq_o[...] = at_ref[1].astype(F32)
    gl_o[...] = at_ref[2, :, 0:512].astype(F32)
    gk_o[...] = at_ref[2, 0:16, 512:1024].astype(F32)
    gv_o[...] = at_ref[2, 16:32, 512:1024].astype(F32)
    takes[3].wait()
    place = lax.rem(lax.axis_index("fsdp"), 4)
    picked = sum(jnp.where(place == k, gain_ref[:, 32 * k : 32 * k + 32], 0.0) for k in range(4))
    ga_o[...] = picked[0:1]
    gf_o[...] = picked[1:2]
    for k in range(2, 9):
        gives[k].start()
    for give in gives:
        give.wait()


def kernel_on_device(
    tokens, seq_lengths, cotangent, w_query, w_latent, w_keyup, w_valup, w_output, norm_attn, norm_ffn,
    w_gate, w_up, w_down,
):
    hbm, vmem = pl.BlockSpec(memory_space=pl.ANY), pl.BlockSpec(memory_space=pltpu.VMEM)
    smem = pl.BlockSpec(memory_space=pltpu.SMEM)
    shape = jax.ShapeDtypeStruct
    outs = [
        shape((ROWS, WIDTH), BF16), shape((ROWS, WIDTH), F32), shape((3, 32, WIDTH), BF16), shape((8, 128), F32),
        shape((2, 32, HALF), BF16), shape((2, 32, HALF), BF16), shape((2 * DOWN, 512), BF16),
    ]
    V = pltpu.VMEM
    units = [(2 * DOWN, 512), *[(2, 32, width) for width in PARTS for _ in range(2)]]
    act = V((ROWS, WIDTH), BF16)
    scratch = [
        V((2, 2, 2, 4, 2, 32, WIDTH), BF16), V((2, 2, 4, 2, 32, WIDTH + 128), BF16),
        *[V((2, 4, 2, *unit), BF16) for unit in units[1:]],
        V((2, 4, 2, 2 * DOWN, 512), BF16), V((HALF, WIDTH), BF16), V((16, WIDTH), F32),
        V((2, ROWS, WIDTH), BF16), V((2, 8, 128), F32), V((2, ROWS, ROWS), F32), act, act, V((ROWS, 512), BF16), act, act, act, V((ROWS, 128), F32),
        V((ROWS, WIDTH), F32), V((2, ROWS, WIDTH), BF16), V((2, ROWS, WIDTH), BF16),
        V((512, HALF), BF16), V((512, HALF), BF16), V((512, HALF), BF16), V((ROWS + 768, WIDTH), F32),
        act, act, act,
        V((ROWS, WIDTH), F32), act, act, act, act, act, V((ROWS, 512), BF16),
        V((3, 2, 2, 4, 2, 32, WIDTH), BF16),
        *[V((2, 4, *unit), BF16) for unit in units],
        *[V((4, *unit), BF16) for unit in units],
        *[V((3, *unit), BF16) for unit in units],
        *[V(unit[1:], BF16) for unit in units[1:]],
        V((3, 2, 4, 2, 32, WIDTH), BF16), V((3, 4, 2, 32, WIDTH), BF16),
        V((3, 3, 2, 32, WIDTH), BF16), V((3, 32, WIDTH), BF16), V((8, WIDTH), F32), V((5, 8, WIDTH), F32),
        pltpu.SemaphoreType.DMA((SLOTS.count,)), pltpu.SemaphoreType.DMA((SLOTS.count,)), pltpu.SemaphoreType.DMA((PUT + 8 + 2 * FFN,)),
    ]
    res = pl.pallas_call(
        layer_kernel,
        out_shape=outs,
        in_specs=[hbm, smem, hbm, hbm, hbm, hbm, hbm, hbm, vmem, vmem, hbm, hbm, vmem],
        out_specs=[hbm] * len(outs),
        scratch_shapes=scratch,
        compiler_params=pltpu.CompilerParams(
            collective_id=0, has_side_effects=True, vmem_limit_bytes=63 * 2**20
        ),
    )(
        tokens, seq_lengths, cotangent, w_query, w_latent, w_keyup, w_valup, w_output, norm_attn, norm_ffn,
        w_gate, w_up, w_down,
    )
    final = [
        shape((ROWS, WIDTH), BF16), shape((ROWS, WIDTH), F32), shape((32, WIDTH), F32), shape((32, 512), F32),
        shape((16, 512), F32), shape((16, 512), F32), shape((32, WIDTH), F32), shape((1, 32), F32), shape((1, 32), F32),
        shape((32, 2 * HALF), F32), shape((32, 2 * HALF), F32), shape((DOWN, WIDTH), F32),
    ]
    out = pl.pallas_call(
        finish_kernel,
        out_shape=final,
        in_specs=[hbm] * 7,
        out_specs=[hbm] * 12,
        scratch_shapes=[
            *[V(one.shape, one.dtype) for one in [*outs, *final[2:]]],
            pltpu.SemaphoreType.DMA((7,)), pltpu.SemaphoreType.DMA((12,)),
        ],
    )(*res)
    return tuple(out[:7]) + (out[7].reshape(32), out[8].reshape(32)) + tuple(out[9:])


def solution(mesh):
    fits = dict(mesh.shape) == {"dp": 4, "fsdp": 8}
    return jax.shard_map(
        kernel_on_device if fits else on_device,
        mesh=mesh,
        in_specs=(
            P(("dp", "fsdp"), None),
            P(("dp", "fsdp")),
            P(("dp", "fsdp"), None),
            P(("dp", "fsdp"), None),
            P(("dp", "fsdp"), None),
            P(("dp", "fsdp"), None),
            P(("dp", "fsdp"), None),
            P(("dp", "fsdp"), None),
            P(("dp", "fsdp")),
            P(("dp", "fsdp")),
            P(("dp", "fsdp"), None),
            P(("dp", "fsdp"), None),
            P(("dp", "fsdp"), None),
        ),
        out_specs=(
            P(("dp", "fsdp"), None),
            P(("dp", "fsdp"), None),
            P(("dp", "fsdp"), None),
            P(("dp", "fsdp"), None),
            P(("dp", "fsdp"), None),
            P(("dp", "fsdp"), None),
            P(("dp", "fsdp"), None),
            P(("dp", "fsdp")),
            P(("dp", "fsdp")),
            P(("dp", "fsdp"), None),
            P(("dp", "fsdp"), None),
            P(("dp", "fsdp"), None),
        ),
        check_vma=False,
    )
```

```python
import math

import jax
import jax.numpy as jnp
from jax import lax
from jax.experimental import pallas as pl
from jax.experimental.pallas import tpu as pltpu
from jax.sharding import PartitionSpec as P

HEADS = 16
HEAD_DIM = 64
GROUPS = 2
LATENT = 256


EPSILON = 1e-06


def matmul(left, right):
    return jnp.dot(left, right, preferred_element_type=jnp.float32)


def matmul_left(left, right):
    return lax.dot_general(
        left, right, (((0,), (0,)), ((), ())), preferred_element_type=jnp.float32
    )


def matmul_right(left, right):
    return lax.dot_general(
        left, right, (((1,), (1,)), ((), ())), preferred_element_type=jnp.float32
    )


def segment_mask(lengths, rows):
    position = jnp.arange(rows, dtype=jnp.int32)
    ends = jnp.cumsum(lengths)
    segment = jnp.sum((position[None, :] >= ends[:, None]).astype(jnp.int32), axis=0)
    allowed = (segment[:, None] == segment[None, :]) & (position[None, :] <= position[:, None])
    valid = (position < ends[-1]).astype(jnp.float32)
    return (allowed, valid)


def head_forward(allowed, scale):

    def one_head(operands):
        query, key_rows, value_rows = operands
        scores = jnp.where(allowed, matmul_right(query, key_rows) * scale, -1e30)
        peak = jnp.max(scores, axis=1, keepdims=True)
        expo = jnp.exp(scores - peak)
        total = jnp.sum(expo, axis=1, keepdims=True)
        weights = (expo / total).astype(jnp.bfloat16)
        result = matmul(weights, value_rows).astype(jnp.bfloat16)
        return (result, peak[:, 0] + jnp.log(total[:, 0]))

    return one_head


def head_backward(allowed, scale):

    def one_head(operands):
        query, key_rows, value_rows, grad_out, logsum = operands
        scores = jnp.where(allowed, matmul_right(query, key_rows) * scale, -1e30)
        probs = jnp.exp(scores - logsum[:, None])
        grad_value = matmul_left(probs.astype(jnp.bfloat16), grad_out)
        grad_probs = matmul_right(grad_out, value_rows)
        inner = jnp.sum(probs * grad_probs, axis=1, keepdims=True)
        grad_scores = (probs * (grad_probs - inner)).astype(jnp.bfloat16)
        grad_query = matmul(grad_scores, key_rows) * scale
        grad_key = matmul_left(grad_scores, query) * scale
        return (grad_query, grad_key, grad_value)

    return one_head


def norm_back(grad_normed, inputs, rstd, gain):
    scaled = grad_normed * gain
    grad_in = rstd * (
        scaled - inputs * rstd * rstd * jnp.mean(scaled * inputs, axis=1, keepdims=True)
    )
    grad_gain = jnp.sum(grad_normed * inputs * rstd, axis=0)
    return (grad_in, grad_gain)


def column_term(left, right):
    return matmul_left(left, right).astype(jnp.bfloat16)


def forward(tokens, allowed, attn_w, ffn_w):
    w_query, w_latent, w_keyup, w_valup, w_output, gain_one = attn_w
    gain_two, w_gate, w_up, w_down = ffn_w
    rows = tokens.shape[0]
    inputs = tokens.astype(jnp.float32)
    rstd_one = lax.rsqrt(jnp.mean(inputs * inputs, axis=1, keepdims=True) + EPSILON)
    normed = (inputs * rstd_one * gain_one.astype(jnp.float32)).astype(jnp.bfloat16)
    query = matmul(normed, w_query).astype(jnp.bfloat16)
    latent = matmul(normed, w_latent).astype(jnp.bfloat16)
    lat3 = latent.reshape(rows, GROUPS, LATENT)
    keys = jnp.einsum(
        "tgl,glf->tgf",
        lat3,
        w_keyup.reshape(GROUPS, LATENT, -1),
        preferred_element_type=jnp.float32,
    ).astype(jnp.bfloat16)
    values = jnp.einsum(
        "tgl,glf->tgf",
        lat3,
        w_valup.reshape(GROUPS, LATENT, -1),
        preferred_element_type=jnp.float32,
    ).astype(jnp.bfloat16)
    heads_query = query.reshape(rows, HEADS, HEAD_DIM).transpose(1, 0, 2)
    heads_key = keys.reshape(rows, HEADS, HEAD_DIM).transpose(1, 0, 2)
    heads_value = values.reshape(rows, HEADS, HEAD_DIM).transpose(1, 0, 2)
    attended, logsum = lax.map(
        head_forward(allowed, HEAD_DIM ** (-0.5)), (heads_query, heads_key, heads_value)
    )
    merged = attended.transpose(1, 0, 2).reshape(rows, HEADS * HEAD_DIM)
    middle = inputs + matmul(merged, w_output)
    rstd_two = lax.rsqrt(jnp.mean(middle * middle, axis=1, keepdims=True) + EPSILON)
    normed_two = (middle * rstd_two * gain_two.astype(jnp.float32)).astype(jnp.bfloat16)
    gate = matmul(normed_two, w_gate)
    upper = matmul(normed_two, w_up)
    mixed = (jax.nn.silu(gate) * upper).astype(jnp.bfloat16)
    result = middle + matmul(mixed, w_down)
    return (
        result,
        inputs,
        rstd_one,
        normed,
        lat3,
        heads_query,
        heads_key,
        heads_value,
        logsum,
        merged,
        middle,
        rstd_two,
        normed_two,
        gate,
        upper,
        mixed,
    )


def on_device(
    tokens,
    seq_lengths,
    cotangent,
    w_query,
    w_latent,
    w_keyup,
    w_valup,
    w_output,
    norm_attn,
    norm_ffn,
    w_gate,
    w_up,
    w_down,
):
    rows = tokens.shape[0]
    allowed, valid = segment_mask(seq_lengths, rows)
    attn_w = (
        lax.all_gather(w_query, ("dp", "fsdp"), axis=0, tiled=True),
        lax.all_gather(w_latent, ("dp", "fsdp"), axis=0, tiled=True),
        lax.all_gather(w_keyup, ("dp", "fsdp"), axis=0, tiled=True),
        lax.all_gather(w_valup, ("dp", "fsdp"), axis=0, tiled=True),
        lax.all_gather(w_output, ("dp", "fsdp"), axis=0, tiled=True),
        lax.all_gather(norm_attn, ("dp", "fsdp"), axis=0, tiled=True),
    )
    ffn_w = (
        lax.all_gather(norm_ffn, ("dp", "fsdp"), axis=0, tiled=True),
        lax.all_gather(w_gate, ("dp", "fsdp"), axis=0, tiled=True),
        lax.all_gather(w_up, ("dp", "fsdp"), axis=0, tiled=True),
        lax.all_gather(w_down, ("dp", "fsdp"), axis=0, tiled=True),
    )
    saved = forward(tokens, allowed, attn_w, ffn_w)
    block_out = saved[0].astype(jnp.bfloat16)
    (
        result,
        inputs,
        rstd_one,
        normed,
        lat3,
        heads_query,
        heads_key,
        heads_value,
        logsum,
        merged,
        middle,
        rstd_two,
        normed_two,
        gate,
        upper,
        mixed,
    ) = saved
    full_query, full_latent, full_keyup, full_valup, full_output, gain_one = attn_w
    gain_two, full_gate, full_up, full_down = ffn_w
    ff_width = full_gate.shape[1]
    grad_out = cotangent.astype(jnp.float32) * valid[:, None]
    grad_low = grad_out.astype(jnp.bfloat16)
    grad_mixed = matmul_right(grad_low, full_down)
    sigmoid_gate = jax.nn.sigmoid(gate)
    grad_gate_low = (
        grad_mixed * upper * sigmoid_gate * (1.0 + gate * (1.0 - sigmoid_gate))
    ).astype(jnp.bfloat16)
    grad_upper_low = (grad_mixed * jax.nn.silu(gate)).astype(jnp.bfloat16)
    grad_normed_two = matmul_right(grad_gate_low, full_gate) + matmul_right(grad_upper_low, full_up)
    grad_mid_norm, grad_gain_two = norm_back(
        grad_normed_two, middle, rstd_two, gain_two.astype(jnp.float32)
    )
    grad_middle = grad_out + grad_mid_norm
    down_own = lax.psum_scatter(
        column_term(mixed, grad_low), ("dp", "fsdp"), scatter_dimension=0, tiled=True
    )
    packed_ffn = jnp.concatenate([grad_gate_low, grad_upper_low], axis=1)
    ffn_own = lax.psum_scatter(
        column_term(normed_two, packed_ffn), ("dp", "fsdp"), scatter_dimension=0, tiled=True
    )
    grad_branch = grad_middle.astype(jnp.bfloat16)
    grad_merged = matmul_right(grad_branch, full_output).astype(jnp.bfloat16)
    output_own = lax.psum_scatter(
        column_term(merged, grad_branch), ("dp", "fsdp"), scatter_dimension=0, tiled=True
    )
    heads_grad = grad_merged.reshape(rows, HEADS, HEAD_DIM).transpose(1, 0, 2)
    grad_hq, grad_hk, grad_hv = lax.map(
        head_backward(allowed, HEAD_DIM ** (-0.5)),
        (heads_query, heads_key, heads_value, heads_grad, logsum),
    )
    grad_query_low = grad_hq.transpose(1, 0, 2).reshape(rows, HEADS * HEAD_DIM).astype(jnp.bfloat16)
    grad_keys_low = grad_hk.transpose(1, 0, 2).reshape(rows, GROUPS, -1).astype(jnp.bfloat16)
    grad_values_low = grad_hv.transpose(1, 0, 2).reshape(rows, GROUPS, -1).astype(jnp.bfloat16)
    head_cols = grad_keys_low.shape[2]
    keyup3 = full_keyup.reshape(GROUPS, LATENT, -1)
    valup3 = full_valup.reshape(GROUPS, LATENT, -1)
    grad_lat = jnp.einsum("tgf,glf->tgl", grad_keys_low, keyup3, preferred_element_type=jnp.float32)
    grad_lat = grad_lat + jnp.einsum(
        "tgf,glf->tgl", grad_values_low, valup3, preferred_element_type=jnp.float32
    )
    grad_latent_low = grad_lat.reshape(rows, GROUPS * LATENT).astype(jnp.bfloat16)
    latent_flat = lat3.reshape(rows, GROUPS * LATENT)
    paired = jnp.concatenate([grad_keys_low, grad_values_low], axis=2).reshape(
        rows, GROUPS * 2 * head_cols
    )
    count = w_keyup.shape[0] * lax.axis_size(("dp", "fsdp"))
    product = matmul_left(latent_flat, paired).reshape(count, GROUPS, 2 * head_cols)
    owner = jnp.arange(count, dtype=jnp.int32) // LATENT
    picker = (owner[:, None] == jnp.arange(GROUPS, dtype=jnp.int32)[None, :]).astype(jnp.float32)
    latent_own = lax.psum_scatter(
        jnp.sum(product * picker[:, :, None], axis=1).astype(jnp.bfloat16),
        ("dp", "fsdp"),
        scatter_dimension=0,
        tiled=True,
    )
    grad_normed = matmul_right(grad_query_low, full_query) + matmul_right(
        grad_latent_low, full_latent
    )
    packed_attn = jnp.concatenate([grad_query_low, grad_latent_low], axis=1)
    attn_own = lax.psum_scatter(
        column_term(normed, packed_attn), ("dp", "fsdp"), scatter_dimension=0, tiled=True
    )
    grad_in_norm, grad_gain_one = norm_back(
        grad_normed, inputs, rstd_one, gain_one.astype(jnp.float32)
    )
    grad_tokens = grad_middle + grad_in_norm
    gains_own = (
        lax.psum_scatter(grad_gain_one, ("dp", "fsdp"), scatter_dimension=0, tiled=True),
        lax.psum_scatter(grad_gain_two, ("dp", "fsdp"), scatter_dimension=0, tiled=True),
    )
    query_cols = HEADS * HEAD_DIM
    return (
        block_out,
        grad_tokens,
        attn_own[:, :query_cols].astype(jnp.float32),
        attn_own[:, query_cols:].astype(jnp.float32),
        latent_own[:, :head_cols].astype(jnp.float32),
        latent_own[:, head_cols:].astype(jnp.float32),
        output_own.astype(jnp.float32),
        gains_own[0],
        gains_own[1],
        ffn_own[:, :ff_width].astype(jnp.float32),
        ffn_own[:, ff_width:].astype(jnp.float32),
        down_own.astype(jnp.float32),
    )


MESH = pl.DeviceIdType.MESH
F32 = jnp.float32
BF16 = jnp.bfloat16
SCALE = HEAD_DIM ** (-0.5)
ROWS = 256
WIDTH = 1024
HALF = 1408
PARTS = (768, 640)
FFN = 1 + 2 * len(PARTS)
PUT = 3
DOWN = 88


ROUTE = ("y21xs", "y21xs", "21xys", "21yxs")
SUM_X_FIRST = (True, False, True, True)


class Slots:
    def __init__(self):
        self.count = 0

    def take(self, number):
        first = self.count
        self.count += number
        return first


SLOTS = Slots()
S_A = [SLOTS.take(16) for _ in range(4)]
S_HALF = SLOTS.take(FFN)
S_F = [SLOTS.take(8) for _ in range(FFN)]
S_COT, S_TOK, S_DN2, S_OUT, S_END = (SLOTS.take(1) for _ in range(5))
S_R = [SLOTS.take(10) for _ in range(FFN + 4)]
S_SUM = SLOTS.take(5)


def nn(left, right):
    return jnp.dot(left, right, preferred_element_type=F32)


def nt(left, right):
    return lax.dot_general(left, right, (((1,), (1,)), ((), ())), preferred_element_type=F32)


def tn(left, right):
    return lax.dot_general(left, right, (((0,), (0,)), ((), ())), preferred_element_type=F32)


(
    AA, AG, AT, H_S, H_R, FA, FG, FT, COT_S, COT_R, TOK_S, TOK_R, END_S, END_R, DN2_S, DN2_R, OUT_S,
    OUT_R, R_GO, R_S, R_B, R_A, R_1, R_2, R_L, R_E, SUM_S, SUM_R,
) = range(28)
(
    G_START, G_WEIGHTS, G_ACROSS, G_DOWN_W, G_QUERY, G_OUTPUT_W, G_FFN_A, G_FFN_B, G_BACK, G_RESULT,
    G_TAIL, G_MASK, G_NORM, G_LATENT, G_KEYS, G_NORM_P, G_LATENT_P, G_KEYS_P, G_COMPACT, G_ATTEND,
    G_QUERY_P, G_ATTEND_P, G_MIDDLE, G_NORM2, G_MIDDLE_P, G_NORM2_P, G_HIDDEN_A, G_DN_A, G_GATEUP_A,
    G_DN_B, G_HIDDEN_B, G_DOWN, G_GATEUP_B, G_OUT, G_OUTPUT, G_ATTENDB, G_PROJQ, G_PROJL, G_DNORMED,
    G_NORM1B, G_GAIN, G_NORM2B, G_DMERGED, G_LATENTB,
) = range(44)
PLAN = {
    G_START: (
        (H_S, 2), (AA, 2, 0), (AG, 2, 0, 1), (H_S, 1), (H_S, 4), (H_S, 3), (FA, 0, 0), (AA, 0, 0),
    ),
    (G_MASK, 3): (
        (TOK_S, 2), (AA, 1, 0), (FG, 0, 0, 0), (FG, 0, 0, 1),
    ),
    G_WEIGHTS: (
        (AG, 1, 0, 0), (AG, 0, 0, 1), (H_R, 4), (AG, 0, 0, 2), (TOK_S, 1), (TOK_S, 0), (AA, 3, 0),
        (FA, 4, 0), (AG, 0, 0, 0), (AA, 0, 1), (AG, 2, 0, 0), (AA, 1, 1), (AG, 3, 0, 1), (H_R, 2),
        (H_R, 1), (TOK_S, 3), (FG, 0, 0, 2), (AG, 0, 1, 1), (FA, 0, 1), (FG, 0, 1, 2), (AG, 0, 1, 2),
        (FA, 0, 2), (H_R, 3), (AG, 3, 0, 0), (AG, 0, 1, 3), (AA, 2, 1), (FA, 1, 0), (AA, 0, 2),
        (AG, 0, 2, 2), (AG, 0, 0, 3), (AG, 2, 1, 2), (AG, 2, 1, 1), (FG, 1, 0, 2), (AA, 0, 3),
        (FA, 2, 0), (AA, 3, 2), (AG, 1, 0, 1), (AG, 1, 0, 3), (FG, 2, 0, 2), (AG, 2, 1, 3),
        (AG, 0, 2, 3), (AG, 3, 0, 2), (AA, 0, 4), (AG, 1, 0, 2), (AA, 2, 5), (FG, 4, 0, 2),
        (AG, 0, 3, 2), (AA, 2, 2), (FA, 3, 0), (AG, 0, 3, 3), (AG, 1, 1, 1), (FA, 2, 4),
        (FG, 0, 1, 1), (AG, 2, 5, 3), (AA, 1, 8), (FG, 1, 0, 0), (AA, 3, 1), (AA, 0, 8), (AA, 2, 3),
        (AG, 2, 0, 2), (AG, 0, 4, 3), (FA, 0, 5), (AG, 1, 1, 2), (FG, 0, 2, 2), (AA, 0, 6),
        (AA, 0, 5), (AG, 3, 1, 2), (AG, 0, 6, 3), (AA, 0, 7), (FA, 0, 4), (AA, 0, 11), (AG, 0, 5, 3),
        (AG, 2, 3, 2), (AA, 0, 9), (AA, 3, 4), (AA, 1, 2), (AG, 3, 2, 2), (FA, 1, 4), (AA, 1, 3),
        (AG, 3, 1, 1), (AG, 0, 7, 3), (AA, 0, 13), (AG, 2, 2, 3), (AG, 1, 1, 3), (AA, 1, 4),
        (AA, 2, 9), (AA, 2, 4), (AG, 1, 2, 3), (AG, 1, 2, 2), (AG, 2, 2, 2), (AA, 2, 7), (AA, 2, 13),
        (END_S,), (AA, 0, 10), (FA, 0, 3), (FG, 0, 3, 2), (AA, 0, 12), (AG, 1, 3, 2), (FA, 4, 4),
        (AA, 0, 15), (FG, 2, 0, 0), (AA, 0, 14), (AG, 1, 3, 3), (TOK_R,), (AT, 0), (FG, 3, 0, 2),
        (AA, 2, 10), (AA, 1, 5), (FA, 1, 1), (AG, 1, 4, 3), (FG, 1, 0, 1),
    ),
    (G_NORM, 3): (
        (AA, 3, 3), (AA, 3, 5), (AG, 2, 3, 3), (AG, 2, 4, 3),
    ),
    (G_LATENT, 1): (
        (FG, 4, 0, 0), (AA, 1, 6), (AG, 1, 5, 3), (AA, 3, 6),
    ),
    (G_KEYS, 1): (
        (AG, 3, 3, 2), (FA, 0, 6), (AG, 2, 7, 3),
    ),
    G_ACROSS: (
        (AA, 2, 6), (FA, 0, 7), (AA, 1, 7), (AG, 1, 6, 3), (FG, 2, 0, 1), (FG, 1, 1, 1),
        (FG, 1, 1, 2), (END_R,), (AA, 1, 9),
    ),
    (G_NORM_P, 3): (
        (AG, 1, 7, 3), (FT, 0),
    ),
    (G_LATENT_P, 1): (
        (AA, 1, 12), (AA, 3, 7), (AG, 2, 0, 3), (AG, 3, 0, 3),
    ),
    (G_KEYS_P, 1): (
        (AG, 3, 5, 3), (FA, 2, 1), (AA, 1, 14),
    ),
    G_DOWN_W: (
        (AA, 1, 11), (AG, 3, 4, 3), (AG, 3, 3, 3), (FG, 3, 0, 0), (FG, 2, 1, 2), (FG, 2, 1, 1),
        (AA, 1, 13), (AG, 2, 6, 3),
    ),
    (G_COMPACT, 7): (
        (FG, 3, 0, 1), (AG, 3, 7, 3),
    ),
    G_QUERY: (
        (AG, 3, 6, 3), (AA, 1, 15), (AA, 1, 10), (FA, 1, 5), (AG, 3, 2, 3), (FA, 1, 2),
        (FG, 1, 2, 2), (AG, 3, 1, 3), (AA, 2, 8), (COT_S, 2), (COT_S, 1), (AT, 1), (FA, 4, 1),
        (AA, 2, 15), (AA, 2, 11),
    ),
    (G_QUERY, 3): (
        (AA, 2, 12),
    ),
    (G_ATTEND, 3): (
        (AA, 2, 14), (FG, 4, 1, 2), (AA, 3, 8), (AA, 3, 13),
    ),
    (G_ATTEND, 7): (
        (FA, 1, 3), (FG, 1, 3, 2), (FG, 4, 0, 1), (AA, 3, 12), (AA, 3, 10), (FA, 2, 2),
    ),
    (G_QUERY_P, 3): (
        (FA, 1, 6), (AT, 2), (FG, 4, 1, 1), (AA, 3, 14), (FA, 2, 5), (AA, 3, 15), (COT_S, 3),
        (AA, 3, 11), (FG, 2, 2, 2), (FA, 3, 1), (AA, 3, 9), (FG, 3, 1, 1),
    ),
    (G_ATTEND_P, 3): (
        (FA, 2, 3), (AT, 3), (FG, 2, 3, 2),
    ),
    G_OUTPUT_W: (
        (COT_S, 0), (FA, 1, 7),
    ),
    (G_MIDDLE, 3): (
        (FA, 3, 2), (FG, 3, 2, 2),
    ),
    (G_NORM2, 3): (
        (FG, 3, 1, 2), (FA, 4, 5), (FA, 2, 6), (FA, 4, 2),
    ),
    (G_MIDDLE_P, 3): (
        (FA, 2, 7), (FG, 4, 2, 2),
    ),
    (G_NORM2_P, 3): (
        (FA, 3, 4), (FT, 1),
    ),
    G_FFN_A: (
        (FT, 2),
    ),
    (G_HIDDEN_A, 0): (
        (FA, 3, 3), (FA, 4, 3), (FG, 3, 3, 2), (COT_R,),
    ),
    (G_DN_A, 0): (
        (FG, 4, 3, 2),
    ),
    (G_GATEUP_A, 1): (
        (R_GO, 1), (FA, 3, 5),
    ),
    (G_GATEUP_A, 3): (
        (FA, 4, 6), (FA, 3, 7), (FA, 3, 6), (R_S, 1, 1), (R_B, 1, 3),
    ),
    G_FFN_B: (
        (R_B, 1, 1), (FA, 4, 7), (R_B, 1, 2), (R_S, 1, 0), (R_GO, 2), (FT, 3), (FT, 4),
    ),
    (G_DN_B, 1): (
        (DN2_S,), (R_S, 2, 1),
    ),
    (G_HIDDEN_B, 0): (
        (R_B, 2, 3),
    ),
    (G_DN_B, 0): (
        (R_B, 2, 1), (R_A, 1, 3),
    ),
    (G_DOWN, 0): (
        (R_GO, 0), (R_A, 1, 1), (R_S, 2, 0),
    ),
    (G_GATEUP_B, 1): (
        (R_S, 0, 1), (R_GO, 3), (R_B, 0, 3), (R_A, 2, 3), (R_A, 1, 2), (R_GO, 4), (R_S, 0, 0),
    ),
    (G_GATEUP_B, 3): (
        (R_S, 3, 1), (R_A, 2, 1),
    ),
    (G_OUT, 0): (
        (R_B, 2, 2), (OUT_S, 1), (OUT_S, 2), (R_S, 4, 1), (R_1, 1, 1), (R_B, 3, 1), (R_S, 3, 0),
    ),
    (G_OUT, 1): (
        (R_B, 3, 3), (R_B, 0, 2), (OUT_S, 0), (R_B, 4, 3), (R_A, 0, 3), (R_B, 1, 0),
    ),
    G_BACK: (
        (DN2_R,),
    ),
    (G_OUTPUT, 1): (
        (R_A, 2, 2), (R_1, 2, 1), (OUT_S, 3),
    ),
    (G_OUTPUT, 3): (
        (R_GO, 5),
    ),
    (G_ATTENDB, 3): (
        (R_A, 3, 1), (R_A, 3, 3),
    ),
    (G_PROJQ, 1): (
        (R_S, 5, 1), (R_A, 0, 2),
    ),
    (G_PROJQ, 3): (
        (R_B, 5, 1), (R_1, 0, 1), (R_S, 4, 0), (R_A, 4, 3), (R_B, 4, 1),
    ),
    (G_PROJL, 1): (
        (R_B, 5, 3), (R_B, 4, 2), (R_S, 5, 0), (R_GO, 6), (R_B, 3, 2),
    ),
    (G_PROJL, 3): (
        (R_GO, 7), (R_B, 2, 0), (OUT_R,), (R_A, 5, 1), (R_B, 5, 0),
    ),
    (G_DNORMED, 3): (
        (R_S, 6, 1),
    ),
    (G_NORM1B, 7): (
        (R_B, 4, 0), (R_B, 3, 0), (R_A, 4, 2), (R_A, 5, 3), (R_GO, 8), (R_S, 7, 1), (R_S, 8, 0),
        (R_B, 6, 3), (R_A, 1, 0),
    ),
    G_RESULT: (
        (R_1, 4, 1), (R_1, 1, 0), (R_A, 4, 1), (R_B, 5, 2), (R_B, 6, 2), (R_B, 7, 1), (R_A, 2, 0),
    ),
    (G_RESULT, 7): (
        (R_A, 3, 2), (SUM_S, 0), (R_B, 0, 0), (SUM_R, 0), (R_1, 3, 1), (R_A, 3, 0), (R_A, 4, 0),
        (R_S, 8, 1), (R_S, 7, 0), (R_A, 5, 0), (R_B, 8, 3), (R_A, 5, 2), (SUM_S, 1), (R_B, 7, 2),
        (R_B, 8, 0), (R_1, 3, 0), (R_S, 6, 0), (R_2, 1), (R_A, 6, 3), (R_1, 2, 0), (R_B, 6, 1),
        (R_B, 8, 1), (R_B, 7, 0), (R_1, 5, 1), (R_A, 8, 3), (R_1, 5, 0), (R_A, 8, 0), (R_A, 6, 2),
        (R_B, 0, 1), (R_B, 6, 0), (R_B, 8, 2), (R_B, 7, 3), (R_A, 8, 1), (R_2, 2),
    ),
    G_TAIL: (
        (R_1, 6, 1), (R_A, 7, 1), (R_2, 3), (R_A, 8, 2), (R_1, 8, 0), (SUM_R, 1), (R_1, 4, 0),
        (R_A, 7, 3), (SUM_S, 2), (R_1, 8, 1), (R_A, 6, 1), (R_L, 3), (R_A, 6, 0), (R_A, 7, 2),
        (R_2, 4), (SUM_R, 2), (SUM_S, 3), (R_L, 1), (R_1, 7, 1), (R_2, 8), (R_A, 7, 0), (R_2, 5),
        (R_L, 4), (R_L, 5), (R_L, 8), (R_E, 3), (R_A, 0, 0), (R_A, 0, 1), (R_L, 2), (SUM_R, 3),
        (R_1, 7, 0), (R_E, 1), (R_1, 6, 0), (SUM_S, 4), (R_2, 6), (R_E, 2), (R_L, 6), (R_2, 7),
        (R_L, 7), (R_1, 0, 0), (R_E, 4), (R_E, 5), (R_E, 8), (R_2, 0), (R_E, 7), (R_E, 6),
        (SUM_R, 4), (R_L, 0),
    ),
}


def layer_kernel(
    tok_hbm, len_ref, cot_hbm, wq_hbm, wl_hbm, wk_hbm, wv_hbm, wo_hbm, gain_one, gain_two, wg_hbm, wu_hbm, wd_ref,
    out_hbm, gtok_hbm, at_hbm, gain_hbm, gg_hbm, gu_hbm, gd_hbm,
    attn, latw, gate_a, up_a, gate_b, up_b, down_w, down_c, gain_full,
    tok, ends, bias, normed, query, latent, keys, values, merged, lse, middle, normed2, dout,
    mixed, dgate, dup, tmp, rcv_dn2, snd_out, rcv_out,
    dmid, dmid_low, dmerged, dquery, dkeys, dvalues, dlatent,
    pattn,
    s_d, s_ga, s_ua, s_gb, s_ub,
    y_d, y_ga, y_ua, y_gb, y_ub,
    z_d, z_ga, z_ua, z_gb, z_ub,
    x_ga, x_ua, x_gb, x_ub,
    s_a, x_a, z_a, y_a, sum_own, sum_rcv,
    send_sem, recv_sem, local_sem,
):
    snd_dn2 = dquery
    dp = lax.axis_index("dp")
    fs = lax.axis_index("fsdp")
    x, c, z, y = lax.div(dp, 2), lax.rem(dp, 2), lax.div(fs, 2), lax.rem(fs, 2)
    zh, zl = lax.div(z, 2), lax.rem(z, 2)
    sib = (x * 2 + 1 - c, fs)
    xp = ((1 - x) * 2 + c, fs)
    yp = (dp, z * 2 + 1 - y)
    z1 = (dp, (zh * 2 + 1 - zl) * 2 + y)
    z2 = (dp, ((1 - zh) * 2 + zl) * 2 + y)

    def rel(v, other):
        return 1 - v if other else v

    def line(dh, dl):
        return rel(zh, dh) * 2 + rel(zl, dl)

    sent, groups = {}, []

    def copy(src, dst, slot, target, group):
        if group not in groups:
            groups.append(group)
        return pltpu.make_async_remote_copy(
            src_ref=src, dst_ref=dst, send_sem=send_sem.at[groups.index(group)], recv_sem=recv_sem.at[slot],
            device_id=target, device_id_type=MESH,
        )

    def send(group, src, dst, slot, target):
        copy(src, dst, slot, target, group).start()
        sent[group] = sent.get(group, 0) + math.prod(src.shape) * src.dtype.itemsize

    def drain(group):
        tiles = sent.pop(group, 0) // 4096
        if tiles:
            wide = next(n for n in range(8, 0, -1) if tiles % n == 0 and tiles // n <= 128)
            size = tmp.at[pl.ds(0, tiles // wide * 8), pl.ds(0, wide * 128)]
            copy(size, size, 0, sib, group).wait_send()

    def arrive(dst, slot):
        copy(dst, dst, slot, sib, "sum").wait_recv()

    def local(src, dst, k):
        return pltpu.make_async_copy(src, dst, local_sem.at[k])

    def put(src, dst, k):
        local(src, dst, k).start()

    def add(dst, src):
        dst[...] = dst[...] + src[...]

    def cols(n, width=256):
        return pl.ds(pl.multiple_of(n * width, width), width)

    ops = {}

    def op(code):
        def enter(fn):
            ops[code] = fn
            return fn

        return enter

    def run(items):
        for name, *rest in items:
            ops[name](*rest)

    def gap(name):
        run(PLAN.get(name, ()))

    def loop(count, *stages, at=(), unroll=1):
        ends = [*at, count]
        for first, last in zip([0, *at], ends):

            def step(k, carry):
                for _, body in stages:
                    body(k)
                return carry

            if last - first == 1:
                for name, body in stages:
                    body(first)
                    gap((name, first))
            else:
                lax.fori_loop(first, last, step, 0, unroll=unroll)
                gap((stages[-1][0], last - 1))

    ways = {"y": yp, "x": xp, "1": z1, "2": z2, "s": sib}

    def a_blk(w, bits):
        route = ROUTE[w]
        across = {way: bits >> k & 1 for k, way in enumerate(route)}
        xx, cc, yy = rel(x, across["x"]), rel(c, across["s"]), rel(y, across["y"])
        zz = line(across["2"], across["1"])
        if w == 0:
            return latw.at[xx, cc, zz, yy]
        if w == 1:
            return attn.at[0, xx, cc, zz, yy]
        return attn.at[1, xx, cc, zz, yy, :, pl.ds(512 * (w - 2), 512)]

    def a_send(w, bits, k):
        blk = a_blk(w, bits)
        send("a%d" % w, blk, blk, S_A[w] + (bits + (1 << k) if k < 4 else 0), ways[ROUTE[w][k]])

    @op(AA)
    def aa(w, bits):
        if bits:
            arrive(a_blk(w, bits), S_A[w] + bits)
        a_send(w, bits, 4)

    @op(AG)
    def ag(w, bits, k):
        a_send(w, bits, k)

    @op(AT)
    def at(w):
        other = 1 - c
        half = pl.ds(512 * (w - 2), 512)
        arrive((latw.at[:, other], attn.at[0, :, other], attn.at[1, :, other, :, :, :, half])[min(w, 2)], S_A[w])

    ffn = (down_w, gate_a, up_a, gate_b, up_b)
    ffn_hbm = (None, wg_hbm, wu_hbm, wg_hbm, wu_hbm)
    starts = (None, 0, 0, 768, 768)

    def half_cols(xx, t):
        return pl.ds(pl.multiple_of(xx * HALF + starts[t], 128), ffn[t].shape[-1])

    @op(H_S)
    def h_s(t):
        send("half", ffn_hbm[t].at[:, half_cols(1 - x, t)], ffn[t].at[c, z, y, x], S_HALF + t, xp)

    @op(H_R)
    def h_r(t):
        arrive(ffn[t].at[c, z, y, 1 - x], S_HALF + t)

    def f_blk(t, bits):
        return ffn[t].at[rel(c, bits >> 3 & 1), line(bits & 1, bits >> 1 & 1), rel(y, bits >> 2 & 1)]

    def f_send(t, bits, k):
        blk = f_blk(t, bits)
        send("ffn%d" % t, blk, blk, S_F[t] + (bits + (1 << k) if k < 3 else 0), (z2, z1, yp, sib)[k])

    @op(FA)
    def fa(t, bits):
        if bits:
            arrive(f_blk(t, bits), S_F[t] + bits)
        f_send(t, bits, 3)

    @op(FG)
    def fg(t, bits, k):
        f_send(t, bits, k)

    @op(FT)
    def ft(t):
        arrive(ffn[t].at[1 - c], S_F[t])

    def quarter(ref, k):
        return ref.at[pl.ds(k * 64, 64)]

    @op(COT_S)
    def cot_s(k):
        send("cot", quarter(dout.at[x], k), quarter(dout.at[x], k), S_COT, xp)

    @op(COT_R)
    def cot_r():
        arrive(dout.at[1 - x], S_COT)

    @op(TOK_S)
    def tok_s(k):
        send("tok", quarter(tok.at[x], k), quarter(tok.at[x], k), S_TOK, xp)

    @op(TOK_R)
    def tok_r():
        arrive(tok.at[1 - x], S_TOK)

    @op(END_S)
    def end_s():
        send("tok", ends.at[x], ends.at[x], S_END, xp)

    @op(END_R)
    def end_r():
        arrive(ends.at[1 - x], S_END)

    @op(DN2_S)
    def dn2_s():
        send("dn2", snd_dn2, rcv_dn2, S_DN2, xp)

    @op(DN2_R)
    def dn2_r():
        arrive(rcv_dn2, S_DN2)

    @op(OUT_S)
    def out_s(k):
        send("out", quarter(snd_out, k), quarter(rcv_out, k), S_OUT, xp)

    @op(OUT_R)
    def out_r():
        arrive(rcv_out, S_OUT)

    ffn_s = (s_d, s_ga, s_ua, s_gb, s_ub)
    ffn_y = (y_d, y_ga, y_ua, y_gb, y_ub)
    ffn_zb = (z_d, z_ga, z_ua, z_gb, z_ub)
    ffn_x = (None, x_ga, x_ua, x_gb, x_ub)
    out_cols = (None, *[pl.ds(starts[t], ffn[t].shape[-1]) for t in range(1, FFN)])
    ffn_out = (None, *[gg_hbm, gu_hbm] * 2)

    def pick(i):
        return ((0, pl.ds(0, WIDTH)), (1, pl.ds(0, WIDTH)), (2, pl.ds(0, 512)), (2, pl.ds(512, 512)))[i - FFN]

    def sib_part(i, other):
        if i < FFN:
            yy = rel(y, other)
            return yy, ffn[i].at[1 - c, :, yy], ffn_s[i].at[yy], lambda zz: (ffn[i].at[c, zz, yy], ffn_s[i].at[yy, zz])
        k, cl = pick(i)
        if SUM_X_FIRST[i - FFN]:
            xx = rel(x, other)
            return (
                xx,
                pattn.at[k, xx, 1 - c, :, :, :, cl],
                s_a.at[k, xx, :, :, :, cl],
                lambda zz: (pattn.at[k, xx, c, zz, :, :, cl], s_a.at[k, xx, zz, :, :, cl]),
            )
        yy = rel(y, other)
        return (
            yy,
            pattn.at[k, :, 1 - c, :, yy, :, cl],
            s_a.at[k, :, :, yy, :, cl],
            lambda zz: (pattn.at[k, :, c, zz, yy, :, cl], s_a.at[k, :, zz, yy, :, cl]),
        )

    def first_hop(i, d):
        if i < FFN:
            return yp, ffn[i].at[c, d, 1 - y], ffn_y[i].at[d]
        k, cl = pick(i)
        if SUM_X_FIRST[i - FFN]:
            return xp, pattn.at[k, 1 - x, c, d, :, :, cl], x_a.at[k, d, :, :, cl]
        return yp, pattn.at[k, :, c, d, 1 - y, :, cl], x_a.at[k, d, :, :, cl]

    def line_blk(i, d):
        if i < FFN:
            return ffn[i].at[c, d, y]
        k, cl = pick(i)
        if SUM_X_FIRST[i - FFN]:
            return pattn.at[k, x, c, d, :, :, cl]
        return pattn.at[k, :, c, d, y, :, cl]

    def line_buf(i, b):
        if i < FFN:
            return ffn_zb[i].at[b]
        k, cl = pick(i)
        return z_a.at[k, b, :, :, cl]

    def last_hop(i):
        if i < FFN:
            return xp, ffn[i].at[c, z, y, 1 - x], ffn_x[i]
        k, cl = pick(i)
        if SUM_X_FIRST[i - FFN]:
            return yp, pattn.at[k, x, c, z, 1 - y, :, cl], y_a.at[k, :, cl]
        return xp, pattn.at[k, 1 - x, c, z, y, :, cl], y_a.at[k, :, cl]

    @op(R_GO)
    def r_go(i):
        for other in (1, 0):
            k, src, dst, _ = sib_part(i, other)
            send("r%d" % i, src, dst, S_R[i] + k, sib)

    @op(R_S)
    def r_s(i, other):
        k, _, dst, pairs = sib_part(i, other)
        arrive(dst, S_R[i] + k)
        if not other:
            for zz in range(4):
                add(*pairs(zz))

    @op(R_B)
    def r_b(i, bits):
        d = line(bits >> 1, bits & 1)
        add(*sib_part(i, 1)[3](d))
        target, src, buf = first_hop(i, d)
        send("r%d" % i, src, buf, S_R[i] + 2 + bits, target)

    @op(R_A)
    def r_a(i, bits):
        d = line(bits >> 1, bits & 1)
        _, _, buf = first_hop(i, d)
        arrive(buf, S_R[i] + 2 + bits)
        add(line_blk(i, d), buf)
        if bits & 1:
            send("r%d" % i, line_blk(i, d), line_buf(i, bits >> 1), S_R[i] + 6 + (bits >> 1), z1)

    @op(R_1)
    def r_1(i, dh):
        d = line(dh, 0)
        arrive(line_buf(i, dh), S_R[i] + 6 + dh)
        add(line_blk(i, d), line_buf(i, dh))
        if dh:
            send("r%d" % i, line_blk(i, d), line_buf(i, 2), S_R[i] + 8, z2)

    @op(R_2)
    def r_2(i):
        arrive(line_buf(i, 2), S_R[i] + 8)
        add(line_blk(i, z), line_buf(i, 2))

    @op(R_L)
    def r_l(i):
        if i == 0:
            put(down_w.at[c, z, y], gd_hbm, PUT)
            return
        target, src, buf = last_hop(i)
        send("r%d" % i, src, buf, S_R[i] + 9, target)
        if i < FFN:
            put(ffn[i].at[c, z, y, x], ffn_out[i].at[x, :, out_cols[i]], PUT + i * 2)

    @op(R_E)
    def r_e(i):
        _, _, buf = last_hop(i)
        arrive(buf, S_R[i] + 9)
        if i < FFN:
            put(buf, ffn_out[i].at[1 - x, :, out_cols[i]], PUT + 1 + i * 2)
        else:
            k, cl = pick(i)
            blk = pattn.at[k, x, c, z, y, :, cl]
            add(blk, buf)
            put(blk, at_hbm.at[k, :, cl], PUT + 4 + FFN + i)

    def wait_out():
        local(down_w.at[c, z, y], gd_hbm, PUT).wait()
        for i in range(1, FFN):
            local(ffn[i].at[c, z, y, x], ffn_out[i].at[x, :, out_cols[i]], PUT + i * 2).wait()
            local(ffn_x[i], ffn_out[i].at[1 - x, :, out_cols[i]], PUT + 1 + i * 2).wait()
        for i in range(FFN, FFN + 4):
            k, cl = pick(i)
            local(pattn.at[k, x, c, z, y, :, cl], at_hbm.at[k, :, cl], PUT + 4 + FFN + i).wait()

    sum_to = (sib, yp, xp, z1, z2)

    @op(SUM_S)
    def sum_s(i):
        copy(sum_own, sum_rcv.at[i], S_SUM + i, sum_to[i], "sum").start()

    @op(SUM_R)
    def sum_r(i):
        copy(sum_own, sum_rcv.at[i], S_SUM + i, sum_to[i], "sum").wait_send()
        arrive(sum_rcv.at[i], S_SUM + i)
        add(sum_own, sum_rcv.at[i])

    loads = [
        (wq_hbm, attn.at[0, x, c, z, y]),
        (wl_hbm, latw.at[x, c, z, y, :, pl.ds(0, 512)]),
        (wk_hbm, latw.at[x, c, z, y, pl.ds(0, 16), pl.ds(512, 512)]),
        (wv_hbm, latw.at[x, c, z, y, pl.ds(16, 16), pl.ds(512, 512)]),
        (wo_hbm, attn.at[1, x, c, z, y]),
        (tok_hbm, tok.at[x]),
        (cot_hbm, dout.at[x]),
        *[(ffn_hbm[t].at[:, half_cols(x, t)], ffn[t].at[c, z, y, x]) for t in range(1, FFN)],
    ]
    loads = [local(src, dst, k) for k, (src, dst) in enumerate(loads)]
    for load in loads:
        load.start()
    bar = pltpu.get_barrier_semaphore()

    def hello(target):
        pl.semaphore_signal(bar, inc=1, device_id=target, device_id_type=MESH)

    for target in (sib, xp, yp, z1, z2):
        hello(target)

    def piled(rows):
        return jnp.concatenate([rows[:, 0:512], rows[:, 512:WIDTH]], axis=0).astype(BF16)

    def stage_own():
        down_w[c, z, y] = piled(wd_ref[...].astype(F32))
        lane = lax.broadcasted_iota(jnp.int32, (16, 128), 1)
        mine = lax.div(lane, 32) == lax.rem(fs, 4)
        two = [ref[...].astype(F32).reshape(1, 32) for ref in (gain_one, gain_two)]
        two = jnp.concatenate([*two, jnp.zeros((14, 32), F32)], axis=0)
        two = jnp.where(mine, jnp.concatenate([two] * 4, axis=1), 0.0)
        latw[x, c, z, y, pl.ds(0, 16), pl.ds(WIDTH, 128)] = two.astype(BF16)
        latw[x, c, z, y, pl.ds(16, 16), pl.ds(WIDTH, 128)] = jnp.zeros((16, 128), BF16)

    e0 = len_ref[0]
    e1 = e0 + len_ref[1]
    e2 = e1 + len_ref[2]
    e3 = e2 + len_ref[3]

    def stage_ends():
        place = lax.broadcasted_iota(jnp.int32, (8, 128), 0)
        ends[x] = sum(jnp.where(place == k, e, 0) for k, e in enumerate((e0, e1, e2, e3))).astype(F32)

    stage_own()
    stage_ends()
    for load in loads[:5]:
        load.wait()
    pl.semaphore_wait(bar, 5)
    gap(G_START)

    for load in loads[5:]:
        load.wait()

    def mask_rows(k):
        rows = pl.ds(pl.multiple_of(k * 64, 64), 64)
        position = lax.broadcasted_iota(jnp.int32, (64, WIDTH), 0) + k * 64
        dout[x, rows] = jnp.where(position < e3, dout[x, rows].astype(F32), 0.0).astype(BF16)

    loop(4, (G_MASK, mask_rows))
    gap(G_WEIGHTS)

    def gain_rows(k):
        g = latw.at[lax.div(k, 4), lax.div(lax.rem(k, 4), 2)]
        part = g[pl.ds(lax.rem(k, 2) * 2, 2), :, 0:16, WIDTH : WIDTH + 128].astype(F32)
        gain_full[:, pl.ds(pl.multiple_of(k * 128, 128), 128)] = part[0, 0] + part[0, 1] + part[1, 0] + part[1, 1]

    loop(8, (G_GAIN, gain_rows))

    low_half = lax.broadcasted_iota(jnp.int32, (ROWS, 128), 1) < HEAD_DIM
    head_lane = lax.broadcasted_iota(jnp.int32, (ROWS, 128), 1)

    def halves(v):
        zero = jnp.zeros_like(v)
        return (jnp.where(low_half, v, zero), jnp.where(low_half, zero, v))

    def both(v):
        return jnp.concatenate(halves(v), axis=0)

    def scaled(v):
        return (v.astype(F32) * SCALE).astype(BF16)

    def up_weight(g, first):
        return latw[g, :, :, :, pl.ds(first, 16), pl.ds(512, 512)].reshape(256, 512)

    def segment(m, shape, axis):
        position = lax.broadcasted_iota(jnp.int32, shape, axis).astype(F32)
        return sum((position >= ends[m, pl.ds(k, 1), pl.ds(0, 1)]).astype(F32) for k in range(4))

    def stage_masks(m):
        row = lax.broadcasted_iota(jnp.int32, (ROWS, ROWS), 0)
        col = lax.broadcasted_iota(jnp.int32, (ROWS, ROWS), 1)
        same = segment(m, (ROWS, 1), 0) == segment(m, (1, ROWS), 1)
        bias[m] = jnp.where(same & (col <= row), 0.0, -1e30)

    def attention(m, own, at, normed, query, latent, keys, values, merged, middle):
        at_norm, at_latent, at_keys, at_query, at_attend, at_middle, at_norm2 = at

        def norm_rows(k):
            rows = pl.ds(pl.multiple_of(k * 64, 64), 64)
            val = tok[m, rows].astype(F32)
            r1 = lax.rsqrt(jnp.mean(val * val, axis=1, keepdims=True) + EPSILON)
            normed[rows] = (val * r1 * gain_full[0:1, :]).astype(BF16)

        def latent_cols(n):
            w = latw[:, :, :, :, :, cols(n)].reshape(WIDTH, 256)
            latent[:, cols(n)] = nn(normed[...], w).astype(BF16)

        def key_cols(g):
            lat = latent[:, cols(g)]
            keys[:, cols(g, 512)] = nn(lat, up_weight(g, 0)).astype(BF16)
            values[:, cols(g, 512)] = nn(lat, up_weight(g, 16)).astype(BF16)

        def query_cols(n):
            w = attn[0, :, :, :, :, :, cols(n)].reshape(WIDTH, 256)
            query[:, cols(n)] = nn(normed[...], w).astype(BF16)

        def attend(j):
            pair = cols(j, 128)
            s = nt(both(scaled(query[:, pair])), keys[:, pair]) + jnp.concatenate([bias[m]] * 2, axis=0)
            peak = jnp.max(s, axis=1, keepdims=True)
            expo = jnp.exp(s - peak)
            total = jnp.sum(expo, axis=1, keepdims=True)
            res = nn((expo / total).astype(BF16), values[:, pair])
            merged[:, pair] = jnp.where(low_half, res[0:ROWS], res[ROWS : 2 * ROWS]).astype(BF16)
            if own:
                logsum = peak + jnp.log(total)
                lse[...] = jnp.where(
                    head_lane == j * 2,
                    logsum[0:ROWS],
                    jnp.where(head_lane == j * 2 + 1, logsum[ROWS : 2 * ROWS], lse[...]),
                )

        def middle_cols(n):
            w = attn[1, :, :, :, :, :, cols(n)].reshape(WIDTH, 256)
            middle[:, cols(n)] = tok[m, :, cols(n)].astype(F32) + nn(merged[...], w)

        def norm2_rows(k):
            rows = pl.ds(pl.multiple_of(k * 64, 64), 64)
            val = middle[rows]
            r2 = lax.rsqrt(jnp.mean(val * val, axis=1, keepdims=True) + EPSILON)
            normed2[m, rows] = (val * r2 * gain_full[1:2, :]).astype(BF16)

        def first():
            stage_masks(m)
            loop(4, (at_norm, norm_rows))
            loop(2, (at_latent, latent_cols), unroll=2)
            loop(GROUPS, (at_keys, key_cols), unroll=2)

        def second():
            loop(4, (at_query, query_cols), unroll=2)
            loop(8, (at_attend, attend), at=(4,), unroll=4)

        def third():
            loop(4, (at_middle, middle_cols), unroll=2)
            loop(4, (at_norm2, norm2_rows))

        return first, second, third

    def compact(k):
        pair = down_w.at[lax.div(k, 4), lax.rem(k, 4)]
        one, two = pair[0].astype(F32), pair[1].astype(F32)
        rows = pl.ds(pl.multiple_of(k * 2 * DOWN, 16), 2 * DOWN)
        for half in range(2):
            part = slice(half * DOWN, (half + 1) * DOWN)
            down_c[rows, pl.ds(half * 512, 512)] = jnp.concatenate([one[part], two[part]], axis=0).astype(BF16)

    at = (G_NORM, G_LATENT, G_KEYS, G_QUERY, G_ATTEND, G_MIDDLE, G_NORM2)
    own = attention(x, True, at, normed, query, latent, keys, values, merged, middle)
    at = (G_NORM_P, G_LATENT_P, G_KEYS_P, G_QUERY_P, G_ATTEND_P, G_MIDDLE_P, G_NORM2_P)
    across = attention(1 - x, False, at, dmid_low, dquery, dlatent, dkeys, dvalues, dmerged, dmid)
    own[0]()
    gap(G_ACROSS)
    across[0]()
    gap(G_DOWN_W)
    loop(8, (G_COMPACT, compact))
    gap(G_QUERY)
    own[1]()
    across[1]()
    gap(G_OUTPUT_W)
    own[2]()
    across[2]()
    gap(G_FFN_A)

    def ffn_w(ref, half, sl=slice(None)):
        w = ref[:, :, :, half, :, sl]
        return w.reshape(512, w.shape[-1])

    def hidden(it, gate_w, up_w, base, widths):
        m = rel(x, it)
        rows = pl.ds(pl.multiple_of(m * ROWS, ROWS), ROWS)
        for first, width in widths:
            sl, at = pl.ds(first, width), pl.ds(base + first, width)
            n2 = normed2[m]
            gate = nn(n2[:, 0:512], ffn_w(gate_w, 0, sl)) + nn(n2[:, 512:1024], ffn_w(gate_w, 1, sl))
            upper = nn(n2[:, 0:512], ffn_w(up_w, 0, sl)) + nn(n2[:, 512:1024], ffn_w(up_w, 1, sl))
            dmix = nt(dout[m], down_c[at])
            sig = jax.nn.sigmoid(gate)
            silu = gate * sig
            mixed[rows, at] = (silu * upper).astype(BF16)
            dgate[rows, at] = (dmix * upper * sig * (1.0 + gate * (1.0 - sig))).astype(BF16)
            dup[rows, at] = (dmix * silu).astype(BF16)

    def dn_half(it, gate_w, up_w, at, more):
        m = rel(x, it)
        rows = pl.ds(pl.multiple_of(m * ROWS, ROWS), ROWS)
        for half in range(2):
            part = nt(dgate[rows, at], ffn_w(gate_w, half)) + nt(dup[rows, at], ffn_w(up_w, half))
            to = (pl.ds(ROWS * it, ROWS), pl.ds(half * 512, 512))
            if more:
                part = part + tmp[to]
            if more == 2 and it:
                snd_dn2[:, pl.ds(half * 512, 512)] = part.astype(BF16)
            else:
                tmp[to] = part

    def grad_gate_up(it, gate_w, up_w, at):
        cc = jnp.where(it < 2, 1 - c, c)
        half = lax.rem(it, 2)
        sl = pl.ds(pl.multiple_of(half * 512 + cc * 256, 256), 256)
        width = gate_w.shape[-1]
        for src, dst in ((dgate, gate_w), (dup, up_w)):
            g = nn(normed2[0, :, sl].T, src[pl.ds(0, ROWS), at]) + nn(normed2[1, :, sl].T, src[pl.ds(ROWS, ROWS), at])
            dst[cc, :, :, half] = g.astype(BF16).reshape(4, 2, 32, width)

    def grad_down(it):
        cc = rel(c, it == 0)
        wide = pl.ds(pl.multiple_of(cc * 640, 128), 768)
        mt = mixed[:, wide].T
        tmp[pl.ds(ROWS, 768)] = nn(mt[:, 0:256], dout[0]) + nn(mt[:, 256:512], dout[1])

        def split(k, carry):
            rows = tmp[pl.ds(pl.multiple_of(ROWS + cc * 64 + k * DOWN, 8), DOWN)]
            down_w[cc, lax.div(k, 2), lax.rem(k, 2)] = piled(rows)
            return carry

        lax.fori_loop(0, 8, split, 0)

    def hidden_a(it):
        hidden(it, gate_a, up_a, 0, ((0, 512), (512, 256)))

    def dn_a(it):
        dn_half(it, gate_a, up_a, pl.ds(0, 768), 0)

    def gateup_a(it):
        grad_gate_up(it, gate_a, up_a, pl.ds(0, 768))

    def hidden_b(it):
        hidden(it, gate_b, up_b, 768, ((0, 512), (512, 128)))

    def dn_b(it):
        dn_half(it, gate_b, up_b, pl.ds(768, 640), 2)

    def gateup_b(it):
        grad_gate_up(it, gate_b, up_b, pl.ds(768, 640))

    def out_half(it):
        m = rel(x, it == 0)
        rows = pl.ds(pl.multiple_of(m * ROWS, ROWS), ROWS)
        part = nn(mixed[rows], down_c[...])
        if it == 0:
            snd_out[...] = part.astype(BF16)
        else:
            tmp[pl.ds(ROWS, ROWS)] = part

    loop(2, (G_HIDDEN_A, hidden_a), at=(1,))
    loop(2, (G_DN_A, dn_a), at=(1,))
    drain("ffn1")
    drain("ffn2")
    loop(4, (G_GATEUP_A, gateup_a), at=(2,))
    gap(G_FFN_B)
    hidden_b(1)
    gap((G_HIDDEN_B, 1))
    dn_b(1)
    gap((G_DN_B, 1))
    hidden_b(0)
    gap((G_HIDDEN_B, 0))
    dn_b(0)
    gap((G_DN_B, 0))
    drain("ffn0")
    loop(2, (G_DOWN, grad_down), at=(1,))
    drain("ffn3")
    drain("ffn4")
    loop(4, (G_GATEUP_B, gateup_b), at=(2,))
    loop(2, (G_OUT, out_half), at=(1,))
    gap(G_BACK)

    sum_own[...] = jnp.zeros((8, WIDTH), F32)

    def back_two(k):
        rows = pl.ds(pl.multiple_of(k * 32, 32), 32)
        mid = middle[rows]
        r2 = lax.rsqrt(jnp.mean(mid * mid, axis=1, keepdims=True) + EPSILON)
        grad = tmp[rows] + rcv_dn2[rows].astype(F32)
        sum_own[1:2] = sum_own[1:2] + jnp.sum(grad * mid * r2, axis=0, keepdims=True)
        s = grad * gain_full[1:2, :]
        res = dout[x, rows].astype(F32) + r2 * (s - mid * r2 * r2 * jnp.mean(s * mid, axis=1, keepdims=True))
        dmid[rows] = res
        dmid_low[rows] = res.astype(BF16)

    loop(8, (G_NORM2B, back_two), unroll=2)

    def dmerged_cols(k):
        w = attn[1, lax.div(k, 2), lax.rem(k, 2)].reshape(256, WIDTH)
        dmerged[:, cols(k)] = nt(dmid_low[...], w).astype(BF16)

    loop(4, (G_DMERGED, dmerged_cols), unroll=2)

    def grad_output(it):
        cc = jnp.where(it < 2, 1 - c, c)
        half = lax.rem(it, 2)
        g = nn(merged[:, cols(half * 2 + cc)].T, dmid_low[...])
        pattn[0, half, cc] = g.astype(BF16).reshape(4, 2, 32, WIDTH)

    loop(4, (G_OUTPUT, grad_output), at=(2,), unroll=2)

    drain("dn2")

    def attend_back(j):
        pair = cols(j, 128)
        k_pair, v_pair = keys[:, pair], values[:, pair]
        q, do = both(scaled(query[:, pair])), both(dmerged[:, pair])
        logsum = jnp.concatenate(
            [jnp.sum(jnp.where(head_lane == j * 2 + h, lse[...], 0.0), axis=1, keepdims=True) for h in (0, 1)], axis=0
        )
        probs = jnp.exp(nt(q, k_pair) + jnp.concatenate([bias[x]] * 2, axis=0) - logsum)
        dprobs = nt(do, v_pair)
        dvalues[:, pair] = tn(probs.astype(BF16), do).astype(BF16)
        row_sum = jnp.sum(probs * dprobs, axis=1, keepdims=True)
        dscores = (probs * (dprobs - row_sum)).astype(BF16)
        dq = nn(dscores, k_pair)
        dkeys[:, pair] = tn(dscores, q).astype(BF16)
        dquery[:, pair] = (jnp.where(low_half, dq[0:ROWS], dq[ROWS : 2 * ROWS]) * SCALE).astype(BF16)

    loop(8, (G_ATTENDB, attend_back), at=(4,), unroll=2)

    def other_first(it):
        cc = jnp.where(it < 2, 1 - c, c)
        return lax.rem(it, 2), cc

    def grad_query(it):
        half, cc = other_first(it)
        g = nn(normed[:, cols(half * 2 + cc)].T, dquery[...])
        pattn[1, half, cc] = g.astype(BF16).reshape(4, 2, 32, WIDTH)

    loop(4, (G_PROJQ, grad_query), at=(2,), unroll=2)

    def latent_back(g):
        dk, dv = dkeys[:, cols(g, 512)], dvalues[:, cols(g, 512)]
        dlatent[:, cols(g)] = (nt(dk, up_weight(g, 0)) + nt(dv, up_weight(g, 16))).astype(BF16)
        lat = latent[:, cols(g)].T
        pattn[2, g, :, :, :, pl.ds(0, 16), pl.ds(512, 512)] = nn(lat, dk).astype(BF16).reshape(2, 4, 2, 16, 512)
        pattn[2, g, :, :, :, pl.ds(16, 16), pl.ds(512, 512)] = nn(lat, dv).astype(BF16).reshape(2, 4, 2, 16, 512)

    loop(GROUPS, (G_LATENTB, latent_back))

    def grad_latent(it):
        half, cc = other_first(it)
        g = nn(normed[:, cols(half * 2 + cc)].T, dlatent[...])
        pattn[2, half, cc, :, :, :, pl.ds(0, 512)] = g.astype(BF16).reshape(4, 2, 32, 512)

    loop(4, (G_PROJL, grad_latent), at=(2,), unroll=2)

    def dnormed_cols(k):
        xx, cc = lax.div(k, 2), lax.rem(k, 2)
        part = nt(dquery[...], attn[0, xx, cc].reshape(256, WIDTH))
        part = part + nt(dlatent[...], latw[xx, cc, :, :, :, pl.ds(0, 512)].reshape(256, 512))
        tmp[pl.ds(0, ROWS), cols(k)] = part

    loop(4, (G_DNORMED, dnormed_cols), unroll=2)

    def back_one(k):
        rows = pl.ds(pl.multiple_of(k * 32, 32), 32)
        val = tok[x, rows].astype(F32)
        r1 = lax.rsqrt(jnp.mean(val * val, axis=1, keepdims=True) + EPSILON)
        grad = tmp[rows]
        sum_own[0:1] = sum_own[0:1] + jnp.sum(grad * val * r1, axis=0, keepdims=True)
        s = grad * gain_full[0:1, :]
        dmid[rows] = dmid[rows] + r1 * (s - val * r1 * r1 * jnp.mean(s * val, axis=1, keepdims=True))

    loop(8, (G_NORM1B, back_one), unroll=2)
    to_gtok = local(dmid, gtok_hbm, 0)
    to_gtok.start()
    gap(G_RESULT)

    def out_rows(k):
        rows = pl.ds(pl.multiple_of(k * 32, 32), 32)
        part = tmp[pl.ds(pl.multiple_of(ROWS + k * 32, 32), 32)]
        tok[x, rows] = (middle[rows] + (part + rcv_out[rows].astype(F32))).astype(BF16)

    drain("tok")
    loop(8, (G_RESULT, out_rows))
    to_out = local(tok.at[x], out_hbm, 1)
    to_out.start()
    gap(G_TAIL)
    to_gain = local(sum_own.at[:, pl.ds(pl.multiple_of((dp * 2 + lax.div(fs, 4)) * 128, 128), 128)], gain_hbm, 2)
    to_gain.start()
    for group in list(sent):
        drain(group)
    to_gtok.wait()
    to_out.wait()
    to_gain.wait()
    wait_out()


def finish_kernel(*refs):
    given, outs, bufs, casts = refs[:7], refs[7:19], refs[19:26], refs[26:36]
    in_sem, out_sem = refs[36:]
    takes = [pltpu.make_async_copy(src, dst, in_sem.at[k]) for k, (src, dst) in enumerate(zip(given, bufs))]
    gives = [pltpu.make_async_copy(src, dst, out_sem.at[k]) for k, (src, dst) in enumerate(zip([*bufs[:2], *casts], outs))]
    for k in (1, 0, 4, 5, 6, 2, 3):
        takes[k].start()
    for k in (1, 0):
        takes[k].wait()
        gives[k].start()
    _, _, at_ref, gain_ref, gg_ref, gu_ref, gd_ref = bufs
    gq_o, gl_o, gk_o, gv_o, go_o, ga_o, gf_o, gg_o, gu_o, gd_o = casts
    for k, src, dst in ((4, gg_ref, gg_o), (5, gu_ref, gu_o)):
        takes[k].wait()
        dst[:, 0:HALF] = src[0].astype(F32)
        dst[:, HALF : 2 * HALF] = src[1].astype(F32)
        gives[k + 5].start()
    takes[6].wait()
    gd = gd_ref[...].astype(F32)
    gd_o[:, 0:512] = gd[0:DOWN]
    gd_o[:, 512:WIDTH] = gd[DOWN : 2 * DOWN]
    gives[11].start()
    takes[2].wait()
    go_o[...] = at_ref[0].astype(F32)
    gq_o[...] = at_ref[1].astype(F32)
    gl_o[...] = at_ref[2, :, 0:512].astype(F32)
    gk_o[...] = at_ref[2, 0:16, 512:1024].astype(F32)
    gv_o[...] = at_ref[2, 16:32, 512:1024].astype(F32)
    takes[3].wait()
    place = lax.rem(lax.axis_index("fsdp"), 4)
    picked = sum(jnp.where(place == k, gain_ref[:, 32 * k : 32 * k + 32], 0.0) for k in range(4))
    ga_o[...] = picked[0:1]
    gf_o[...] = picked[1:2]
    for k in range(2, 9):
        gives[k].start()
    for give in gives:
        give.wait()


def kernel_on_device(
    tokens, seq_lengths, cotangent, w_query, w_latent, w_keyup, w_valup, w_output, norm_attn, norm_ffn,
    w_gate, w_up, w_down,
):
    hbm, vmem = pl.BlockSpec(memory_space=pl.ANY), pl.BlockSpec(memory_space=pltpu.VMEM)
    smem = pl.BlockSpec(memory_space=pltpu.SMEM)
    shape = jax.ShapeDtypeStruct
    outs = [
        shape((ROWS, WIDTH), BF16), shape((ROWS, WIDTH), F32), shape((3, 32, WIDTH), BF16), shape((8, 128), F32),
        shape((2, 32, HALF), BF16), shape((2, 32, HALF), BF16), shape((2 * DOWN, 512), BF16),
    ]
    V = pltpu.VMEM
    units = [(2 * DOWN, 512), *[(2, 32, width) for width in PARTS for _ in range(2)]]
    act = V((ROWS, WIDTH), BF16)
    scratch = [
        V((2, 2, 2, 4, 2, 32, WIDTH), BF16), V((2, 2, 4, 2, 32, WIDTH + 128), BF16),
        *[V((2, 4, 2, *unit), BF16) for unit in units[1:]],
        V((2, 4, 2, 2 * DOWN, 512), BF16), V((HALF, WIDTH), BF16), V((16, WIDTH), F32),
        V((2, ROWS, WIDTH), BF16), V((2, 8, 128), F32), V((2, ROWS, ROWS), F32), act, act, V((ROWS, 512), BF16), act, act, act, V((ROWS, 128), F32),
        V((ROWS, WIDTH), F32), V((2, ROWS, WIDTH), BF16), V((2, ROWS, WIDTH), BF16),
        V((512, HALF), BF16), V((512, HALF), BF16), V((512, HALF), BF16), V((ROWS + 768, WIDTH), F32),
        act, act, act,
        V((ROWS, WIDTH), F32), act, act, act, act, act, V((ROWS, 512), BF16),
        V((3, 2, 2, 4, 2, 32, WIDTH), BF16),
        *[V((2, 4, *unit), BF16) for unit in units],
        *[V((4, *unit), BF16) for unit in units],
        *[V((3, *unit), BF16) for unit in units],
        *[V(unit[1:], BF16) for unit in units[1:]],
        V((3, 2, 4, 2, 32, WIDTH), BF16), V((3, 4, 2, 32, WIDTH), BF16),
        V((3, 3, 2, 32, WIDTH), BF16), V((3, 32, WIDTH), BF16), V((8, WIDTH), F32), V((5, 8, WIDTH), F32),
        pltpu.SemaphoreType.DMA((2 * FFN + 14,)), pltpu.SemaphoreType.DMA((SLOTS.count,)), pltpu.SemaphoreType.DMA((PUT + 8 + 2 * FFN,)),
    ]
    res = pl.pallas_call(
        layer_kernel,
        out_shape=outs,
        in_specs=[hbm, smem, hbm, hbm, hbm, hbm, hbm, hbm, vmem, vmem, hbm, hbm, vmem],
        out_specs=[hbm] * len(outs),
        scratch_shapes=scratch,
        compiler_params=pltpu.CompilerParams(
            collective_id=0, has_side_effects=True, vmem_limit_bytes=63 * 2**20
        ),
    )(
        tokens, seq_lengths, cotangent, w_query, w_latent, w_keyup, w_valup, w_output, norm_attn, norm_ffn,
        w_gate, w_up, w_down,
    )
    final = [
        shape((ROWS, WIDTH), BF16), shape((ROWS, WIDTH), F32), shape((32, WIDTH), F32), shape((32, 512), F32),
        shape((16, 512), F32), shape((16, 512), F32), shape((32, WIDTH), F32), shape((1, 32), F32), shape((1, 32), F32),
        shape((32, 2 * HALF), F32), shape((32, 2 * HALF), F32), shape((DOWN, WIDTH), F32),
    ]
    out = pl.pallas_call(
        finish_kernel,
        out_shape=final,
        in_specs=[hbm] * 7,
        out_specs=[hbm] * 12,
        scratch_shapes=[
            *[V(one.shape, one.dtype) for one in [*outs, *final[2:]]],
            pltpu.SemaphoreType.DMA((7,)), pltpu.SemaphoreType.DMA((12,)),
        ],
    )(*res)
    return tuple(out[:7]) + (out[7].reshape(32), out[8].reshape(32)) + tuple(out[9:])


def solution(mesh):
    fits = dict(mesh.shape) == {"dp": 4, "fsdp": 8}
    return jax.shard_map(
        kernel_on_device if fits else on_device,
        mesh=mesh,
        in_specs=(
            P(("dp", "fsdp"), None),
            P(("dp", "fsdp")),
            P(("dp", "fsdp"), None),
            P(("dp", "fsdp"), None),
            P(("dp", "fsdp"), None),
            P(("dp", "fsdp"), None),
            P(("dp", "fsdp"), None),
            P(("dp", "fsdp"), None),
            P(("dp", "fsdp")),
            P(("dp", "fsdp")),
            P(("dp", "fsdp"), None),
            P(("dp", "fsdp"), None),
            P(("dp", "fsdp"), None),
        ),
        out_specs=(
            P(("dp", "fsdp"), None),
            P(("dp", "fsdp"), None),
            P(("dp", "fsdp"), None),
            P(("dp", "fsdp"), None),
            P(("dp", "fsdp"), None),
            P(("dp", "fsdp"), None),
            P(("dp", "fsdp"), None),
            P(("dp", "fsdp")),
            P(("dp", "fsdp")),
            P(("dp", "fsdp"), None),
            P(("dp", "fsdp"), None),
            P(("dp", "fsdp"), None),
        ),
        check_vma=False,
    )
```

```python
import math

import jax
import jax.numpy as jnp
from jax import lax
from jax.experimental import pallas as pl
from jax.experimental.pallas import tpu as pltpu
from jax.sharding import PartitionSpec as P

HEADS = 16
HEAD_DIM = 64
GROUPS = 2
LATENT = 256


EPSILON = 1e-06


def matmul(left, right):
    return jnp.dot(left, right, preferred_element_type=jnp.float32)


def matmul_left(left, right):
    return lax.dot_general(
        left, right, (((0,), (0,)), ((), ())), preferred_element_type=jnp.float32
    )


def matmul_right(left, right):
    return lax.dot_general(
        left, right, (((1,), (1,)), ((), ())), preferred_element_type=jnp.float32
    )


def segment_mask(lengths, rows):
    position = jnp.arange(rows, dtype=jnp.int32)
    ends = jnp.cumsum(lengths)
    segment = jnp.sum((position[None, :] >= ends[:, None]).astype(jnp.int32), axis=0)
    allowed = (segment[:, None] == segment[None, :]) & (position[None, :] <= position[:, None])
    valid = (position < ends[-1]).astype(jnp.float32)
    return (allowed, valid)


def head_forward(allowed, scale):

    def one_head(operands):
        query, key_rows, value_rows = operands
        scores = jnp.where(allowed, matmul_right(query, key_rows) * scale, -1e30)
        peak = jnp.max(scores, axis=1, keepdims=True)
        expo = jnp.exp(scores - peak)
        total = jnp.sum(expo, axis=1, keepdims=True)
        weights = (expo / total).astype(jnp.bfloat16)
        result = matmul(weights, value_rows).astype(jnp.bfloat16)
        return (result, peak[:, 0] + jnp.log(total[:, 0]))

    return one_head


def head_backward(allowed, scale):

    def one_head(operands):
        query, key_rows, value_rows, grad_out, logsum = operands
        scores = jnp.where(allowed, matmul_right(query, key_rows) * scale, -1e30)
        probs = jnp.exp(scores - logsum[:, None])
        grad_value = matmul_left(probs.astype(jnp.bfloat16), grad_out)
        grad_probs = matmul_right(grad_out, value_rows)
        inner = jnp.sum(probs * grad_probs, axis=1, keepdims=True)
        grad_scores = (probs * (grad_probs - inner)).astype(jnp.bfloat16)
        grad_query = matmul(grad_scores, key_rows) * scale
        grad_key = matmul_left(grad_scores, query) * scale
        return (grad_query, grad_key, grad_value)

    return one_head


def norm_back(grad_normed, inputs, rstd, gain):
    scaled = grad_normed * gain
    grad_in = rstd * (
        scaled - inputs * rstd * rstd * jnp.mean(scaled * inputs, axis=1, keepdims=True)
    )
    grad_gain = jnp.sum(grad_normed * inputs * rstd, axis=0)
    return (grad_in, grad_gain)


def column_term(left, right):
    return matmul_left(left, right).astype(jnp.bfloat16)


def forward(tokens, allowed, attn_w, ffn_w):
    w_query, w_latent, w_keyup, w_valup, w_output, gain_one = attn_w
    gain_two, w_gate, w_up, w_down = ffn_w
    rows = tokens.shape[0]
    inputs = tokens.astype(jnp.float32)
    rstd_one = lax.rsqrt(jnp.mean(inputs * inputs, axis=1, keepdims=True) + EPSILON)
    normed = (inputs * rstd_one * gain_one.astype(jnp.float32)).astype(jnp.bfloat16)
    query = matmul(normed, w_query).astype(jnp.bfloat16)
    latent = matmul(normed, w_latent).astype(jnp.bfloat16)
    lat3 = latent.reshape(rows, GROUPS, LATENT)
    keys = jnp.einsum(
        "tgl,glf->tgf",
        lat3,
        w_keyup.reshape(GROUPS, LATENT, -1),
        preferred_element_type=jnp.float32,
    ).astype(jnp.bfloat16)
    values = jnp.einsum(
        "tgl,glf->tgf",
        lat3,
        w_valup.reshape(GROUPS, LATENT, -1),
        preferred_element_type=jnp.float32,
    ).astype(jnp.bfloat16)
    heads_query = query.reshape(rows, HEADS, HEAD_DIM).transpose(1, 0, 2)
    heads_key = keys.reshape(rows, HEADS, HEAD_DIM).transpose(1, 0, 2)
    heads_value = values.reshape(rows, HEADS, HEAD_DIM).transpose(1, 0, 2)
    attended, logsum = lax.map(
        head_forward(allowed, HEAD_DIM ** (-0.5)), (heads_query, heads_key, heads_value)
    )
    merged = attended.transpose(1, 0, 2).reshape(rows, HEADS * HEAD_DIM)
    middle = inputs + matmul(merged, w_output)
    rstd_two = lax.rsqrt(jnp.mean(middle * middle, axis=1, keepdims=True) + EPSILON)
    normed_two = (middle * rstd_two * gain_two.astype(jnp.float32)).astype(jnp.bfloat16)
    gate = matmul(normed_two, w_gate)
    upper = matmul(normed_two, w_up)
    mixed = (jax.nn.silu(gate) * upper).astype(jnp.bfloat16)
    result = middle + matmul(mixed, w_down)
    return (
        result,
        inputs,
        rstd_one,
        normed,
        lat3,
        heads_query,
        heads_key,
        heads_value,
        logsum,
        merged,
        middle,
        rstd_two,
        normed_two,
        gate,
        upper,
        mixed,
    )


def on_device(
    tokens,
    seq_lengths,
    cotangent,
    w_query,
    w_latent,
    w_keyup,
    w_valup,
    w_output,
    norm_attn,
    norm_ffn,
    w_gate,
    w_up,
    w_down,
):
    rows = tokens.shape[0]
    allowed, valid = segment_mask(seq_lengths, rows)
    attn_w = (
        lax.all_gather(w_query, ("dp", "fsdp"), axis=0, tiled=True),
        lax.all_gather(w_latent, ("dp", "fsdp"), axis=0, tiled=True),
        lax.all_gather(w_keyup, ("dp", "fsdp"), axis=0, tiled=True),
        lax.all_gather(w_valup, ("dp", "fsdp"), axis=0, tiled=True),
        lax.all_gather(w_output, ("dp", "fsdp"), axis=0, tiled=True),
        lax.all_gather(norm_attn, ("dp", "fsdp"), axis=0, tiled=True),
    )
    ffn_w = (
        lax.all_gather(norm_ffn, ("dp", "fsdp"), axis=0, tiled=True),
        lax.all_gather(w_gate, ("dp", "fsdp"), axis=0, tiled=True),
        lax.all_gather(w_up, ("dp", "fsdp"), axis=0, tiled=True),
        lax.all_gather(w_down, ("dp", "fsdp"), axis=0, tiled=True),
    )
    saved = forward(tokens, allowed, attn_w, ffn_w)
    block_out = saved[0].astype(jnp.bfloat16)
    (
        result,
        inputs,
        rstd_one,
        normed,
        lat3,
        heads_query,
        heads_key,
        heads_value,
        logsum,
        merged,
        middle,
        rstd_two,
        normed_two,
        gate,
        upper,
        mixed,
    ) = saved
    full_query, full_latent, full_keyup, full_valup, full_output, gain_one = attn_w
    gain_two, full_gate, full_up, full_down = ffn_w
    ff_width = full_gate.shape[1]
    grad_out = cotangent.astype(jnp.float32) * valid[:, None]
    grad_low = grad_out.astype(jnp.bfloat16)
    grad_mixed = matmul_right(grad_low, full_down)
    sigmoid_gate = jax.nn.sigmoid(gate)
    grad_gate_low = (
        grad_mixed * upper * sigmoid_gate * (1.0 + gate * (1.0 - sigmoid_gate))
    ).astype(jnp.bfloat16)
    grad_upper_low = (grad_mixed * jax.nn.silu(gate)).astype(jnp.bfloat16)
    grad_normed_two = matmul_right(grad_gate_low, full_gate) + matmul_right(grad_upper_low, full_up)
    grad_mid_norm, grad_gain_two = norm_back(
        grad_normed_two, middle, rstd_two, gain_two.astype(jnp.float32)
    )
    grad_middle = grad_out + grad_mid_norm
    down_own = lax.psum_scatter(
        column_term(mixed, grad_low), ("dp", "fsdp"), scatter_dimension=0, tiled=True
    )
    packed_ffn = jnp.concatenate([grad_gate_low, grad_upper_low], axis=1)
    ffn_own = lax.psum_scatter(
        column_term(normed_two, packed_ffn), ("dp", "fsdp"), scatter_dimension=0, tiled=True
    )
    grad_branch = grad_middle.astype(jnp.bfloat16)
    grad_merged = matmul_right(grad_branch, full_output).astype(jnp.bfloat16)
    output_own = lax.psum_scatter(
        column_term(merged, grad_branch), ("dp", "fsdp"), scatter_dimension=0, tiled=True
    )
    heads_grad = grad_merged.reshape(rows, HEADS, HEAD_DIM).transpose(1, 0, 2)
    grad_hq, grad_hk, grad_hv = lax.map(
        head_backward(allowed, HEAD_DIM ** (-0.5)),
        (heads_query, heads_key, heads_value, heads_grad, logsum),
    )
    grad_query_low = grad_hq.transpose(1, 0, 2).reshape(rows, HEADS * HEAD_DIM).astype(jnp.bfloat16)
    grad_keys_low = grad_hk.transpose(1, 0, 2).reshape(rows, GROUPS, -1).astype(jnp.bfloat16)
    grad_values_low = grad_hv.transpose(1, 0, 2).reshape(rows, GROUPS, -1).astype(jnp.bfloat16)
    head_cols = grad_keys_low.shape[2]
    keyup3 = full_keyup.reshape(GROUPS, LATENT, -1)
    valup3 = full_valup.reshape(GROUPS, LATENT, -1)
    grad_lat = jnp.einsum("tgf,glf->tgl", grad_keys_low, keyup3, preferred_element_type=jnp.float32)
    grad_lat = grad_lat + jnp.einsum(
        "tgf,glf->tgl", grad_values_low, valup3, preferred_element_type=jnp.float32
    )
    grad_latent_low = grad_lat.reshape(rows, GROUPS * LATENT).astype(jnp.bfloat16)
    latent_flat = lat3.reshape(rows, GROUPS * LATENT)
    paired = jnp.concatenate([grad_keys_low, grad_values_low], axis=2).reshape(
        rows, GROUPS * 2 * head_cols
    )
    count = w_keyup.shape[0] * lax.axis_size(("dp", "fsdp"))
    product = matmul_left(latent_flat, paired).reshape(count, GROUPS, 2 * head_cols)
    owner = jnp.arange(count, dtype=jnp.int32) // LATENT
    picker = (owner[:, None] == jnp.arange(GROUPS, dtype=jnp.int32)[None, :]).astype(jnp.float32)
    latent_own = lax.psum_scatter(
        jnp.sum(product * picker[:, :, None], axis=1).astype(jnp.bfloat16),
        ("dp", "fsdp"),
        scatter_dimension=0,
        tiled=True,
    )
    grad_normed = matmul_right(grad_query_low, full_query) + matmul_right(
        grad_latent_low, full_latent
    )
    packed_attn = jnp.concatenate([grad_query_low, grad_latent_low], axis=1)
    attn_own = lax.psum_scatter(
        column_term(normed, packed_attn), ("dp", "fsdp"), scatter_dimension=0, tiled=True
    )
    grad_in_norm, grad_gain_one = norm_back(
        grad_normed, inputs, rstd_one, gain_one.astype(jnp.float32)
    )
    grad_tokens = grad_middle + grad_in_norm
    gains_own = (
        lax.psum_scatter(grad_gain_one, ("dp", "fsdp"), scatter_dimension=0, tiled=True),
        lax.psum_scatter(grad_gain_two, ("dp", "fsdp"), scatter_dimension=0, tiled=True),
    )
    query_cols = HEADS * HEAD_DIM
    return (
        block_out,
        grad_tokens,
        attn_own[:, :query_cols].astype(jnp.float32),
        attn_own[:, query_cols:].astype(jnp.float32),
        latent_own[:, :head_cols].astype(jnp.float32),
        latent_own[:, head_cols:].astype(jnp.float32),
        output_own.astype(jnp.float32),
        gains_own[0],
        gains_own[1],
        ffn_own[:, :ff_width].astype(jnp.float32),
        ffn_own[:, ff_width:].astype(jnp.float32),
        down_own.astype(jnp.float32),
    )


MESH = pl.DeviceIdType.MESH
F32 = jnp.float32
BF16 = jnp.bfloat16
SCALE = HEAD_DIM ** (-0.5)
ROWS = 256
WIDTH = 1024
HALF = 1408
PARTS = (768, 640)
FFN = 1 + 2 * len(PARTS)
PUT = 3
DOWN = 88


ROUTE = ("y21xs", "y21xs", "21xys", "21yxs")
SUM_X_FIRST = (True, True, True, True)


class Slots:
    def __init__(self):
        self.count = 0

    def take(self, number):
        first = self.count
        self.count += number
        return first


SLOTS = Slots()
S_A = [SLOTS.take(16) for _ in range(4)]
S_HALF = SLOTS.take(FFN)
S_F = [SLOTS.take(8) for _ in range(FFN)]
S_COT, S_TOK, S_DN2, S_OUT, S_END = (SLOTS.take(1) for _ in range(5))
S_R = [SLOTS.take(10) for _ in range(FFN + 4)]
S_SUM = SLOTS.take(5)


def nn(left, right):
    return jnp.dot(left, right, preferred_element_type=F32)


def nt(left, right):
    return lax.dot_general(left, right, (((1,), (1,)), ((), ())), preferred_element_type=F32)


def tn(left, right):
    return lax.dot_general(left, right, (((0,), (0,)), ((), ())), preferred_element_type=F32)


(
    AA, AG, AT, H_S, H_R, FA, FG, FT, COT_S, COT_R, TOK_S, TOK_R, END_S, END_R, DN2_S, DN2_R, OUT_S,
    OUT_R, R_GO, R_S, R_B, R_A, R_1, R_2, R_L, R_E, SUM_S, SUM_R,
) = range(28)
(
    G_START, G_WEIGHTS, G_ACROSS, G_DOWN_W, G_QUERY, G_OUTPUT_W, G_FFN_A, G_FFN_B, G_BACK, G_RESULT,
    G_TAIL, G_MASK, G_GAIN, G_NORM, G_LATENT, G_KEYS, G_NORM_P, G_LATENT_P, G_KEYS_P, G_COMPACT,
    G_ATTEND, G_QUERY_P, G_ATTEND_P, G_MIDDLE, G_NORM2, G_MIDDLE_P, G_NORM2_P, G_HIDDEN_A, G_DN_A,
    G_GATEUP_A, G_DN_B, G_DOWN, G_GATEUP_B, G_OUT, G_DMERGED, G_OUTPUT, G_ATTENDB, G_PROJQ, G_PROJL,
    G_DNORMED, G_NORM1B, G_HIDDEN_B, G_NORM2B, G_LATENTB,
) = range(44)
PLAN = {
    G_START: (
        (H_S, 1), (AA, 2, 0), (AG, 2, 0, 1), (FA, 0, 0), (AA, 0, 0), (AA, 1, 0), (FG, 0, 0, 0),
        (AG, 0, 0, 0), (FG, 0, 0, 2),
    ),
    (G_MASK, 3): (
        (AG, 2, 0, 2), (H_S, 2), (FG, 0, 0, 1), (TOK_S, 1), (AA, 0, 1), (TOK_S, 3), (H_S, 4),
    ),
    G_WEIGHTS: (
        (AG, 0, 0, 1), (AG, 0, 0, 2), (AG, 0, 1, 3), (AG, 1, 0, 3), (H_R, 2), (H_S, 3),
        (AG, 0, 0, 3), (AA, 3, 0), (AG, 3, 0, 1), (AG, 1, 0, 0), (FA, 0, 2), (FA, 0, 1),
        (FG, 0, 2, 2), (TOK_S, 2), (AG, 2, 0, 0), (FG, 0, 1, 2), (AA, 0, 2), (AG, 0, 1, 2),
        (AA, 0, 4), (H_R, 1), (AG, 0, 1, 1), (AG, 0, 2, 2), (AA, 2, 2), (AA, 3, 2), (H_R, 3),
        (AG, 3, 0, 2), (AG, 0, 4, 3), (AG, 1, 0, 1), (AA, 2, 4), (AA, 1, 1), (AA, 0, 8),
        (AG, 1, 1, 3), (FG, 0, 1, 1), (AA, 0, 5), (AG, 3, 0, 0), (AG, 2, 2, 2), (FA, 1, 0),
        (AA, 0, 3), (AG, 0, 3, 3), (FA, 2, 0), (AG, 1, 1, 1), (H_R, 4), (FG, 1, 0, 2), (AG, 3, 2, 2),
        (AG, 0, 3, 2), (AG, 0, 2, 3), (AG, 0, 5, 3), (TOK_S, 0), (AA, 0, 12), (AG, 2, 0, 3),
        (AA, 0, 6), (AA, 2, 6), (FG, 2, 0, 2), (AA, 2, 1), (AG, 2, 1, 3), (AG, 1, 0, 2), (FA, 0, 3),
        (AG, 2, 4, 3), (AG, 2, 1, 1), (AA, 1, 2), (AG, 0, 6, 3), (AA, 3, 1), (FA, 1, 4), (FA, 3, 0),
        (AG, 1, 1, 2), (FG, 0, 3, 2), (AA, 0, 7), (AG, 3, 1, 1), (FG, 3, 0, 2), (FA, 4, 0),
        (AG, 0, 7, 3), (AA, 3, 4), (AA, 2, 12), (AA, 1, 3), (AA, 0, 9), (FA, 0, 4), (FG, 2, 0, 0),
        (FA, 0, 6), (AA, 1, 4), (AG, 1, 2, 2), (AA, 0, 10), (AG, 2, 1, 2), (AA, 0, 11), (AA, 0, 13),
        (END_S,), (FA, 0, 5), (AA, 2, 3), (AG, 1, 3, 3), (AA, 0, 14), (AG, 3, 1, 2), (AG, 2, 2, 3),
        (AG, 1, 3, 2), (AA, 1, 8), (AA, 1, 5), (AG, 2, 3, 3), (FG, 2, 0, 1), (AG, 1, 4, 3),
        (AG, 2, 3, 2), (FG, 1, 0, 0), (FG, 4, 0, 2), (AA, 0, 15), (AA, 3, 6), (AG, 2, 6, 3),
        (AA, 2, 5), (TOK_R,), (AT, 0),
    ),
    (G_GAIN, 7): (
        (AA, 3, 5), (AG, 1, 2, 3),
    ),
    (G_NORM, 3): (
        (AA, 1, 6), (FA, 0, 7), (FG, 1, 0, 1), (AA, 2, 8), (FA, 2, 1), (AG, 1, 6, 3), (FG, 2, 1, 2),
    ),
    (G_LATENT, 1): (
        (AA, 1, 11), (AA, 2, 14), (AG, 2, 5, 3), (END_R,), (AG, 1, 5, 3), (FT, 0), (FA, 3, 4),
        (AA, 3, 3), (AA, 2, 7), (FG, 3, 0, 0), (AA, 1, 7), (AG, 1, 7, 3),
    ),
    (G_KEYS, 1): (
        (AG, 3, 3, 3), (AG, 3, 4, 3),
    ),
    G_ACROSS: (
        (AG, 3, 3, 2), (AG, 2, 7, 3),
    ),
    (G_NORM_P, 3): (
        (FA, 2, 2), (AA, 1, 14), (FG, 2, 1, 1), (FG, 2, 2, 2), (AG, 3, 1, 3), (AA, 1, 9),
    ),
    (G_LATENT_P, 1): (
        (AA, 1, 12),
    ),
    (G_KEYS_P, 1): (
        (AA, 3, 7), (AA, 2, 11), (FA, 1, 1), (AA, 1, 10), (AG, 3, 2, 3), (AA, 1, 15), (FG, 1, 1, 2),
        (AA, 1, 13), (FA, 2, 4), (AG, 3, 0, 3), (FG, 1, 1, 1), (AG, 3, 5, 3), (AG, 3, 7, 3),
    ),
    G_DOWN_W: (
        (FG, 4, 0, 0), (AG, 3, 6, 3), (AA, 2, 13),
    ),
    (G_COMPACT, 7): (
        (FA, 1, 2), (COT_S, 2), (AT, 1),
    ),
    G_QUERY: (
        (FG, 1, 2, 2), (FA, 2, 5), (FG, 3, 0, 1),
    ),
    (G_QUERY, 3): (
        (FA, 3, 1),
    ),
    (G_ATTEND, 3): (
        (FG, 3, 1, 2), (COT_S, 0),
    ),
    (G_ATTEND, 7): (
        (FG, 3, 1, 1), (FA, 2, 3), (FA, 4, 4), (AA, 2, 10), (COT_S, 3), (FG, 4, 0, 1), (FG, 2, 3, 2),
        (AA, 3, 13), (AA, 2, 15), (AA, 3, 14),
    ),
    (G_QUERY_P, 3): (
        (FA, 1, 3), (AA, 3, 15), (AA, 3, 9), (FG, 1, 3, 2),
    ),
    (G_ATTEND_P, 3): (
        (FA, 4, 1), (FA, 1, 6), (FA, 2, 6), (FG, 4, 1, 1), (AA, 3, 11), (FA, 3, 5), (AA, 3, 12),
        (AA, 3, 10), (FG, 4, 1, 2), (AA, 3, 8), (COT_S, 1), (AA, 2, 9),
    ),
    G_OUTPUT_W: (
        (AT, 3), (AT, 2),
    ),
    (G_MIDDLE, 3): (
        (FA, 3, 3), (FA, 1, 7), (FA, 2, 7), (FG, 3, 3, 2),
    ),
    (G_NORM2, 3): (
        (FA, 3, 2), (FA, 1, 5), (FG, 3, 2, 2),
    ),
    (G_MIDDLE_P, 3): (
        (FA, 4, 2),
    ),
    (G_NORM2_P, 3): (
        (FT, 2), (FT, 1), (FA, 4, 3), (FA, 4, 5),
    ),
    G_FFN_A: (
        (FG, 4, 3, 2),
    ),
    (G_HIDDEN_A, 0): (
        (FG, 4, 2, 2), (FA, 3, 7), (COT_R,),
    ),
    (G_HIDDEN_A, 1): (
        (FA, 3, 6),
    ),
    (G_DN_A, 1): (
        (FA, 4, 7),
    ),
    (G_GATEUP_A, 1): (
        (FA, 4, 6), (R_GO, 1), (R_GO, 2),
    ),
    G_FFN_B: (
        (FT, 4), (FT, 3), (R_S, 1, 1), (R_B, 1, 3),
    ),
    (G_DN_B, 1): (
        (R_S, 2, 1), (DN2_S,), (R_B, 1, 1), (R_S, 1, 0), (R_B, 2, 3),
    ),
    (G_DN_B, 0): (
        (R_A, 1, 3),
    ),
    (G_DOWN, 0): (
        (R_GO, 0), (R_B, 1, 2),
    ),
    (G_DOWN, 1): (
        (R_A, 1, 1), (R_S, 2, 0), (R_S, 0, 1), (R_B, 0, 3),
    ),
    (G_GATEUP_B, 1): (
        (R_A, 2, 3), (R_GO, 4), (R_B, 2, 1),
    ),
    (G_GATEUP_B, 3): (
        (R_A, 1, 2), (R_GO, 3), (R_B, 2, 2), (R_S, 0, 0), (R_1, 1, 1),
    ),
    (G_OUT, 0): (
        (R_S, 4, 1), (OUT_S, 0), (OUT_S, 2),
    ),
    (G_OUT, 1): (
        (R_B, 4, 3), (R_S, 4, 0), (OUT_S, 3), (R_A, 0, 3), (R_S, 3, 0),
    ),
    G_BACK: (
        (DN2_R,), (R_S, 3, 1),
    ),
    (G_DMERGED, 3): (
        (R_B, 3, 3), (R_A, 2, 1),
    ),
    (G_OUTPUT, 3): (
        (R_B, 4, 1), (R_A, 2, 2), (R_B, 4, 0), (R_B, 3, 1), (R_GO, 5), (R_1, 2, 1), (R_B, 4, 2),
    ),
    (G_ATTENDB, 3): (
        (R_S, 5, 1), (R_B, 5, 3), (R_B, 0, 2), (R_B, 1, 0), (R_A, 3, 3), (R_A, 4, 3),
    ),
    (G_ATTENDB, 7): (
        (R_B, 0, 1),
    ),
    (G_PROJQ, 1): (
        (R_A, 4, 1), (R_B, 5, 1), (R_S, 5, 0), (R_B, 5, 2),
    ),
    (G_PROJQ, 3): (
        (R_GO, 6), (R_A, 5, 3),
    ),
    (G_PROJL, 3): (
        (R_B, 3, 0), (R_S, 6, 1),
    ),
    (G_DNORMED, 3): (
        (R_A, 4, 2), (R_GO, 7), (R_1, 4, 1), (R_B, 6, 3),
    ),
    (G_NORM1B, 7): (
        (R_GO, 8), (R_A, 5, 1), (R_S, 8, 1), (SUM_S, 0), (R_A, 4, 0), (R_B, 3, 2), (R_S, 7, 1),
        (R_A, 0, 2), (R_B, 5, 0), (R_A, 5, 2), (R_1, 5, 1), (R_1, 0, 1), (R_B, 2, 0), (R_B, 6, 2),
        (R_B, 6, 1), (R_B, 7, 3), (R_S, 6, 0), (R_B, 7, 0), (SUM_R, 0), (R_1, 4, 0), (SUM_S, 1),
        (R_A, 3, 1), (R_A, 6, 3), (R_A, 5, 0), (R_A, 6, 1), (R_1, 5, 0), (R_B, 7, 2), (R_B, 0, 0),
        (R_A, 3, 2), (R_A, 6, 2),
    ),
    G_RESULT: (
        (R_B, 8, 3), (R_B, 7, 1), (R_S, 8, 0), (R_2, 4), (R_2, 5), (SUM_R, 1), (R_A, 3, 0), (SUM_S, 2),
        (R_1, 3, 1), (R_A, 1, 0), (R_A, 8, 3), (R_B, 6, 0), (R_B, 8, 2), (R_S, 7, 0), (R_1, 6, 1),
        (R_A, 7, 0), (R_A, 2, 0), (R_A, 7, 2), (R_1, 2, 0), (R_1, 1, 0), (R_L, 5), (R_A, 7, 3),
        (SUM_R, 2), (R_A, 7, 1), (R_B, 8, 1), (R_1, 3, 0), (R_L, 4), (R_A, 6, 0), (R_2, 2),
        (OUT_S, 1), (R_1, 7, 1), (R_A, 0, 0), (R_A, 8, 1), (R_1, 6, 0), (R_2, 1), (R_A, 8, 2),
        (R_2, 6), (R_B, 8, 0), (R_E, 4), (R_1, 8, 1), (R_L, 2), (SUM_S, 3), (R_2, 3), (R_1, 7, 0),
        (R_2, 7), (R_L, 6), (R_A, 0, 1), (R_A, 8, 0), (R_L, 3), (R_1, 8, 0), (SUM_R, 3), (R_L, 7),
        (R_E, 5), (OUT_R,), (SUM_S, 4),
    ),
    (G_RESULT, 7): (
        (R_2, 8), (R_L, 8), (R_L, 1), (R_E, 1), (R_E, 8), (R_E, 3), (R_1, 0, 0), (R_E, 2),
    ),
    G_TAIL: (
        (R_2, 0), (R_E, 6), (R_E, 7), (SUM_R, 4), (R_L, 0),
    ),
}


def layer_kernel(
    tok_hbm, len_ref, cot_hbm, wq_hbm, wl_hbm, wk_hbm, wv_hbm, wo_hbm, gain_one, gain_two, wg_hbm, wu_hbm, wd_ref,
    out_hbm, gtok_hbm, at_hbm, gain_hbm, gg_hbm, gu_hbm, gd_hbm,
    attn, latw, gate_a, up_a, gate_b, up_b, down_w, down_c, gain_full,
    tok, ends, bias, normed, query, latent, keys, values, merged, lse, middle, normed2, dout,
    mixed, dgate, dup, tmp, rcv_dn2, snd_out, rcv_out,
    dmid, dmid_low, dmerged, dquery, dkeys, dvalues, dlatent,
    pattn,
    s_d, s_ga, s_ua, s_gb, s_ub,
    y_d, y_ga, y_ua, y_gb, y_ub,
    z_d, z_ga, z_ua, z_gb, z_ub,
    x_ga, x_ua, x_gb, x_ub,
    s_a, x_a, z_a, y_a, sum_own, sum_rcv,
    send_sem, recv_sem, local_sem,
):
    snd_dn2 = dquery
    dp = lax.axis_index("dp")
    fs = lax.axis_index("fsdp")
    x, c, z, y = lax.div(dp, 2), lax.rem(dp, 2), lax.div(fs, 2), lax.rem(fs, 2)
    zh, zl = lax.div(z, 2), lax.rem(z, 2)
    sib = (x * 2 + 1 - c, fs)
    xp = ((1 - x) * 2 + c, fs)
    yp = (dp, z * 2 + 1 - y)
    z1 = (dp, (zh * 2 + 1 - zl) * 2 + y)
    z2 = (dp, ((1 - zh) * 2 + zl) * 2 + y)

    def rel(v, other):
        return 1 - v if other else v

    def line(dh, dl):
        return rel(zh, dh) * 2 + rel(zl, dl)

    sent, groups = {}, []

    def copy(src, dst, slot, target, group):
        if group not in groups:
            groups.append(group)
        return pltpu.make_async_remote_copy(
            src_ref=src, dst_ref=dst, send_sem=send_sem.at[groups.index(group)], recv_sem=recv_sem.at[slot],
            device_id=target, device_id_type=MESH,
        )

    def send(group, src, dst, slot, target):
        copy(src, dst, slot, target, group).start()
        sent[group] = sent.get(group, 0) + math.prod(src.shape) * src.dtype.itemsize

    def drain(group):
        tiles = sent.pop(group, 0) // 4096
        if tiles:
            wide = next(n for n in range(8, 0, -1) if tiles % n == 0 and tiles // n <= 128)
            size = tmp.at[pl.ds(0, tiles // wide * 8), pl.ds(0, wide * 128)]
            copy(size, size, 0, sib, group).wait_send()

    def arrive(dst, slot):
        copy(dst, dst, slot, sib, "sum").wait_recv()

    def local(src, dst, k):
        return pltpu.make_async_copy(src, dst, local_sem.at[k])

    def put(src, dst, k):
        local(src, dst, k).start()

    def add(dst, src):
        dst[...] = dst[...] + src[...]

    def cols(n, width=256):
        return pl.ds(pl.multiple_of(n * width, width), width)

    ops = {}

    def op(code):
        def enter(fn):
            ops[code] = fn
            return fn

        return enter

    def run(items):
        for name, *rest in items:
            ops[name](*rest)

    def gap(name):
        run(PLAN.get(name, ()))

    def loop(count, *stages, at=(), unroll=1):
        ends = [*at, count]
        for first, last in zip([0, *at], ends):

            def step(k, carry):
                for _, body in stages:
                    body(k)
                return carry

            if last - first == 1:
                for name, body in stages:
                    body(first)
                    gap((name, first))
            else:
                lax.fori_loop(first, last, step, 0, unroll=unroll)
                gap((stages[-1][0], last - 1))

    ways = {"y": yp, "x": xp, "1": z1, "2": z2, "s": sib}

    def a_blk(w, bits):
        route = ROUTE[w]
        across = {way: bits >> k & 1 for k, way in enumerate(route)}
        xx, cc, yy = rel(x, across["x"]), rel(c, across["s"]), rel(y, across["y"])
        zz = line(across["2"], across["1"])
        if w == 0:
            return latw.at[xx, cc, zz, yy]
        if w == 1:
            return attn.at[0, xx, cc, zz, yy]
        return attn.at[1, xx, cc, zz, yy, :, pl.ds(512 * (w - 2), 512)]

    def a_send(w, bits, k):
        blk = a_blk(w, bits)
        send("a%d" % w, blk, blk, S_A[w] + (bits + (1 << k) if k < 4 else 0), ways[ROUTE[w][k]])

    @op(AA)
    def aa(w, bits):
        if bits:
            arrive(a_blk(w, bits), S_A[w] + bits)
        a_send(w, bits, 4)

    @op(AG)
    def ag(w, bits, k):
        a_send(w, bits, k)

    @op(AT)
    def at(w):
        other = 1 - c
        half = pl.ds(512 * (w - 2), 512)
        arrive((latw.at[:, other], attn.at[0, :, other], attn.at[1, :, other, :, :, :, half])[min(w, 2)], S_A[w])

    ffn = (down_w, gate_a, up_a, gate_b, up_b)
    ffn_hbm = (None, wg_hbm, wu_hbm, wg_hbm, wu_hbm)
    starts = (None, 0, 0, 768, 768)

    def half_cols(xx, t):
        return pl.ds(pl.multiple_of(xx * HALF + starts[t], 128), ffn[t].shape[-1])

    @op(H_S)
    def h_s(t):
        send("half", ffn_hbm[t].at[:, half_cols(1 - x, t)], ffn[t].at[c, z, y, x], S_HALF + t, xp)

    @op(H_R)
    def h_r(t):
        arrive(ffn[t].at[c, z, y, 1 - x], S_HALF + t)

    def f_blk(t, bits):
        return ffn[t].at[rel(c, bits >> 3 & 1), line(bits & 1, bits >> 1 & 1), rel(y, bits >> 2 & 1)]

    def f_send(t, bits, k):
        blk = f_blk(t, bits)
        send("ffn%d" % t, blk, blk, S_F[t] + (bits + (1 << k) if k < 3 else 0), (z2, z1, yp, sib)[k])

    @op(FA)
    def fa(t, bits):
        if bits:
            arrive(f_blk(t, bits), S_F[t] + bits)
        f_send(t, bits, 3)

    @op(FG)
    def fg(t, bits, k):
        f_send(t, bits, k)

    @op(FT)
    def ft(t):
        arrive(ffn[t].at[1 - c], S_F[t])

    def quarter(ref, k):
        return ref.at[pl.ds(k * 64, 64)]

    @op(COT_S)
    def cot_s(k):
        send("cot", quarter(dout.at[x], k), quarter(dout.at[x], k), S_COT, xp)

    @op(COT_R)
    def cot_r():
        arrive(dout.at[1 - x], S_COT)

    @op(TOK_S)
    def tok_s(k):
        send("tok", quarter(tok.at[x], k), quarter(tok.at[x], k), S_TOK, xp)

    @op(TOK_R)
    def tok_r():
        arrive(tok.at[1 - x], S_TOK)

    @op(END_S)
    def end_s():
        send("tok", ends.at[x], ends.at[x], S_END, xp)

    @op(END_R)
    def end_r():
        arrive(ends.at[1 - x], S_END)

    @op(DN2_S)
    def dn2_s():
        send("dn2", snd_dn2, rcv_dn2, S_DN2, xp)

    @op(DN2_R)
    def dn2_r():
        arrive(rcv_dn2, S_DN2)

    @op(OUT_S)
    def out_s(k):
        send("out", quarter(snd_out, k), quarter(rcv_out, k), S_OUT, xp)

    @op(OUT_R)
    def out_r():
        arrive(rcv_out, S_OUT)

    ffn_s = (s_d, s_ga, s_ua, s_gb, s_ub)
    ffn_y = (y_d, y_ga, y_ua, y_gb, y_ub)
    ffn_zb = (z_d, z_ga, z_ua, z_gb, z_ub)
    ffn_x = (None, x_ga, x_ua, x_gb, x_ub)
    out_cols = (None, *[pl.ds(starts[t], ffn[t].shape[-1]) for t in range(1, FFN)])
    ffn_out = (None, *[gg_hbm, gu_hbm] * 2)

    def pick(i):
        return ((0, pl.ds(0, WIDTH)), (1, pl.ds(0, WIDTH)), (2, pl.ds(0, 512)), (2, pl.ds(512, 512)))[i - FFN]

    def sib_part(i, other):
        if i < FFN:
            yy = rel(y, other)
            return yy, ffn[i].at[1 - c, :, yy], ffn_s[i].at[yy], lambda zz: (ffn[i].at[c, zz, yy], ffn_s[i].at[yy, zz])
        k, cl = pick(i)
        if SUM_X_FIRST[i - FFN]:
            xx = rel(x, other)
            return (
                xx,
                pattn.at[k, xx, 1 - c, :, :, :, cl],
                s_a.at[k, xx, :, :, :, cl],
                lambda zz: (pattn.at[k, xx, c, zz, :, :, cl], s_a.at[k, xx, zz, :, :, cl]),
            )
        yy = rel(y, other)
        return (
            yy,
            pattn.at[k, :, 1 - c, :, yy, :, cl],
            s_a.at[k, :, :, yy, :, cl],
            lambda zz: (pattn.at[k, :, c, zz, yy, :, cl], s_a.at[k, :, zz, yy, :, cl]),
        )

    def first_hop(i, d):
        if i < FFN:
            return yp, ffn[i].at[c, d, 1 - y], ffn_y[i].at[d]
        k, cl = pick(i)
        if SUM_X_FIRST[i - FFN]:
            return xp, pattn.at[k, 1 - x, c, d, :, :, cl], x_a.at[k, d, :, :, cl]
        return yp, pattn.at[k, :, c, d, 1 - y, :, cl], x_a.at[k, d, :, :, cl]

    def line_blk(i, d):
        if i < FFN:
            return ffn[i].at[c, d, y]
        k, cl = pick(i)
        if SUM_X_FIRST[i - FFN]:
            return pattn.at[k, x, c, d, :, :, cl]
        return pattn.at[k, :, c, d, y, :, cl]

    def line_buf(i, b):
        if i < FFN:
            return ffn_zb[i].at[b]
        k, cl = pick(i)
        return z_a.at[k, b, :, :, cl]

    def last_hop(i):
        if i < FFN:
            return xp, ffn[i].at[c, z, y, 1 - x], ffn_x[i]
        k, cl = pick(i)
        if SUM_X_FIRST[i - FFN]:
            return yp, pattn.at[k, x, c, z, 1 - y, :, cl], y_a.at[k, :, cl]
        return xp, pattn.at[k, 1 - x, c, z, y, :, cl], y_a.at[k, :, cl]

    @op(R_GO)
    def r_go(i):
        for other in (1, 0):
            k, src, dst, _ = sib_part(i, other)
            send("r%d" % i, src, dst, S_R[i] + k, sib)

    @op(R_S)
    def r_s(i, other):
        k, _, dst, pairs = sib_part(i, other)
        arrive(dst, S_R[i] + k)
        if not other:
            for zz in range(4):
                add(*pairs(zz))

    @op(R_B)
    def r_b(i, bits):
        d = line(bits >> 1, bits & 1)
        add(*sib_part(i, 1)[3](d))
        target, src, buf = first_hop(i, d)
        send("r%d" % i, src, buf, S_R[i] + 2 + bits, target)

    @op(R_A)
    def r_a(i, bits):
        d = line(bits >> 1, bits & 1)
        _, _, buf = first_hop(i, d)
        arrive(buf, S_R[i] + 2 + bits)
        add(line_blk(i, d), buf)
        if bits & 1:
            send("r%d" % i, line_blk(i, d), line_buf(i, bits >> 1), S_R[i] + 6 + (bits >> 1), z1)

    @op(R_1)
    def r_1(i, dh):
        d = line(dh, 0)
        arrive(line_buf(i, dh), S_R[i] + 6 + dh)
        add(line_blk(i, d), line_buf(i, dh))
        if dh:
            send("r%d" % i, line_blk(i, d), line_buf(i, 2), S_R[i] + 8, z2)

    @op(R_2)
    def r_2(i):
        arrive(line_buf(i, 2), S_R[i] + 8)
        add(line_blk(i, z), line_buf(i, 2))

    @op(R_L)
    def r_l(i):
        if i == 0:
            put(down_w.at[c, z, y], gd_hbm, PUT)
            return
        target, src, buf = last_hop(i)
        send("r%d" % i, src, buf, S_R[i] + 9, target)
        if i < FFN:
            put(ffn[i].at[c, z, y, x], ffn_out[i].at[x, :, out_cols[i]], PUT + i * 2)

    @op(R_E)
    def r_e(i):
        _, _, buf = last_hop(i)
        arrive(buf, S_R[i] + 9)
        if i < FFN:
            put(buf, ffn_out[i].at[1 - x, :, out_cols[i]], PUT + 1 + i * 2)
        else:
            k, cl = pick(i)
            blk = pattn.at[k, x, c, z, y, :, cl]
            add(blk, buf)
            put(blk, at_hbm.at[k, :, cl], PUT + 4 + FFN + i)

    def wait_out():
        local(down_w.at[c, z, y], gd_hbm, PUT).wait()
        for i in range(1, FFN):
            local(ffn[i].at[c, z, y, x], ffn_out[i].at[x, :, out_cols[i]], PUT + i * 2).wait()
            local(ffn_x[i], ffn_out[i].at[1 - x, :, out_cols[i]], PUT + 1 + i * 2).wait()
        for i in range(FFN, FFN + 4):
            k, cl = pick(i)
            local(pattn.at[k, x, c, z, y, :, cl], at_hbm.at[k, :, cl], PUT + 4 + FFN + i).wait()

    sum_to = (sib, yp, xp, z1, z2)

    @op(SUM_S)
    def sum_s(i):
        copy(sum_own, sum_rcv.at[i], S_SUM + i, sum_to[i], "sum").start()

    @op(SUM_R)
    def sum_r(i):
        copy(sum_own, sum_rcv.at[i], S_SUM + i, sum_to[i], "sum").wait_send()
        arrive(sum_rcv.at[i], S_SUM + i)
        add(sum_own, sum_rcv.at[i])

    loads = [
        (wq_hbm, attn.at[0, x, c, z, y]),
        (wl_hbm, latw.at[x, c, z, y, :, pl.ds(0, 512)]),
        (wk_hbm, latw.at[x, c, z, y, pl.ds(0, 16), pl.ds(512, 512)]),
        (wv_hbm, latw.at[x, c, z, y, pl.ds(16, 16), pl.ds(512, 512)]),
        (wo_hbm, attn.at[1, x, c, z, y]),
        (tok_hbm, tok.at[x]),
        (cot_hbm, dout.at[x]),
        *[(ffn_hbm[t].at[:, half_cols(x, t)], ffn[t].at[c, z, y, x]) for t in range(1, FFN)],
    ]
    loads = [local(src, dst, k) for k, (src, dst) in enumerate(loads)]
    for load in loads:
        load.start()
    bar = pltpu.get_barrier_semaphore()

    def hello(target):
        pl.semaphore_signal(bar, inc=1, device_id=target, device_id_type=MESH)

    for target in (sib, xp, yp, z1, z2):
        hello(target)

    def piled(rows):
        return jnp.concatenate([rows[:, 0:512], rows[:, 512:WIDTH]], axis=0).astype(BF16)

    def stage_own():
        down_w[c, z, y] = piled(wd_ref[...].astype(F32))
        lane = lax.broadcasted_iota(jnp.int32, (16, 128), 1)
        mine = lax.div(lane, 32) == lax.rem(fs, 4)
        two = [ref[...].astype(F32).reshape(1, 32) for ref in (gain_one, gain_two)]
        two = jnp.concatenate([*two, jnp.zeros((14, 32), F32)], axis=0)
        two = jnp.where(mine, jnp.concatenate([two] * 4, axis=1), 0.0)
        latw[x, c, z, y, pl.ds(0, 16), pl.ds(WIDTH, 128)] = two.astype(BF16)
        latw[x, c, z, y, pl.ds(16, 16), pl.ds(WIDTH, 128)] = jnp.zeros((16, 128), BF16)

    e0 = len_ref[0]
    e1 = e0 + len_ref[1]
    e2 = e1 + len_ref[2]
    e3 = e2 + len_ref[3]

    def stage_ends():
        place = lax.broadcasted_iota(jnp.int32, (8, 128), 0)
        ends[x] = sum(jnp.where(place == k, e, 0) for k, e in enumerate((e0, e1, e2, e3))).astype(F32)

    stage_own()
    stage_ends()
    for load in loads[:5]:
        load.wait()
    pl.semaphore_wait(bar, 5)
    gap(G_START)

    for load in loads[5:]:
        load.wait()

    def mask_rows(k):
        rows = pl.ds(pl.multiple_of(k * 64, 64), 64)
        position = lax.broadcasted_iota(jnp.int32, (64, WIDTH), 0) + k * 64
        dout[x, rows] = jnp.where(position < e3, dout[x, rows].astype(F32), 0.0).astype(BF16)

    loop(4, (G_MASK, mask_rows))
    gap(G_WEIGHTS)

    def gain_rows(k):
        g = latw.at[lax.div(k, 4), lax.div(lax.rem(k, 4), 2)]
        part = g[pl.ds(lax.rem(k, 2) * 2, 2), :, 0:16, WIDTH : WIDTH + 128].astype(F32)
        gain_full[:, pl.ds(pl.multiple_of(k * 128, 128), 128)] = part[0, 0] + part[0, 1] + part[1, 0] + part[1, 1]

    loop(8, (G_GAIN, gain_rows))

    low_half = lax.broadcasted_iota(jnp.int32, (ROWS, 128), 1) < HEAD_DIM
    head_lane = lax.broadcasted_iota(jnp.int32, (ROWS, 128), 1)

    def halves(v):
        zero = jnp.zeros_like(v)
        return (jnp.where(low_half, v, zero), jnp.where(low_half, zero, v))

    def both(v):
        return jnp.concatenate(halves(v), axis=0)

    def scaled(v):
        return (v.astype(F32) * SCALE).astype(BF16)

    def up_weight(g, first):
        return latw[g, :, :, :, pl.ds(first, 16), pl.ds(512, 512)].reshape(256, 512)

    def segment(m, shape, axis):
        position = lax.broadcasted_iota(jnp.int32, shape, axis).astype(F32)
        return sum((position >= ends[m, pl.ds(k, 1), pl.ds(0, 1)]).astype(F32) for k in range(4))

    def stage_masks(m):
        row = lax.broadcasted_iota(jnp.int32, (ROWS, ROWS), 0)
        col = lax.broadcasted_iota(jnp.int32, (ROWS, ROWS), 1)
        same = segment(m, (ROWS, 1), 0) == segment(m, (1, ROWS), 1)
        bias[m] = jnp.where(same & (col <= row), 0.0, -1e30)

    def attention(m, own, at, normed, query, latent, keys, values, merged, middle):
        at_norm, at_latent, at_keys, at_query, at_attend, at_middle, at_norm2 = at

        def norm_rows(k):
            rows = pl.ds(pl.multiple_of(k * 64, 64), 64)
            val = tok[m, rows].astype(F32)
            r1 = lax.rsqrt(jnp.mean(val * val, axis=1, keepdims=True) + EPSILON)
            normed[rows] = (val * r1 * gain_full[0:1, :]).astype(BF16)

        def latent_cols(n):
            w = latw[:, :, :, :, :, cols(n)].reshape(WIDTH, 256)
            latent[:, cols(n)] = nn(normed[...], w).astype(BF16)

        def key_cols(g):
            lat = latent[:, cols(g)]
            keys[:, cols(g, 512)] = nn(lat, up_weight(g, 0)).astype(BF16)
            values[:, cols(g, 512)] = nn(lat, up_weight(g, 16)).astype(BF16)

        def query_cols(n):
            w = attn[0, :, :, :, :, :, cols(n)].reshape(WIDTH, 256)
            query[:, cols(n)] = nn(normed[...], w).astype(BF16)

        def attend(j):
            pair = cols(j, 128)
            s = nt(both(scaled(query[:, pair])), keys[:, pair]) + jnp.concatenate([bias[m]] * 2, axis=0)
            peak = jnp.max(s, axis=1, keepdims=True)
            expo = jnp.exp(s - peak)
            total = jnp.sum(expo, axis=1, keepdims=True)
            res = nn((expo / total).astype(BF16), values[:, pair])
            merged[:, pair] = jnp.where(low_half, res[0:ROWS], res[ROWS : 2 * ROWS]).astype(BF16)
            if own:
                logsum = peak + jnp.log(total)
                lse[...] = jnp.where(
                    head_lane == j * 2,
                    logsum[0:ROWS],
                    jnp.where(head_lane == j * 2 + 1, logsum[ROWS : 2 * ROWS], lse[...]),
                )

        def middle_cols(n):
            w = attn[1, :, :, :, :, :, cols(n)].reshape(WIDTH, 256)
            middle[:, cols(n)] = tok[m, :, cols(n)].astype(F32) + nn(merged[...], w)

        def norm2_rows(k):
            rows = pl.ds(pl.multiple_of(k * 64, 64), 64)
            val = middle[rows]
            r2 = lax.rsqrt(jnp.mean(val * val, axis=1, keepdims=True) + EPSILON)
            normed2[m, rows] = (val * r2 * gain_full[1:2, :]).astype(BF16)

        def first():
            stage_masks(m)
            loop(4, (at_norm, norm_rows))
            loop(2, (at_latent, latent_cols), unroll=2)
            loop(GROUPS, (at_keys, key_cols), unroll=2)

        def second():
            loop(4, (at_query, query_cols), unroll=2)
            loop(8, (at_attend, attend), at=(4,), unroll=4)

        def third():
            loop(4, (at_middle, middle_cols), unroll=2)
            loop(4, (at_norm2, norm2_rows))

        return first, second, third

    def compact(k):
        pair = down_w.at[lax.div(k, 4), lax.rem(k, 4)]
        one, two = pair[0].astype(F32), pair[1].astype(F32)
        rows = pl.ds(pl.multiple_of(k * 2 * DOWN, 16), 2 * DOWN)
        for half in range(2):
            part = slice(half * DOWN, (half + 1) * DOWN)
            down_c[rows, pl.ds(half * 512, 512)] = jnp.concatenate([one[part], two[part]], axis=0).astype(BF16)

    at = (G_NORM, G_LATENT, G_KEYS, G_QUERY, G_ATTEND, G_MIDDLE, G_NORM2)
    own = attention(x, True, at, normed, query, latent, keys, values, merged, middle)
    at = (G_NORM_P, G_LATENT_P, G_KEYS_P, G_QUERY_P, G_ATTEND_P, G_MIDDLE_P, G_NORM2_P)
    across = attention(1 - x, False, at, dmid_low, dquery, dlatent, dkeys, dvalues, dmerged, dmid)
    own[0]()
    gap(G_ACROSS)
    across[0]()
    gap(G_DOWN_W)
    loop(8, (G_COMPACT, compact))
    gap(G_QUERY)
    own[1]()
    across[1]()
    gap(G_OUTPUT_W)
    own[2]()
    across[2]()
    gap(G_FFN_A)

    def ffn_w(ref, half, sl=slice(None)):
        w = ref[:, :, :, half, :, sl]
        return w.reshape(512, w.shape[-1])

    def hidden(it, gate_w, up_w, base, widths):
        m = rel(x, it)
        rows = pl.ds(pl.multiple_of(m * ROWS, ROWS), ROWS)
        for first, width in widths:
            sl, at = pl.ds(first, width), pl.ds(base + first, width)
            n2 = normed2[m]
            gate = nn(n2[:, 0:512], ffn_w(gate_w, 0, sl)) + nn(n2[:, 512:1024], ffn_w(gate_w, 1, sl))
            upper = nn(n2[:, 0:512], ffn_w(up_w, 0, sl)) + nn(n2[:, 512:1024], ffn_w(up_w, 1, sl))
            dmix = nt(dout[m], down_c[at])
            sig = jax.nn.sigmoid(gate)
            silu = gate * sig
            mixed[rows, at] = (silu * upper).astype(BF16)
            dgate[rows, at] = (dmix * upper * sig * (1.0 + gate * (1.0 - sig))).astype(BF16)
            dup[rows, at] = (dmix * silu).astype(BF16)

    def dn_half(it, gate_w, up_w, at, more):
        m = rel(x, it)
        rows = pl.ds(pl.multiple_of(m * ROWS, ROWS), ROWS)
        for half in range(2):
            part = nt(dgate[rows, at], ffn_w(gate_w, half)) + nt(dup[rows, at], ffn_w(up_w, half))
            to = (pl.ds(ROWS * it, ROWS), pl.ds(half * 512, 512))
            if more:
                part = part + tmp[to]
            if more == 2 and it:
                snd_dn2[:, pl.ds(half * 512, 512)] = part.astype(BF16)
            else:
                tmp[to] = part

    def grad_gate_up(it, gate_w, up_w, at):
        cc = jnp.where(it < 2, 1 - c, c)
        half = lax.rem(it, 2)
        sl = pl.ds(pl.multiple_of(half * 512 + cc * 256, 256), 256)
        width = gate_w.shape[-1]
        for src, dst in ((dgate, gate_w), (dup, up_w)):
            g = nn(normed2[0, :, sl].T, src[pl.ds(0, ROWS), at]) + nn(normed2[1, :, sl].T, src[pl.ds(ROWS, ROWS), at])
            dst[cc, :, :, half] = g.astype(BF16).reshape(4, 2, 32, width)

    def grad_down(it):
        cc = rel(c, it == 0)
        wide = pl.ds(pl.multiple_of(cc * 640, 128), 768)
        mt = mixed[:, wide].T
        tmp[pl.ds(ROWS, 768)] = nn(mt[:, 0:256], dout[0]) + nn(mt[:, 256:512], dout[1])

        def split(k, carry):
            rows = tmp[pl.ds(pl.multiple_of(ROWS + cc * 64 + k * DOWN, 8), DOWN)]
            down_w[cc, lax.div(k, 2), lax.rem(k, 2)] = piled(rows)
            return carry

        lax.fori_loop(0, 8, split, 0)

    def hidden_a(it):
        hidden(it, gate_a, up_a, 0, ((0, 512), (512, 256)))

    def dn_a(it):
        dn_half(it, gate_a, up_a, pl.ds(0, 768), 0)

    def gateup_a(it):
        grad_gate_up(it, gate_a, up_a, pl.ds(0, 768))

    def hidden_b(it):
        hidden(it, gate_b, up_b, 768, ((0, 512), (512, 128)))

    def dn_b(it):
        dn_half(it, gate_b, up_b, pl.ds(768, 640), 2)

    def gateup_b(it):
        grad_gate_up(it, gate_b, up_b, pl.ds(768, 640))

    def out_half(it):
        m = rel(x, it == 0)
        rows = pl.ds(pl.multiple_of(m * ROWS, ROWS), ROWS)
        part = nn(mixed[rows], down_c[...])
        if it == 0:
            snd_out[...] = part.astype(BF16)
        else:
            tmp[pl.ds(ROWS, ROWS)] = part

    loop(2, (G_HIDDEN_A, hidden_a), at=(1,))
    loop(2, (G_DN_A, dn_a), at=(1,))
    drain("ffn1")
    drain("ffn2")
    loop(4, (G_GATEUP_A, gateup_a), at=(2,))
    gap(G_FFN_B)
    hidden_b(1)
    gap((G_HIDDEN_B, 1))
    dn_b(1)
    gap((G_DN_B, 1))
    hidden_b(0)
    gap((G_HIDDEN_B, 0))
    dn_b(0)
    gap((G_DN_B, 0))
    drain("ffn0")
    loop(2, (G_DOWN, grad_down), at=(1,))
    drain("ffn3")
    drain("ffn4")
    loop(4, (G_GATEUP_B, gateup_b), at=(2,))
    loop(2, (G_OUT, out_half), at=(1,))
    gap(G_BACK)

    sum_own[...] = jnp.zeros((8, WIDTH), F32)

    def back_two(k):
        rows = pl.ds(pl.multiple_of(k * 32, 32), 32)
        mid = middle[rows]
        r2 = lax.rsqrt(jnp.mean(mid * mid, axis=1, keepdims=True) + EPSILON)
        grad = tmp[rows] + rcv_dn2[rows].astype(F32)
        sum_own[1:2] = sum_own[1:2] + jnp.sum(grad * mid * r2, axis=0, keepdims=True)
        s = grad * gain_full[1:2, :]
        res = dout[x, rows].astype(F32) + r2 * (s - mid * r2 * r2 * jnp.mean(s * mid, axis=1, keepdims=True))
        dmid[rows] = res
        dmid_low[rows] = res.astype(BF16)

    loop(8, (G_NORM2B, back_two), unroll=2)

    def dmerged_cols(k):
        w = attn[1, lax.div(k, 2), lax.rem(k, 2)].reshape(256, WIDTH)
        dmerged[:, cols(k)] = nt(dmid_low[...], w).astype(BF16)

    loop(4, (G_DMERGED, dmerged_cols), unroll=2)

    def grad_output(it):
        cc = jnp.where(it < 2, 1 - c, c)
        half = lax.rem(it, 2)
        g = nn(merged[:, cols(half * 2 + cc)].T, dmid_low[...])
        pattn[0, half, cc] = g.astype(BF16).reshape(4, 2, 32, WIDTH)

    loop(4, (G_OUTPUT, grad_output), at=(2,), unroll=2)

    drain("dn2")

    def attend_back(j):
        pair = cols(j, 128)
        k_pair, v_pair = keys[:, pair], values[:, pair]
        q, do = both(scaled(query[:, pair])), both(dmerged[:, pair])
        logsum = jnp.concatenate(
            [jnp.sum(jnp.where(head_lane == j * 2 + h, lse[...], 0.0), axis=1, keepdims=True) for h in (0, 1)], axis=0
        )
        probs = jnp.exp(nt(q, k_pair) + jnp.concatenate([bias[x]] * 2, axis=0) - logsum)
        dprobs = nt(do, v_pair)
        dvalues[:, pair] = tn(probs.astype(BF16), do).astype(BF16)
        row_sum = jnp.sum(probs * dprobs, axis=1, keepdims=True)
        dscores = (probs * (dprobs - row_sum)).astype(BF16)
        dq = nn(dscores, k_pair)
        dkeys[:, pair] = tn(dscores, q).astype(BF16)
        dquery[:, pair] = (jnp.where(low_half, dq[0:ROWS], dq[ROWS : 2 * ROWS]) * SCALE).astype(BF16)

    loop(8, (G_ATTENDB, attend_back), at=(4,), unroll=2)

    def other_first(it):
        cc = jnp.where(it < 2, 1 - c, c)
        return lax.rem(it, 2), cc

    def grad_query(it):
        half, cc = other_first(it)
        g = nn(normed[:, cols(half * 2 + cc)].T, dquery[...])
        pattn[1, half, cc] = g.astype(BF16).reshape(4, 2, 32, WIDTH)

    loop(4, (G_PROJQ, grad_query), at=(2,), unroll=2)

    def latent_back(g):
        dk, dv = dkeys[:, cols(g, 512)], dvalues[:, cols(g, 512)]
        dlatent[:, cols(g)] = (nt(dk, up_weight(g, 0)) + nt(dv, up_weight(g, 16))).astype(BF16)
        lat = latent[:, cols(g)].T
        pattn[2, g, :, :, :, pl.ds(0, 16), pl.ds(512, 512)] = nn(lat, dk).astype(BF16).reshape(2, 4, 2, 16, 512)
        pattn[2, g, :, :, :, pl.ds(16, 16), pl.ds(512, 512)] = nn(lat, dv).astype(BF16).reshape(2, 4, 2, 16, 512)

    loop(GROUPS, (G_LATENTB, latent_back))

    def grad_latent(it):
        half, cc = other_first(it)
        g = nn(normed[:, cols(half * 2 + cc)].T, dlatent[...])
        pattn[2, half, cc, :, :, :, pl.ds(0, 512)] = g.astype(BF16).reshape(4, 2, 32, 512)

    loop(4, (G_PROJL, grad_latent), at=(2,), unroll=2)

    def dnormed_cols(k):
        xx, cc = lax.div(k, 2), lax.rem(k, 2)
        part = nt(dquery[...], attn[0, xx, cc].reshape(256, WIDTH))
        part = part + nt(dlatent[...], latw[xx, cc, :, :, :, pl.ds(0, 512)].reshape(256, 512))
        tmp[pl.ds(0, ROWS), cols(k)] = part

    loop(4, (G_DNORMED, dnormed_cols), unroll=2)

    def back_one(k):
        rows = pl.ds(pl.multiple_of(k * 32, 32), 32)
        val = tok[x, rows].astype(F32)
        r1 = lax.rsqrt(jnp.mean(val * val, axis=1, keepdims=True) + EPSILON)
        grad = tmp[rows]
        sum_own[0:1] = sum_own[0:1] + jnp.sum(grad * val * r1, axis=0, keepdims=True)
        s = grad * gain_full[0:1, :]
        dmid[rows] = dmid[rows] + r1 * (s - val * r1 * r1 * jnp.mean(s * val, axis=1, keepdims=True))

    loop(8, (G_NORM1B, back_one), unroll=2)
    to_gtok = local(dmid, gtok_hbm, 0)
    to_gtok.start()
    gap(G_RESULT)

    def out_rows(k):
        rows = pl.ds(pl.multiple_of(k * 32, 32), 32)
        part = tmp[pl.ds(pl.multiple_of(ROWS + k * 32, 32), 32)]
        tok[x, rows] = (middle[rows] + (part + rcv_out[rows].astype(F32))).astype(BF16)

    drain("tok")
    loop(8, (G_RESULT, out_rows))
    to_out = local(tok.at[x], out_hbm, 1)
    to_out.start()
    gap(G_TAIL)
    to_gain = local(sum_own.at[:, pl.ds(pl.multiple_of((dp * 2 + lax.div(fs, 4)) * 128, 128), 128)], gain_hbm, 2)
    to_gain.start()
    for group in list(sent):
        drain(group)
    to_gtok.wait()
    to_out.wait()
    to_gain.wait()
    wait_out()


def finish_kernel(*refs):
    given, outs, bufs, casts = refs[:7], refs[7:19], refs[19:26], refs[26:36]
    in_sem, out_sem = refs[36:]
    takes = [pltpu.make_async_copy(src, dst, in_sem.at[k]) for k, (src, dst) in enumerate(zip(given, bufs))]
    gives = [pltpu.make_async_copy(src, dst, out_sem.at[k]) for k, (src, dst) in enumerate(zip([*bufs[:2], *casts], outs))]
    for k in (1, 0, 4, 5, 6, 2, 3):
        takes[k].start()
    for k in (1, 0):
        takes[k].wait()
        gives[k].start()
    _, _, at_ref, gain_ref, gg_ref, gu_ref, gd_ref = bufs
    gq_o, gl_o, gk_o, gv_o, go_o, ga_o, gf_o, gg_o, gu_o, gd_o = casts
    for k, src, dst in ((4, gg_ref, gg_o), (5, gu_ref, gu_o)):
        takes[k].wait()
        dst[:, 0:HALF] = src[0].astype(F32)
        dst[:, HALF : 2 * HALF] = src[1].astype(F32)
        gives[k + 5].start()
    takes[6].wait()
    gd = gd_ref[...].astype(F32)
    gd_o[:, 0:512] = gd[0:DOWN]
    gd_o[:, 512:WIDTH] = gd[DOWN : 2 * DOWN]
    gives[11].start()
    takes[2].wait()
    go_o[...] = at_ref[0].astype(F32)
    gq_o[...] = at_ref[1].astype(F32)
    gl_o[...] = at_ref[2, :, 0:512].astype(F32)
    gk_o[...] = at_ref[2, 0:16, 512:1024].astype(F32)
    gv_o[...] = at_ref[2, 16:32, 512:1024].astype(F32)
    takes[3].wait()
    place = lax.rem(lax.axis_index("fsdp"), 4)
    picked = sum(jnp.where(place == k, gain_ref[:, 32 * k : 32 * k + 32], 0.0) for k in range(4))
    ga_o[...] = picked[0:1]
    gf_o[...] = picked[1:2]
    for k in range(2, 9):
        gives[k].start()
    for give in gives:
        give.wait()


def kernel_on_device(
    tokens, seq_lengths, cotangent, w_query, w_latent, w_keyup, w_valup, w_output, norm_attn, norm_ffn,
    w_gate, w_up, w_down,
):
    hbm, vmem = pl.BlockSpec(memory_space=pl.ANY), pl.BlockSpec(memory_space=pltpu.VMEM)
    smem = pl.BlockSpec(memory_space=pltpu.SMEM)
    shape = jax.ShapeDtypeStruct
    outs = [
        shape((ROWS, WIDTH), BF16), shape((ROWS, WIDTH), F32), shape((3, 32, WIDTH), BF16), shape((8, 128), F32),
        shape((2, 32, HALF), BF16), shape((2, 32, HALF), BF16), shape((2 * DOWN, 512), BF16),
    ]
    V = pltpu.VMEM
    units = [(2 * DOWN, 512), *[(2, 32, width) for width in PARTS for _ in range(2)]]
    act = V((ROWS, WIDTH), BF16)
    scratch = [
        V((2, 2, 2, 4, 2, 32, WIDTH), BF16), V((2, 2, 4, 2, 32, WIDTH + 128), BF16),
        *[V((2, 4, 2, *unit), BF16) for unit in units[1:]],
        V((2, 4, 2, 2 * DOWN, 512), BF16), V((HALF, WIDTH), BF16), V((16, WIDTH), F32),
        V((2, ROWS, WIDTH), BF16), V((2, 8, 128), F32), V((2, ROWS, ROWS), F32), act, act, V((ROWS, 512), BF16), act, act, act, V((ROWS, 128), F32),
        V((ROWS, WIDTH), F32), V((2, ROWS, WIDTH), BF16), V((2, ROWS, WIDTH), BF16),
        V((512, HALF), BF16), V((512, HALF), BF16), V((512, HALF), BF16), V((ROWS + 768, WIDTH), F32),
        act, act, act,
        V((ROWS, WIDTH), F32), act, act, act, act, act, V((ROWS, 512), BF16),
        V((3, 2, 2, 4, 2, 32, WIDTH), BF16),
        *[V((2, 4, *unit), BF16) for unit in units],
        *[V((4, *unit), BF16) for unit in units],
        *[V((3, *unit), BF16) for unit in units],
        *[V(unit[1:], BF16) for unit in units[1:]],
        V((3, 2, 4, 2, 32, WIDTH), BF16), V((3, 4, 2, 32, WIDTH), BF16),
        V((3, 3, 2, 32, WIDTH), BF16), V((3, 32, WIDTH), BF16), V((8, WIDTH), F32), V((5, 8, WIDTH), F32),
        pltpu.SemaphoreType.DMA((2 * FFN + 14,)), pltpu.SemaphoreType.DMA((SLOTS.count,)), pltpu.SemaphoreType.DMA((PUT + 8 + 2 * FFN,)),
    ]
    res = pl.pallas_call(
        layer_kernel,
        out_shape=outs,
        in_specs=[hbm, smem, hbm, hbm, hbm, hbm, hbm, hbm, vmem, vmem, hbm, hbm, vmem],
        out_specs=[hbm] * len(outs),
        scratch_shapes=scratch,
        compiler_params=pltpu.CompilerParams(
            collective_id=0, has_side_effects=True, vmem_limit_bytes=63 * 2**20
        ),
    )(
        tokens, seq_lengths, cotangent, w_query, w_latent, w_keyup, w_valup, w_output, norm_attn, norm_ffn,
        w_gate, w_up, w_down,
    )
    final = [
        shape((ROWS, WIDTH), BF16), shape((ROWS, WIDTH), F32), shape((32, WIDTH), F32), shape((32, 512), F32),
        shape((16, 512), F32), shape((16, 512), F32), shape((32, WIDTH), F32), shape((1, 32), F32), shape((1, 32), F32),
        shape((32, 2 * HALF), F32), shape((32, 2 * HALF), F32), shape((DOWN, WIDTH), F32),
    ]
    out = pl.pallas_call(
        finish_kernel,
        out_shape=final,
        in_specs=[hbm] * 7,
        out_specs=[hbm] * 12,
        scratch_shapes=[
            *[V(one.shape, one.dtype) for one in [*outs, *final[2:]]],
            pltpu.SemaphoreType.DMA((7,)), pltpu.SemaphoreType.DMA((12,)),
        ],
    )(*res)
    return tuple(out[:7]) + (out[7].reshape(32), out[8].reshape(32)) + tuple(out[9:])


def solution(mesh):
    fits = dict(mesh.shape) == {"dp": 4, "fsdp": 8}
    return jax.shard_map(
        kernel_on_device if fits else on_device,
        mesh=mesh,
        in_specs=(
            P(("dp", "fsdp"), None),
            P(("dp", "fsdp")),
            P(("dp", "fsdp"), None),
            P(("dp", "fsdp"), None),
            P(("dp", "fsdp"), None),
            P(("dp", "fsdp"), None),
            P(("dp", "fsdp"), None),
            P(("dp", "fsdp"), None),
            P(("dp", "fsdp")),
            P(("dp", "fsdp")),
            P(("dp", "fsdp"), None),
            P(("dp", "fsdp"), None),
            P(("dp", "fsdp"), None),
        ),
        out_specs=(
            P(("dp", "fsdp"), None),
            P(("dp", "fsdp"), None),
            P(("dp", "fsdp"), None),
            P(("dp", "fsdp"), None),
            P(("dp", "fsdp"), None),
            P(("dp", "fsdp"), None),
            P(("dp", "fsdp"), None),
            P(("dp", "fsdp")),
            P(("dp", "fsdp")),
            P(("dp", "fsdp"), None),
            P(("dp", "fsdp"), None),
            P(("dp", "fsdp"), None),
        ),
        check_vma=False,
    )
```

```python
import math

import jax
import jax.numpy as jnp
from jax import lax
from jax.experimental import pallas as pl
from jax.experimental.pallas import tpu as pltpu
from jax.sharding import PartitionSpec as P

HEADS = 16
HEAD_DIM = 64
GROUPS = 2
LATENT = 256


EPSILON = 1e-06


def matmul(left, right):
    return jnp.dot(left, right, preferred_element_type=jnp.float32)


def matmul_left(left, right):
    return lax.dot_general(
        left, right, (((0,), (0,)), ((), ())), preferred_element_type=jnp.float32
    )


def matmul_right(left, right):
    return lax.dot_general(
        left, right, (((1,), (1,)), ((), ())), preferred_element_type=jnp.float32
    )


def segment_mask(lengths, rows):
    position = jnp.arange(rows, dtype=jnp.int32)
    ends = jnp.cumsum(lengths)
    segment = jnp.sum((position[None, :] >= ends[:, None]).astype(jnp.int32), axis=0)
    allowed = (segment[:, None] == segment[None, :]) & (position[None, :] <= position[:, None])
    valid = (position < ends[-1]).astype(jnp.float32)
    return (allowed, valid)


def head_forward(allowed, scale):

    def one_head(operands):
        query, key_rows, value_rows = operands
        scores = jnp.where(allowed, matmul_right(query, key_rows) * scale, -1e30)
        peak = jnp.max(scores, axis=1, keepdims=True)
        expo = jnp.exp(scores - peak)
        total = jnp.sum(expo, axis=1, keepdims=True)
        weights = (expo / total).astype(jnp.bfloat16)
        result = matmul(weights, value_rows).astype(jnp.bfloat16)
        return (result, peak[:, 0] + jnp.log(total[:, 0]))

    return one_head


def head_backward(allowed, scale):

    def one_head(operands):
        query, key_rows, value_rows, grad_out, logsum = operands
        scores = jnp.where(allowed, matmul_right(query, key_rows) * scale, -1e30)
        probs = jnp.exp(scores - logsum[:, None])
        grad_value = matmul_left(probs.astype(jnp.bfloat16), grad_out)
        grad_probs = matmul_right(grad_out, value_rows)
        inner = jnp.sum(probs * grad_probs, axis=1, keepdims=True)
        grad_scores = (probs * (grad_probs - inner)).astype(jnp.bfloat16)
        grad_query = matmul(grad_scores, key_rows) * scale
        grad_key = matmul_left(grad_scores, query) * scale
        return (grad_query, grad_key, grad_value)

    return one_head


def norm_back(grad_normed, inputs, rstd, gain):
    scaled = grad_normed * gain
    grad_in = rstd * (
        scaled - inputs * rstd * rstd * jnp.mean(scaled * inputs, axis=1, keepdims=True)
    )
    grad_gain = jnp.sum(grad_normed * inputs * rstd, axis=0)
    return (grad_in, grad_gain)


def column_term(left, right):
    return matmul_left(left, right).astype(jnp.bfloat16)


def forward(tokens, allowed, attn_w, ffn_w):
    w_query, w_latent, w_keyup, w_valup, w_output, gain_one = attn_w
    gain_two, w_gate, w_up, w_down = ffn_w
    rows = tokens.shape[0]
    inputs = tokens.astype(jnp.float32)
    rstd_one = lax.rsqrt(jnp.mean(inputs * inputs, axis=1, keepdims=True) + EPSILON)
    normed = (inputs * rstd_one * gain_one.astype(jnp.float32)).astype(jnp.bfloat16)
    query = matmul(normed, w_query).astype(jnp.bfloat16)
    latent = matmul(normed, w_latent).astype(jnp.bfloat16)
    lat3 = latent.reshape(rows, GROUPS, LATENT)
    keys = jnp.einsum(
        "tgl,glf->tgf",
        lat3,
        w_keyup.reshape(GROUPS, LATENT, -1),
        preferred_element_type=jnp.float32,
    ).astype(jnp.bfloat16)
    values = jnp.einsum(
        "tgl,glf->tgf",
        lat3,
        w_valup.reshape(GROUPS, LATENT, -1),
        preferred_element_type=jnp.float32,
    ).astype(jnp.bfloat16)
    heads_query = query.reshape(rows, HEADS, HEAD_DIM).transpose(1, 0, 2)
    heads_key = keys.reshape(rows, HEADS, HEAD_DIM).transpose(1, 0, 2)
    heads_value = values.reshape(rows, HEADS, HEAD_DIM).transpose(1, 0, 2)
    attended, logsum = lax.map(
        head_forward(allowed, HEAD_DIM ** (-0.5)), (heads_query, heads_key, heads_value)
    )
    merged = attended.transpose(1, 0, 2).reshape(rows, HEADS * HEAD_DIM)
    middle = inputs + matmul(merged, w_output)
    rstd_two = lax.rsqrt(jnp.mean(middle * middle, axis=1, keepdims=True) + EPSILON)
    normed_two = (middle * rstd_two * gain_two.astype(jnp.float32)).astype(jnp.bfloat16)
    gate = matmul(normed_two, w_gate)
    upper = matmul(normed_two, w_up)
    mixed = (jax.nn.silu(gate) * upper).astype(jnp.bfloat16)
    result = middle + matmul(mixed, w_down)
    return (
        result,
        inputs,
        rstd_one,
        normed,
        lat3,
        heads_query,
        heads_key,
        heads_value,
        logsum,
        merged,
        middle,
        rstd_two,
        normed_two,
        gate,
        upper,
        mixed,
    )


def on_device(
    tokens,
    seq_lengths,
    cotangent,
    w_query,
    w_latent,
    w_keyup,
    w_valup,
    w_output,
    norm_attn,
    norm_ffn,
    w_gate,
    w_up,
    w_down,
):
    rows = tokens.shape[0]
    allowed, valid = segment_mask(seq_lengths, rows)
    attn_w = (
        lax.all_gather(w_query, ("dp", "fsdp"), axis=0, tiled=True),
        lax.all_gather(w_latent, ("dp", "fsdp"), axis=0, tiled=True),
        lax.all_gather(w_keyup, ("dp", "fsdp"), axis=0, tiled=True),
        lax.all_gather(w_valup, ("dp", "fsdp"), axis=0, tiled=True),
        lax.all_gather(w_output, ("dp", "fsdp"), axis=0, tiled=True),
        lax.all_gather(norm_attn, ("dp", "fsdp"), axis=0, tiled=True),
    )
    ffn_w = (
        lax.all_gather(norm_ffn, ("dp", "fsdp"), axis=0, tiled=True),
        lax.all_gather(w_gate, ("dp", "fsdp"), axis=0, tiled=True),
        lax.all_gather(w_up, ("dp", "fsdp"), axis=0, tiled=True),
        lax.all_gather(w_down, ("dp", "fsdp"), axis=0, tiled=True),
    )
    saved = forward(tokens, allowed, attn_w, ffn_w)
    block_out = saved[0].astype(jnp.bfloat16)
    (
        result,
        inputs,
        rstd_one,
        normed,
        lat3,
        heads_query,
        heads_key,
        heads_value,
        logsum,
        merged,
        middle,
        rstd_two,
        normed_two,
        gate,
        upper,
        mixed,
    ) = saved
    full_query, full_latent, full_keyup, full_valup, full_output, gain_one = attn_w
    gain_two, full_gate, full_up, full_down = ffn_w
    ff_width = full_gate.shape[1]
    grad_out = cotangent.astype(jnp.float32) * valid[:, None]
    grad_low = grad_out.astype(jnp.bfloat16)
    grad_mixed = matmul_right(grad_low, full_down)
    sigmoid_gate = jax.nn.sigmoid(gate)
    grad_gate_low = (
        grad_mixed * upper * sigmoid_gate * (1.0 + gate * (1.0 - sigmoid_gate))
    ).astype(jnp.bfloat16)
    grad_upper_low = (grad_mixed * jax.nn.silu(gate)).astype(jnp.bfloat16)
    grad_normed_two = matmul_right(grad_gate_low, full_gate) + matmul_right(grad_upper_low, full_up)
    grad_mid_norm, grad_gain_two = norm_back(
        grad_normed_two, middle, rstd_two, gain_two.astype(jnp.float32)
    )
    grad_middle = grad_out + grad_mid_norm
    down_own = lax.psum_scatter(
        column_term(mixed, grad_low), ("dp", "fsdp"), scatter_dimension=0, tiled=True
    )
    packed_ffn = jnp.concatenate([grad_gate_low, grad_upper_low], axis=1)
    ffn_own = lax.psum_scatter(
        column_term(normed_two, packed_ffn), ("dp", "fsdp"), scatter_dimension=0, tiled=True
    )
    grad_branch = grad_middle.astype(jnp.bfloat16)
    grad_merged = matmul_right(grad_branch, full_output).astype(jnp.bfloat16)
    output_own = lax.psum_scatter(
        column_term(merged, grad_branch), ("dp", "fsdp"), scatter_dimension=0, tiled=True
    )
    heads_grad = grad_merged.reshape(rows, HEADS, HEAD_DIM).transpose(1, 0, 2)
    grad_hq, grad_hk, grad_hv = lax.map(
        head_backward(allowed, HEAD_DIM ** (-0.5)),
        (heads_query, heads_key, heads_value, heads_grad, logsum),
    )
    grad_query_low = grad_hq.transpose(1, 0, 2).reshape(rows, HEADS * HEAD_DIM).astype(jnp.bfloat16)
    grad_keys_low = grad_hk.transpose(1, 0, 2).reshape(rows, GROUPS, -1).astype(jnp.bfloat16)
    grad_values_low = grad_hv.transpose(1, 0, 2).reshape(rows, GROUPS, -1).astype(jnp.bfloat16)
    head_cols = grad_keys_low.shape[2]
    keyup3 = full_keyup.reshape(GROUPS, LATENT, -1)
    valup3 = full_valup.reshape(GROUPS, LATENT, -1)
    grad_lat = jnp.einsum("tgf,glf->tgl", grad_keys_low, keyup3, preferred_element_type=jnp.float32)
    grad_lat = grad_lat + jnp.einsum(
        "tgf,glf->tgl", grad_values_low, valup3, preferred_element_type=jnp.float32
    )
    grad_latent_low = grad_lat.reshape(rows, GROUPS * LATENT).astype(jnp.bfloat16)
    latent_flat = lat3.reshape(rows, GROUPS * LATENT)
    paired = jnp.concatenate([grad_keys_low, grad_values_low], axis=2).reshape(
        rows, GROUPS * 2 * head_cols
    )
    count = w_keyup.shape[0] * lax.axis_size(("dp", "fsdp"))
    product = matmul_left(latent_flat, paired).reshape(count, GROUPS, 2 * head_cols)
    owner = jnp.arange(count, dtype=jnp.int32) // LATENT
    picker = (owner[:, None] == jnp.arange(GROUPS, dtype=jnp.int32)[None, :]).astype(jnp.float32)
    latent_own = lax.psum_scatter(
        jnp.sum(product * picker[:, :, None], axis=1).astype(jnp.bfloat16),
        ("dp", "fsdp"),
        scatter_dimension=0,
        tiled=True,
    )
    grad_normed = matmul_right(grad_query_low, full_query) + matmul_right(
        grad_latent_low, full_latent
    )
    packed_attn = jnp.concatenate([grad_query_low, grad_latent_low], axis=1)
    attn_own = lax.psum_scatter(
        column_term(normed, packed_attn), ("dp", "fsdp"), scatter_dimension=0, tiled=True
    )
    grad_in_norm, grad_gain_one = norm_back(
        grad_normed, inputs, rstd_one, gain_one.astype(jnp.float32)
    )
    grad_tokens = grad_middle + grad_in_norm
    gains_own = (
        lax.psum_scatter(grad_gain_one, ("dp", "fsdp"), scatter_dimension=0, tiled=True),
        lax.psum_scatter(grad_gain_two, ("dp", "fsdp"), scatter_dimension=0, tiled=True),
    )
    query_cols = HEADS * HEAD_DIM
    return (
        block_out,
        grad_tokens,
        attn_own[:, :query_cols].astype(jnp.float32),
        attn_own[:, query_cols:].astype(jnp.float32),
        latent_own[:, :head_cols].astype(jnp.float32),
        latent_own[:, head_cols:].astype(jnp.float32),
        output_own.astype(jnp.float32),
        gains_own[0],
        gains_own[1],
        ffn_own[:, :ff_width].astype(jnp.float32),
        ffn_own[:, ff_width:].astype(jnp.float32),
        down_own.astype(jnp.float32),
    )


MESH = pl.DeviceIdType.MESH
F32 = jnp.float32
BF16 = jnp.bfloat16
SCALE = HEAD_DIM ** (-0.5)
ROWS = 256
WIDTH = 1024
HALF = 1408
PARTS = (768, 640)
FFN = 1 + 2 * len(PARTS)
PUT = 3
DOWN = 88


ROUTE = ("y21xs", "y21xs", "21xys", "21yxs")
SUM_X_FIRST = (True, True, True, True)


class Slots:
    def __init__(self):
        self.count = 0

    def take(self, number):
        first = self.count
        self.count += number
        return first


SLOTS = Slots()
S_A = [SLOTS.take(16) for _ in range(4)]
S_HALF = SLOTS.take(FFN)
S_F = [SLOTS.take(8) for _ in range(FFN)]
S_COT, S_TOK, S_DN2, S_OUT, S_END = (SLOTS.take(1) for _ in range(5))
S_R = [SLOTS.take(10) for _ in range(FFN + 4)]
S_SUM = SLOTS.take(5)


def nn(left, right):
    return jnp.dot(left, right, preferred_element_type=F32)


def nt(left, right):
    return lax.dot_general(left, right, (((1,), (1,)), ((), ())), preferred_element_type=F32)


def tn(left, right):
    return lax.dot_general(left, right, (((0,), (0,)), ((), ())), preferred_element_type=F32)


(
    AA, AG, AT, H_S, H_R, FA, FG, FT, COT_S, COT_R, TOK_S, TOK_R, END_S, END_R, DN2_S, DN2_R, OUT_S,
    OUT_R, R_GO, R_S, R_B, R_A, R_1, R_2, R_L, R_E, SUM_S, SUM_R,
) = range(28)
(
    G_START, G_WEIGHTS, G_ACROSS, G_DOWN_W, G_QUERY, G_OUTPUT_W, G_FFN_A, G_FFN_B, G_BACK, G_RESULT,
    G_TAIL, G_MASK, G_GAIN, G_NORM, G_LATENT, G_KEYS, G_NORM_P, G_LATENT_P, G_KEYS_P, G_COMPACT,
    G_ATTEND, G_QUERY_P, G_ATTEND_P, G_MIDDLE, G_NORM2, G_MIDDLE_P, G_NORM2_P, G_HIDDEN_A, G_DN_A,
    G_GATEUP_A, G_DN_B, G_DOWN, G_GATEUP_B, G_OUT, G_DMERGED, G_OUTPUT, G_ATTENDB, G_PROJQ, G_PROJL,
    G_DNORMED, G_NORM1B, G_HIDDEN_B, G_NORM2B, G_LATENTB,
) = range(44)
PLAN = {
    G_START: (
        (H_S, 1), (AA, 2, 0), (AG, 2, 0, 1), (FA, 0, 0), (AA, 0, 0), (AA, 1, 0), (FG, 0, 0, 0),
        (AG, 0, 0, 0), (FG, 0, 0, 2),
    ),
    (G_MASK, 3): (
        (AG, 2, 0, 2), (H_S, 2), (FG, 0, 0, 1), (TOK_S, 1), (AA, 0, 1), (TOK_S, 3), (H_S, 4),
    ),
    G_WEIGHTS: (
        (AG, 0, 0, 1), (AG, 0, 0, 2), (AG, 0, 1, 3), (AG, 1, 0, 3), (H_R, 2), (H_S, 3),
        (AG, 0, 0, 3), (AA, 3, 0), (AG, 3, 0, 1), (AG, 1, 0, 0), (FA, 0, 2), (FA, 0, 1),
        (FG, 0, 2, 2), (TOK_S, 2), (AG, 2, 0, 0), (FG, 0, 1, 2), (AA, 0, 2), (AG, 0, 1, 2),
        (AA, 0, 4), (H_R, 1), (AG, 0, 1, 1), (AG, 0, 2, 2), (AA, 2, 2), (AA, 3, 2), (H_R, 3),
        (AG, 3, 0, 2), (AG, 0, 4, 3), (AG, 1, 0, 1), (AA, 2, 4), (AA, 1, 1), (AA, 0, 8),
        (AG, 1, 1, 3), (FG, 0, 1, 1), (AA, 0, 5), (AG, 3, 0, 0), (AG, 2, 2, 2), (FA, 1, 0),
        (AA, 0, 3), (AG, 0, 3, 3), (FA, 2, 0), (AG, 1, 1, 1), (H_R, 4), (FG, 1, 0, 2), (AG, 3, 2, 2),
        (AG, 0, 3, 2), (AG, 0, 2, 3), (AG, 0, 5, 3), (TOK_S, 0), (AA, 0, 12), (AG, 2, 0, 3),
        (AA, 0, 6), (AA, 2, 6), (FG, 2, 0, 2), (AA, 2, 1), (AG, 2, 1, 3), (AG, 1, 0, 2), (FA, 0, 3),
        (AG, 2, 4, 3), (AG, 2, 1, 1), (AA, 1, 2), (AG, 0, 6, 3), (AA, 3, 1), (FA, 1, 4), (FA, 3, 0),
        (AG, 1, 1, 2), (FG, 0, 3, 2), (AA, 0, 7), (AG, 3, 1, 1), (FG, 3, 0, 2), (FA, 4, 0),
        (AG, 0, 7, 3), (AA, 3, 4), (AA, 2, 12), (AA, 1, 3), (AA, 0, 9), (FA, 0, 4), (FG, 2, 0, 0),
        (FA, 0, 6), (AA, 1, 4), (AG, 1, 2, 2), (AA, 0, 10), (AG, 2, 1, 2), (AA, 0, 11), (AA, 0, 13),
        (END_S,), (FA, 0, 5), (AA, 2, 3), (AG, 1, 3, 3), (AA, 0, 14), (AG, 3, 1, 2), (AG, 2, 2, 3),
        (AG, 1, 3, 2), (AA, 1, 8), (AA, 1, 5), (AG, 2, 3, 3), (FG, 2, 0, 1), (AG, 1, 4, 3),
        (AG, 2, 3, 2), (FG, 1, 0, 0), (FG, 4, 0, 2), (AA, 0, 15), (AA, 3, 6), (AG, 2, 6, 3),
        (AA, 2, 5), (TOK_R,), (AT, 0),
    ),
    (G_GAIN, 7): (
        (AA, 3, 5), (AG, 1, 2, 3),
    ),
    (G_NORM, 3): (
        (AA, 1, 6), (FA, 0, 7), (FG, 1, 0, 1), (AA, 2, 8), (FA, 2, 1), (AG, 1, 6, 3), (FG, 2, 1, 2),
    ),
    (G_LATENT, 1): (
        (AA, 1, 11), (AA, 2, 14), (AG, 2, 5, 3), (END_R,), (AG, 1, 5, 3), (FT, 0), (FA, 3, 4),
        (AA, 3, 3), (AA, 2, 7), (FG, 3, 0, 0), (AA, 1, 7), (AG, 1, 7, 3),
    ),
    (G_KEYS, 1): (
        (AG, 3, 3, 3), (AG, 3, 4, 3),
    ),
    G_ACROSS: (
        (AG, 3, 3, 2), (AG, 2, 7, 3),
    ),
    (G_NORM_P, 3): (
        (FA, 2, 2), (AA, 1, 14), (FG, 2, 1, 1), (FG, 2, 2, 2), (AG, 3, 1, 3), (AA, 1, 9),
    ),
    (G_LATENT_P, 1): (
        (AA, 1, 12),
    ),
    (G_KEYS_P, 1): (
        (AA, 3, 7), (AA, 2, 11), (FA, 1, 1), (AA, 1, 10), (AG, 3, 2, 3), (AA, 1, 15), (FG, 1, 1, 2),
        (AA, 1, 13), (FA, 2, 4), (AG, 3, 0, 3), (FG, 1, 1, 1), (AG, 3, 5, 3), (AG, 3, 7, 3),
    ),
    G_DOWN_W: (
        (FG, 4, 0, 0), (AG, 3, 6, 3), (AA, 2, 13),
    ),
    (G_COMPACT, 7): (
        (FA, 1, 2), (COT_S, 2), (AT, 1),
    ),
    G_QUERY: (
        (FG, 1, 2, 2), (FA, 2, 5), (FG, 3, 0, 1),
    ),
    (G_QUERY, 3): (
        (FA, 3, 1),
    ),
    (G_ATTEND, 3): (
        (FG, 3, 1, 2), (COT_S, 0),
    ),
    (G_ATTEND, 7): (
        (FG, 3, 1, 1), (FA, 2, 3), (FA, 4, 4), (AA, 2, 10), (COT_S, 3), (FG, 4, 0, 1), (FG, 2, 3, 2),
        (AA, 3, 13), (AA, 2, 15), (AA, 3, 14),
    ),
    (G_QUERY_P, 3): (
        (FA, 1, 3), (AA, 3, 15), (AA, 3, 9), (FG, 1, 3, 2),
    ),
    (G_ATTEND_P, 3): (
        (FA, 4, 1), (FA, 1, 6), (FA, 2, 6), (FG, 4, 1, 1), (AA, 3, 11), (FA, 3, 5), (AA, 3, 12),
        (AA, 3, 10), (FG, 4, 1, 2), (AA, 3, 8), (COT_S, 1), (AA, 2, 9),
    ),
    G_OUTPUT_W: (
        (AT, 3), (AT, 2),
    ),
    (G_MIDDLE, 3): (
        (FA, 3, 3), (FA, 1, 7), (FA, 2, 7), (FG, 3, 3, 2),
    ),
    (G_NORM2, 3): (
        (FA, 3, 2), (FA, 1, 5), (FG, 3, 2, 2),
    ),
    (G_MIDDLE_P, 3): (
        (FA, 4, 2),
    ),
    (G_NORM2_P, 3): (
        (FT, 2), (FT, 1), (FA, 4, 3), (FA, 4, 5),
    ),
    G_FFN_A: (
        (FG, 4, 3, 2),
    ),
    (G_HIDDEN_A, 0): (
        (FG, 4, 2, 2), (FA, 3, 7), (COT_R,),
    ),
    (G_HIDDEN_A, 1): (
        (FA, 3, 6),
    ),
    (G_DN_A, 1): (
        (FA, 4, 7),
    ),
    (G_GATEUP_A, 1): (
        (FA, 4, 6), (R_GO, 1), (R_GO, 2),
    ),
    G_FFN_B: (
        (FT, 4), (FT, 3), (R_S, 1, 1), (R_B, 1, 3),
    ),
    (G_DN_B, 1): (
        (R_S, 2, 1), (DN2_S,), (R_B, 1, 1), (R_S, 1, 0), (R_B, 2, 3),
    ),
    (G_DN_B, 0): (
        (R_A, 1, 3),
    ),
    (G_DOWN, 0): (
        (R_GO, 0), (R_B, 1, 2),
    ),
    (G_DOWN, 1): (
        (R_A, 1, 1), (R_S, 2, 0), (R_S, 0, 1), (R_B, 0, 3),
    ),
    (G_GATEUP_B, 1): (
        (R_A, 2, 3), (R_GO, 4), (R_B, 2, 1),
    ),
    (G_GATEUP_B, 3): (
        (R_A, 1, 2), (R_GO, 3), (R_B, 2, 2), (R_S, 0, 0), (R_1, 1, 1),
    ),
    (G_OUT, 0): (
        (R_S, 4, 1), (OUT_S, 0), (OUT_S, 2),
    ),
    (G_OUT, 1): (
        (R_B, 4, 3), (R_S, 4, 0), (OUT_S, 3), (R_A, 0, 3), (R_S, 3, 0),
    ),
    G_BACK: (
        (DN2_R,), (R_S, 3, 1),
    ),
    (G_DMERGED, 3): (
        (R_B, 3, 3), (R_A, 2, 1),
    ),
    (G_OUTPUT, 3): (
        (R_B, 4, 1), (R_A, 2, 2), (R_B, 4, 0), (R_B, 3, 1), (R_GO, 5), (R_1, 2, 1), (R_B, 4, 2),
    ),
    (G_ATTENDB, 3): (
        (R_S, 5, 1), (R_B, 5, 3), (R_B, 0, 2), (R_B, 1, 0), (R_A, 3, 3), (R_A, 4, 3),
    ),
    (G_ATTENDB, 7): (
        (R_B, 0, 1),
    ),
    (G_PROJQ, 1): (
        (R_A, 4, 1), (R_B, 5, 1), (R_S, 5, 0), (R_B, 5, 2),
    ),
    (G_PROJQ, 3): (
        (R_GO, 6), (R_A, 5, 3),
    ),
    (G_PROJL, 3): (
        (R_B, 3, 0), (R_S, 6, 1),
    ),
    (G_DNORMED, 3): (
        (R_A, 4, 2), (R_GO, 7), (R_1, 4, 1), (R_B, 6, 3),
    ),
    (G_NORM1B, 7): (
        (R_GO, 8), (R_A, 5, 1), (R_S, 8, 1), (SUM_S, 0), (R_A, 4, 0), (R_B, 3, 2), (R_S, 7, 1),
        (R_A, 0, 2), (R_B, 5, 0), (R_A, 5, 2), (R_1, 5, 1), (R_1, 0, 1), (R_B, 2, 0), (R_B, 6, 2),
        (R_B, 6, 1), (R_B, 7, 3), (R_S, 6, 0), (R_B, 7, 0), (SUM_R, 0), (R_1, 4, 0), (SUM_S, 1),
        (R_A, 3, 1), (R_A, 6, 3), (R_A, 5, 0), (R_A, 6, 1), (R_1, 5, 0), (R_B, 7, 2), (R_B, 0, 0),
        (R_A, 3, 2), (R_A, 6, 2),
    ),
    G_RESULT: (
        (R_B, 8, 3), (R_B, 7, 1), (R_S, 8, 0), (R_2, 4), (R_2, 5), (SUM_R, 1), (R_A, 3, 0), (SUM_S, 2),
        (R_1, 3, 1), (R_A, 1, 0), (R_A, 8, 3), (R_B, 6, 0), (R_B, 8, 2), (R_S, 7, 0), (R_1, 6, 1),
        (R_A, 7, 0), (R_A, 2, 0), (R_A, 7, 2), (R_1, 2, 0), (R_1, 1, 0), (R_L, 5), (R_A, 7, 3),
        (SUM_R, 2), (R_A, 7, 1), (R_B, 8, 1), (R_1, 3, 0), (R_L, 4), (R_A, 6, 0), (R_2, 2),
        (OUT_S, 1), (R_1, 7, 1), (R_A, 0, 0), (R_A, 8, 1), (R_1, 6, 0), (R_2, 1), (R_A, 8, 2),
        (R_2, 6), (R_B, 8, 0), (R_E, 4), (R_1, 8, 1), (R_L, 2), (SUM_S, 3), (R_2, 3), (R_1, 7, 0),
        (R_2, 7), (R_L, 6), (R_A, 0, 1), (R_A, 8, 0), (R_L, 3), (R_1, 8, 0), (SUM_R, 3), (R_L, 7),
        (R_E, 5), (OUT_R,), (SUM_S, 4),
    ),
    (G_RESULT, 7): (
        (R_2, 8), (R_L, 8), (R_L, 1), (R_E, 1), (R_E, 8), (R_E, 3), (R_1, 0, 0), (R_E, 2),
    ),
    G_TAIL: (
        (R_2, 0), (R_E, 6), (R_E, 7), (SUM_R, 4), (R_L, 0),
    ),
}


def layer_kernel(
    tok_hbm, len_ref, cot_hbm, wq_hbm, wl_hbm, wk_hbm, wv_hbm, wo_hbm, gain_one, gain_two, wg_hbm, wu_hbm, wd_ref,
    out_hbm, gtok_hbm, at_hbm, gain_hbm, gg_hbm, gu_hbm, gd_hbm,
    attn, latw, gate_a, up_a, gate_b, up_b, down_w, down_c, gain_full,
    tok, ends, bias, normed, query, latent, keys, values, merged, lse, middle, normed2, dout,
    mixed, dgate, dup, tmp, rcv_dn2, snd_out, rcv_out,
    dmid, dmid_low, dmerged, dquery, dkeys, dvalues, dlatent,
    pattn,
    s_d, s_ga, s_ua, s_gb, s_ub,
    y_d, y_ga, y_ua, y_gb, y_ub,
    z_d, z_ga, z_ua, z_gb, z_ub,
    x_ga, x_ua, x_gb, x_ub,
    s_a, x_a, z_a, y_a, sum_own, sum_rcv,
    send_sem, recv_sem, local_sem,
):
    snd_dn2 = dquery
    dp = lax.axis_index("dp")
    fs = lax.axis_index("fsdp")
    x, c, z, y = lax.div(dp, 2), lax.rem(dp, 2), lax.div(fs, 2), lax.rem(fs, 2)
    zh, zl = lax.div(z, 2), lax.rem(z, 2)
    sib = (x * 2 + 1 - c, fs)
    xp = ((1 - x) * 2 + c, fs)
    yp = (dp, z * 2 + 1 - y)
    z1 = (dp, (zh * 2 + 1 - zl) * 2 + y)
    z2 = (dp, ((1 - zh) * 2 + zl) * 2 + y)

    def rel(v, other):
        return 1 - v if other else v

    def line(dh, dl):
        return rel(zh, dh) * 2 + rel(zl, dl)

    sent, groups = {}, []

    def copy(src, dst, slot, target, group):
        if group not in groups:
            groups.append(group)
        return pltpu.make_async_remote_copy(
            src_ref=src, dst_ref=dst, send_sem=send_sem.at[groups.index(group)], recv_sem=recv_sem.at[slot],
            device_id=target, device_id_type=MESH,
        )

    def send(group, src, dst, slot, target):
        copy(src, dst, slot, target, group).start()
        sent[group] = sent.get(group, 0) + math.prod(src.shape) * src.dtype.itemsize

    def drain(group):
        tiles = sent.pop(group, 0) // 4096
        if tiles:
            wide = next(n for n in range(8, 0, -1) if tiles % n == 0 and tiles // n <= 128)
            size = tmp.at[pl.ds(0, tiles // wide * 8), pl.ds(0, wide * 128)]
            copy(size, size, 0, sib, group).wait_send()

    def arrive(dst, slot):
        copy(dst, dst, slot, sib, "sum").wait_recv()

    def local(src, dst, k):
        return pltpu.make_async_copy(src, dst, local_sem.at[k])

    def put(src, dst, k):
        local(src, dst, k).start()

    def add(dst, src):
        dst[...] = dst[...] + src[...]

    def cols(n, width=256):
        return pl.ds(pl.multiple_of(n * width, width), width)

    ops = {}

    def op(code):
        def enter(fn):
            ops[code] = fn
            return fn

        return enter

    def run(items):
        for name, *rest in items:
            ops[name](*rest)

    def gap(name):
        run(PLAN.get(name, ()))

    def loop(count, *stages, at=(), unroll=1):
        ends = [*at, count]
        for first, last in zip([0, *at], ends):

            def step(k, carry):
                for _, body in stages:
                    body(k)
                return carry

            if last - first == 1:
                for name, body in stages:
                    body(first)
                    gap((name, first))
            else:
                lax.fori_loop(first, last, step, 0, unroll=unroll)
                gap((stages[-1][0], last - 1))

    ways = {"y": yp, "x": xp, "1": z1, "2": z2, "s": sib}

    def a_blk(w, bits):
        route = ROUTE[w]
        across = {way: bits >> k & 1 for k, way in enumerate(route)}
        xx, cc, yy = rel(x, across["x"]), rel(c, across["s"]), rel(y, across["y"])
        zz = line(across["2"], across["1"])
        if w == 0:
            return latw.at[xx, cc, zz, yy]
        if w == 1:
            return attn.at[0, xx, cc, zz, yy]
        return attn.at[1, xx, cc, zz, yy, :, pl.ds(512 * (w - 2), 512)]

    def a_send(w, bits, k):
        blk = a_blk(w, bits)
        send("a%d" % w, blk, blk, S_A[w] + (bits + (1 << k) if k < 4 else 0), ways[ROUTE[w][k]])

    @op(AA)
    def aa(w, bits):
        if bits:
            arrive(a_blk(w, bits), S_A[w] + bits)
        a_send(w, bits, 4)

    @op(AG)
    def ag(w, bits, k):
        a_send(w, bits, k)

    @op(AT)
    def at(w):
        other = 1 - c
        half = pl.ds(512 * (w - 2), 512)
        arrive((latw.at[:, other], attn.at[0, :, other], attn.at[1, :, other, :, :, :, half])[min(w, 2)], S_A[w])

    ffn = (down_w, gate_a, up_a, gate_b, up_b)
    ffn_hbm = (None, wg_hbm, wu_hbm, wg_hbm, wu_hbm)
    starts = (None, 0, 0, 768, 768)

    def half_cols(xx, t):
        return pl.ds(pl.multiple_of(xx * HALF + starts[t], 128), ffn[t].shape[-1])

    @op(H_S)
    def h_s(t):
        send("half", ffn_hbm[t].at[:, half_cols(1 - x, t)], ffn[t].at[c, z, y, x], S_HALF + t, xp)

    @op(H_R)
    def h_r(t):
        arrive(ffn[t].at[c, z, y, 1 - x], S_HALF + t)

    def f_blk(t, bits):
        return ffn[t].at[rel(c, bits >> 3 & 1), line(bits & 1, bits >> 1 & 1), rel(y, bits >> 2 & 1)]

    def f_send(t, bits, k):
        blk = f_blk(t, bits)
        send("ffn%d" % t, blk, blk, S_F[t] + (bits + (1 << k) if k < 3 else 0), (z2, z1, yp, sib)[k])

    @op(FA)
    def fa(t, bits):
        if bits:
            arrive(f_blk(t, bits), S_F[t] + bits)
        f_send(t, bits, 3)

    @op(FG)
    def fg(t, bits, k):
        f_send(t, bits, k)

    @op(FT)
    def ft(t):
        arrive(ffn[t].at[1 - c], S_F[t])

    def quarter(ref, k):
        return ref.at[pl.ds(k * 64, 64)]

    @op(COT_S)
    def cot_s(k):
        send("cot", quarter(dout.at[x], k), quarter(dout.at[x], k), S_COT, xp)

    @op(COT_R)
    def cot_r():
        arrive(dout.at[1 - x], S_COT)

    @op(TOK_S)
    def tok_s(k):
        send("tok", quarter(tok.at[x], k), quarter(tok.at[x], k), S_TOK, xp)

    @op(TOK_R)
    def tok_r():
        arrive(tok.at[1 - x], S_TOK)

    @op(END_S)
    def end_s():
        send("tok", ends.at[x], ends.at[x], S_END, xp)

    @op(END_R)
    def end_r():
        arrive(ends.at[1 - x], S_END)

    @op(DN2_S)
    def dn2_s():
        send("dn2", snd_dn2, rcv_dn2, S_DN2, xp)

    @op(DN2_R)
    def dn2_r():
        arrive(rcv_dn2, S_DN2)

    @op(OUT_S)
    def out_s(k):
        send("out", quarter(snd_out, k), quarter(rcv_out, k), S_OUT, xp)

    @op(OUT_R)
    def out_r():
        arrive(rcv_out, S_OUT)

    ffn_s = (s_d, s_ga, s_ua, s_gb, s_ub)
    ffn_y = (y_d, y_ga, y_ua, y_gb, y_ub)
    ffn_zb = (z_d, z_ga, z_ua, z_gb, z_ub)
    ffn_x = (None, x_ga, x_ua, x_gb, x_ub)
    out_cols = (None, *[pl.ds(starts[t], ffn[t].shape[-1]) for t in range(1, FFN)])
    ffn_out = (None, *[gg_hbm, gu_hbm] * 2)

    def pick(i):
        return ((0, pl.ds(0, WIDTH)), (1, pl.ds(0, WIDTH)), (2, pl.ds(0, 512)), (2, pl.ds(512, 512)))[i - FFN]

    def sib_part(i, other):
        if i < FFN:
            yy = rel(y, other)
            return yy, ffn[i].at[1 - c, :, yy], ffn_s[i].at[yy], lambda zz: (ffn[i].at[c, zz, yy], ffn_s[i].at[yy, zz])
        k, cl = pick(i)
        if SUM_X_FIRST[i - FFN]:
            xx = rel(x, other)
            return (
                xx,
                pattn.at[k, xx, 1 - c, :, :, :, cl],
                s_a.at[k, xx, :, :, :, cl],
                lambda zz: (pattn.at[k, xx, c, zz, :, :, cl], s_a.at[k, xx, zz, :, :, cl]),
            )
        yy = rel(y, other)
        return (
            yy,
            pattn.at[k, :, 1 - c, :, yy, :, cl],
            s_a.at[k, :, :, yy, :, cl],
            lambda zz: (pattn.at[k, :, c, zz, yy, :, cl], s_a.at[k, :, zz, yy, :, cl]),
        )

    def first_hop(i, d):
        if i < FFN:
            return yp, ffn[i].at[c, d, 1 - y], ffn_y[i].at[d]
        k, cl = pick(i)
        if SUM_X_FIRST[i - FFN]:
            return xp, pattn.at[k, 1 - x, c, d, :, :, cl], x_a.at[k, d, :, :, cl]
        return yp, pattn.at[k, :, c, d, 1 - y, :, cl], x_a.at[k, d, :, :, cl]

    def line_blk(i, d):
        if i < FFN:
            return ffn[i].at[c, d, y]
        k, cl = pick(i)
        if SUM_X_FIRST[i - FFN]:
            return pattn.at[k, x, c, d, :, :, cl]
        return pattn.at[k, :, c, d, y, :, cl]

    def line_buf(i, b):
        if i < FFN:
            return ffn_zb[i].at[b]
        k, cl = pick(i)
        return z_a.at[k, b, :, :, cl]

    def last_hop(i):
        if i < FFN:
            return xp, ffn[i].at[c, z, y, 1 - x], ffn_x[i]
        k, cl = pick(i)
        if SUM_X_FIRST[i - FFN]:
            return yp, pattn.at[k, x, c, z, 1 - y, :, cl], y_a.at[k, :, cl]
        return xp, pattn.at[k, 1 - x, c, z, y, :, cl], y_a.at[k, :, cl]

    @op(R_GO)
    def r_go(i):
        for other in (1, 0):
            k, src, dst, _ = sib_part(i, other)
            send("r%d" % i, src, dst, S_R[i] + k, sib)

    @op(R_S)
    def r_s(i, other):
        k, _, dst, pairs = sib_part(i, other)
        arrive(dst, S_R[i] + k)
        if not other:
            for zz in range(4):
                add(*pairs(zz))

    @op(R_B)
    def r_b(i, bits):
        d = line(bits >> 1, bits & 1)
        add(*sib_part(i, 1)[3](d))
        target, src, buf = first_hop(i, d)
        send("r%d" % i, src, buf, S_R[i] + 2 + bits, target)

    @op(R_A)
    def r_a(i, bits):
        d = line(bits >> 1, bits & 1)
        _, _, buf = first_hop(i, d)
        arrive(buf, S_R[i] + 2 + bits)
        add(line_blk(i, d), buf)
        if bits & 1:
            send("r%d" % i, line_blk(i, d), line_buf(i, bits >> 1), S_R[i] + 6 + (bits >> 1), z1)

    @op(R_1)
    def r_1(i, dh):
        d = line(dh, 0)
        arrive(line_buf(i, dh), S_R[i] + 6 + dh)
        add(line_blk(i, d), line_buf(i, dh))
        if dh:
            send("r%d" % i, line_blk(i, d), line_buf(i, 2), S_R[i] + 8, z2)

    @op(R_2)
    def r_2(i):
        arrive(line_buf(i, 2), S_R[i] + 8)
        add(line_blk(i, z), line_buf(i, 2))

    @op(R_L)
    def r_l(i):
        if i == 0:
            put(down_w.at[c, z, y], gd_hbm, PUT)
            return
        target, src, buf = last_hop(i)
        send("r%d" % i, src, buf, S_R[i] + 9, target)
        if i < FFN:
            put(ffn[i].at[c, z, y, x], ffn_out[i].at[x, :, out_cols[i]], PUT + i * 2)

    @op(R_E)
    def r_e(i):
        _, _, buf = last_hop(i)
        arrive(buf, S_R[i] + 9)
        if i < FFN:
            put(buf, ffn_out[i].at[1 - x, :, out_cols[i]], PUT + 1 + i * 2)
        else:
            k, cl = pick(i)
            blk = pattn.at[k, x, c, z, y, :, cl]
            add(blk, buf)
            put(blk, at_hbm.at[k, :, cl], PUT + 4 + FFN + i)

    def wait_out():
        local(down_w.at[c, z, y], gd_hbm, PUT).wait()
        for i in range(1, FFN):
            local(ffn[i].at[c, z, y, x], ffn_out[i].at[x, :, out_cols[i]], PUT + i * 2).wait()
            local(ffn_x[i], ffn_out[i].at[1 - x, :, out_cols[i]], PUT + 1 + i * 2).wait()
        for i in range(FFN, FFN + 4):
            k, cl = pick(i)
            local(pattn.at[k, x, c, z, y, :, cl], at_hbm.at[k, :, cl], PUT + 4 + FFN + i).wait()

    sum_to = (sib, yp, xp, z1, z2)

    @op(SUM_S)
    def sum_s(i):
        copy(sum_own, sum_rcv.at[i], S_SUM + i, sum_to[i], "sum").start()

    @op(SUM_R)
    def sum_r(i):
        copy(sum_own, sum_rcv.at[i], S_SUM + i, sum_to[i], "sum").wait_send()
        arrive(sum_rcv.at[i], S_SUM + i)
        add(sum_own, sum_rcv.at[i])

    loads = [
        (wq_hbm, attn.at[0, x, c, z, y]),
        (wl_hbm, latw.at[x, c, z, y, :, pl.ds(0, 512)]),
        (wk_hbm, latw.at[x, c, z, y, pl.ds(0, 16), pl.ds(512, 512)]),
        (wv_hbm, latw.at[x, c, z, y, pl.ds(16, 16), pl.ds(512, 512)]),
        (wo_hbm, attn.at[1, x, c, z, y]),
        (tok_hbm, tok.at[x]),
        (cot_hbm, dout.at[x]),
        *[(ffn_hbm[t].at[:, half_cols(x, t)], ffn[t].at[c, z, y, x]) for t in range(1, FFN)],
    ]
    loads = [local(src, dst, k) for k, (src, dst) in enumerate(loads)]
    for load in loads:
        load.start()
    bar = pltpu.get_barrier_semaphore()

    def hello(target):
        pl.semaphore_signal(bar, inc=1, device_id=target, device_id_type=MESH)

    for target in (sib, xp, yp, z1, z2):
        hello(target)

    def piled(rows):
        return jnp.concatenate([rows[:, 0:512], rows[:, 512:WIDTH]], axis=0).astype(BF16)

    def stage_own():
        down_w[c, z, y] = piled(wd_ref[...].astype(F32))
        lane = lax.broadcasted_iota(jnp.int32, (16, 128), 1)
        mine = lax.div(lane, 32) == lax.rem(fs, 4)
        two = [ref[...].astype(F32).reshape(1, 32) for ref in (gain_one, gain_two)]
        two = jnp.concatenate([*two, jnp.zeros((14, 32), F32)], axis=0)
        two = jnp.where(mine, jnp.concatenate([two] * 4, axis=1), 0.0)
        latw[x, c, z, y, pl.ds(0, 16), pl.ds(WIDTH, 128)] = two.astype(BF16)
        latw[x, c, z, y, pl.ds(16, 16), pl.ds(WIDTH, 128)] = jnp.zeros((16, 128), BF16)

    e0 = len_ref[0]
    e1 = e0 + len_ref[1]
    e2 = e1 + len_ref[2]
    e3 = e2 + len_ref[3]

    def stage_ends():
        place = lax.broadcasted_iota(jnp.int32, (8, 128), 0)
        ends[x] = sum(jnp.where(place == k, e, 0) for k, e in enumerate((e0, e1, e2, e3))).astype(F32)

    stage_own()
    stage_ends()
    for load in loads[:5]:
        load.wait()
    pl.semaphore_wait(bar, 5)
    gap(G_START)

    for load in loads[5:]:
        load.wait()

    def mask_rows(k):
        rows = pl.ds(pl.multiple_of(k * 64, 64), 64)
        position = lax.broadcasted_iota(jnp.int32, (64, WIDTH), 0) + k * 64
        dout[x, rows] = jnp.where(position < e3, dout[x, rows].astype(F32), 0.0).astype(BF16)

    loop(4, (G_MASK, mask_rows))
    gap(G_WEIGHTS)

    def gain_rows(k):
        g = latw.at[lax.div(k, 4), lax.div(lax.rem(k, 4), 2)]
        part = g[pl.ds(lax.rem(k, 2) * 2, 2), :, 0:16, WIDTH : WIDTH + 128].astype(F32)
        gain_full[:, pl.ds(pl.multiple_of(k * 128, 128), 128)] = part[0, 0] + part[0, 1] + part[1, 0] + part[1, 1]

    loop(8, (G_GAIN, gain_rows))

    low_half = lax.broadcasted_iota(jnp.int32, (ROWS, 128), 1) < HEAD_DIM
    head_lane = lax.broadcasted_iota(jnp.int32, (ROWS, 128), 1)

    def halves(v):
        zero = jnp.zeros_like(v)
        return (jnp.where(low_half, v, zero), jnp.where(low_half, zero, v))

    def both(v):
        return jnp.concatenate(halves(v), axis=0)

    def scaled(v):
        return (v.astype(F32) * SCALE).astype(BF16)

    def up_weight(g, first):
        return latw[g, :, :, :, pl.ds(first, 16), pl.ds(512, 512)].reshape(256, 512)

    def segment(m, shape, axis):
        position = lax.broadcasted_iota(jnp.int32, shape, axis).astype(F32)
        return sum((position >= ends[m, pl.ds(k, 1), pl.ds(0, 1)]).astype(F32) for k in range(4))

    def stage_masks(m):
        row = lax.broadcasted_iota(jnp.int32, (ROWS, ROWS), 0)
        col = lax.broadcasted_iota(jnp.int32, (ROWS, ROWS), 1)
        same = segment(m, (ROWS, 1), 0) == segment(m, (1, ROWS), 1)
        bias[m] = jnp.where(same & (col <= row), 0.0, -1e30)

    def attention(m, own, at, normed, query, latent, keys, values, merged, middle):
        at_norm, at_latent, at_keys, at_query, at_attend, at_middle, at_norm2 = at

        def norm_rows(k):
            rows = pl.ds(pl.multiple_of(k * 64, 64), 64)
            val = tok[m, rows].astype(F32)
            r1 = lax.rsqrt(jnp.mean(val * val, axis=1, keepdims=True) + EPSILON)
            normed[rows] = (val * r1 * gain_full[0:1, :]).astype(BF16)

        def latent_cols(n):
            w = latw[:, :, :, :, :, cols(n)].reshape(WIDTH, 256)
            latent[:, cols(n)] = nn(normed[...], w).astype(BF16)

        def key_cols(g):
            lat = latent[:, cols(g)]
            keys[:, cols(g, 512)] = nn(lat, up_weight(g, 0)).astype(BF16)
            values[:, cols(g, 512)] = nn(lat, up_weight(g, 16)).astype(BF16)

        def query_cols(n):
            w = attn[0, :, :, :, :, :, cols(n)].reshape(WIDTH, 256)
            query[:, cols(n)] = nn(normed[...], w).astype(BF16)

        def attend(j):
            pair = cols(j, 128)
            s = nt(both(scaled(query[:, pair])), keys[:, pair]) + jnp.concatenate([bias[m]] * 2, axis=0)
            peak = jnp.max(s, axis=1, keepdims=True)
            expo = jnp.exp(s - peak)
            total = jnp.sum(expo, axis=1, keepdims=True)
            res = nn((expo / total).astype(BF16), values[:, pair])
            merged[:, pair] = jnp.where(low_half, res[0:ROWS], res[ROWS : 2 * ROWS]).astype(BF16)
            if own:
                logsum = peak + jnp.log(total)
                lse[...] = jnp.where(
                    head_lane == j * 2,
                    logsum[0:ROWS],
                    jnp.where(head_lane == j * 2 + 1, logsum[ROWS : 2 * ROWS], lse[...]),
                )

        def middle_cols(n):
            w = attn[1, :, :, :, :, :, cols(n)].reshape(WIDTH, 256)
            middle[:, cols(n)] = tok[m, :, cols(n)].astype(F32) + nn(merged[...], w)

        def norm2_rows(k):
            rows = pl.ds(pl.multiple_of(k * 64, 64), 64)
            val = middle[rows]
            r2 = lax.rsqrt(jnp.mean(val * val, axis=1, keepdims=True) + EPSILON)
            normed2[m, rows] = (val * r2 * gain_full[1:2, :]).astype(BF16)

        def first():
            stage_masks(m)
            loop(4, (at_norm, norm_rows))
            loop(2, (at_latent, latent_cols), unroll=2)
            loop(GROUPS, (at_keys, key_cols), unroll=2)

        def second():
            loop(4, (at_query, query_cols), unroll=2)
            loop(8, (at_attend, attend), at=(4,), unroll=4)

        def third():
            loop(4, (at_middle, middle_cols), unroll=2)
            loop(4, (at_norm2, norm2_rows))

        return first, second, third

    def compact(k):
        pair = down_w.at[lax.div(k, 4), lax.rem(k, 4)]
        one, two = pair[0].astype(F32), pair[1].astype(F32)
        rows = pl.ds(pl.multiple_of(k * 2 * DOWN, 16), 2 * DOWN)
        for half in range(2):
            part = slice(half * DOWN, (half + 1) * DOWN)
            down_c[rows, pl.ds(half * 512, 512)] = jnp.concatenate([one[part], two[part]], axis=0).astype(BF16)

    at = (G_NORM, G_LATENT, G_KEYS, G_QUERY, G_ATTEND, G_MIDDLE, G_NORM2)
    own = attention(x, True, at, normed, query, latent, keys, values, merged, middle)
    at = (G_NORM_P, G_LATENT_P, G_KEYS_P, G_QUERY_P, G_ATTEND_P, G_MIDDLE_P, G_NORM2_P)
    across = attention(1 - x, False, at, dmid_low, dquery, dlatent, dkeys, dvalues, dmerged, dmid)
    own[0]()
    gap(G_ACROSS)
    across[0]()
    gap(G_DOWN_W)
    loop(8, (G_COMPACT, compact))
    gap(G_QUERY)
    own[1]()
    across[1]()
    gap(G_OUTPUT_W)
    own[2]()
    across[2]()
    gap(G_FFN_A)

    def ffn_w(ref, half, sl=slice(None)):
        w = ref[:, :, :, half, :, sl]
        return w.reshape(512, w.shape[-1])

    def hidden(it, gate_w, up_w, base, widths):
        m = rel(x, it)
        rows = pl.ds(pl.multiple_of(m * ROWS, ROWS), ROWS)
        for first, width in widths:
            sl, at = pl.ds(first, width), pl.ds(base + first, width)
            n2 = normed2[m]
            gate = nn(n2[:, 0:512], ffn_w(gate_w, 0, sl)) + nn(n2[:, 512:1024], ffn_w(gate_w, 1, sl))
            upper = nn(n2[:, 0:512], ffn_w(up_w, 0, sl)) + nn(n2[:, 512:1024], ffn_w(up_w, 1, sl))
            dmix = nt(dout[m], down_c[at])
            sig = jax.nn.sigmoid(gate)
            silu = gate * sig
            mixed[rows, at] = (silu * upper).astype(BF16)
            dgate[rows, at] = (dmix * upper * sig * (1.0 + gate * (1.0 - sig))).astype(BF16)
            dup[rows, at] = (dmix * silu).astype(BF16)

    def dn_half(it, gate_w, up_w, at, more):
        m = rel(x, it)
        rows = pl.ds(pl.multiple_of(m * ROWS, ROWS), ROWS)
        for half in range(2):
            part = nt(dgate[rows, at], ffn_w(gate_w, half)) + nt(dup[rows, at], ffn_w(up_w, half))
            to = (pl.ds(ROWS * it, ROWS), pl.ds(half * 512, 512))
            if more:
                part = part + tmp[to]
            if more == 2 and it:
                snd_dn2[:, pl.ds(half * 512, 512)] = part.astype(BF16)
            else:
                tmp[to] = part

    def grad_gate_up(it, gate_w, up_w, at):
        cc = jnp.where(it < 2, 1 - c, c)
        half = lax.rem(it, 2)
        sl = pl.ds(pl.multiple_of(half * 512 + cc * 256, 256), 256)
        width = gate_w.shape[-1]
        for src, dst in ((dgate, gate_w), (dup, up_w)):
            g = nn(normed2[0, :, sl].T, src[pl.ds(0, ROWS), at]) + nn(normed2[1, :, sl].T, src[pl.ds(ROWS, ROWS), at])
            dst[cc, :, :, half] = g.astype(BF16).reshape(4, 2, 32, width)

    def grad_down(it):
        cc = rel(c, it == 0)
        wide = pl.ds(pl.multiple_of(cc * 640, 128), 768)
        mt = mixed[:, wide].T
        tmp[pl.ds(ROWS, 768)] = nn(mt[:, 0:256], dout[0]) + nn(mt[:, 256:512], dout[1])

        def split(k, carry):
            rows = tmp[pl.ds(pl.multiple_of(ROWS + cc * 64 + k * DOWN, 8), DOWN)]
            down_w[cc, lax.div(k, 2), lax.rem(k, 2)] = piled(rows)
            return carry

        lax.fori_loop(0, 8, split, 0)

    def hidden_a(it):
        hidden(it, gate_a, up_a, 0, ((0, 512), (512, 256)))

    def dn_a(it):
        dn_half(it, gate_a, up_a, pl.ds(0, 768), 0)

    def gateup_a(it):
        grad_gate_up(it, gate_a, up_a, pl.ds(0, 768))

    def hidden_b(it):
        hidden(it, gate_b, up_b, 768, ((0, 512), (512, 128)))

    def dn_b(it):
        dn_half(it, gate_b, up_b, pl.ds(768, 640), 2)

    def gateup_b(it):
        grad_gate_up(it, gate_b, up_b, pl.ds(768, 640))

    def out_half(it):
        m = rel(x, it == 0)
        rows = pl.ds(pl.multiple_of(m * ROWS, ROWS), ROWS)
        part = nn(mixed[rows], down_c[...])
        if it == 0:
            snd_out[...] = part.astype(BF16)
        else:
            tmp[pl.ds(ROWS, ROWS)] = part

    loop(2, (G_HIDDEN_A, hidden_a), at=(1,))
    loop(2, (G_DN_A, dn_a), at=(1,))
    drain("ffn1")
    drain("ffn2")
    loop(4, (G_GATEUP_A, gateup_a), at=(2,))
    gap(G_FFN_B)
    hidden_b(1)
    gap((G_HIDDEN_B, 1))
    dn_b(1)
    gap((G_DN_B, 1))
    hidden_b(0)
    gap((G_HIDDEN_B, 0))
    dn_b(0)
    gap((G_DN_B, 0))
    drain("ffn0")
    loop(2, (G_DOWN, grad_down), at=(1,))
    drain("ffn3")
    drain("ffn4")
    loop(4, (G_GATEUP_B, gateup_b), at=(2,))
    loop(2, (G_OUT, out_half), at=(1,))
    gap(G_BACK)

    sum_own[...] = jnp.zeros((8, WIDTH), F32)

    def back_two(k):
        rows = pl.ds(pl.multiple_of(k * 32, 32), 32)
        mid = middle[rows]
        r2 = lax.rsqrt(jnp.mean(mid * mid, axis=1, keepdims=True) + EPSILON)
        grad = tmp[rows] + rcv_dn2[rows].astype(F32)
        sum_own[1:2] = sum_own[1:2] + jnp.sum(grad * mid * r2, axis=0, keepdims=True)
        s = grad * gain_full[1:2, :]
        res = dout[x, rows].astype(F32) + r2 * (s - mid * r2 * r2 * jnp.mean(s * mid, axis=1, keepdims=True))
        dmid[rows] = res
        dmid_low[rows] = res.astype(BF16)

    loop(8, (G_NORM2B, back_two), unroll=2)

    def dmerged_cols(k):
        w = attn[1, lax.div(k, 2), lax.rem(k, 2)].reshape(256, WIDTH)
        dmerged[:, cols(k)] = nt(dmid_low[...], w).astype(BF16)

    loop(4, (G_DMERGED, dmerged_cols), unroll=2)

    def grad_output(it):
        cc = jnp.where(it < 2, 1 - c, c)
        half = lax.rem(it, 2)
        g = nn(merged[:, cols(half * 2 + cc)].T, dmid_low[...])
        pattn[0, half, cc] = g.astype(BF16).reshape(4, 2, 32, WIDTH)

    loop(4, (G_OUTPUT, grad_output), at=(2,), unroll=2)

    drain("dn2")

    def attend_back(j):
        pair = cols(j, 128)
        k_pair, v_pair = keys[:, pair], values[:, pair]
        q, do = both(scaled(query[:, pair])), both(dmerged[:, pair])
        logsum = jnp.concatenate(
            [jnp.sum(jnp.where(head_lane == j * 2 + h, lse[...], 0.0), axis=1, keepdims=True) for h in (0, 1)], axis=0
        )
        probs = jnp.exp(nt(q, k_pair) + jnp.concatenate([bias[x]] * 2, axis=0) - logsum)
        dprobs = nt(do, v_pair)
        dvalues[:, pair] = tn(probs.astype(BF16), do).astype(BF16)
        row_sum = jnp.sum(probs * dprobs, axis=1, keepdims=True)
        dscores = (probs * (dprobs - row_sum)).astype(BF16)
        dq = nn(dscores, k_pair)
        dkeys[:, pair] = tn(dscores, q).astype(BF16)
        dquery[:, pair] = (jnp.where(low_half, dq[0:ROWS], dq[ROWS : 2 * ROWS]) * SCALE).astype(BF16)

    loop(8, (G_ATTENDB, attend_back), at=(4,), unroll=2)

    def other_first(it):
        cc = jnp.where(it < 2, 1 - c, c)
        return lax.rem(it, 2), cc

    def grad_query(it):
        half, cc = other_first(it)
        g = nn(normed[:, cols(half * 2 + cc)].T, dquery[...])
        pattn[1, half, cc] = g.astype(BF16).reshape(4, 2, 32, WIDTH)

    loop(4, (G_PROJQ, grad_query), at=(2,), unroll=2)

    def latent_back(g):
        dk, dv = dkeys[:, cols(g, 512)], dvalues[:, cols(g, 512)]
        dlatent[:, cols(g)] = (nt(dk, up_weight(g, 0)) + nt(dv, up_weight(g, 16))).astype(BF16)
        lat = latent[:, cols(g)].T
        pattn[2, g, :, :, :, pl.ds(0, 16), pl.ds(512, 512)] = nn(lat, dk).astype(BF16).reshape(2, 4, 2, 16, 512)
        pattn[2, g, :, :, :, pl.ds(16, 16), pl.ds(512, 512)] = nn(lat, dv).astype(BF16).reshape(2, 4, 2, 16, 512)

    loop(GROUPS, (G_LATENTB, latent_back))

    def grad_latent(it):
        half, cc = other_first(it)
        g = nn(normed[:, cols(half * 2 + cc)].T, dlatent[...])
        pattn[2, half, cc, :, :, :, pl.ds(0, 512)] = g.astype(BF16).reshape(4, 2, 32, 512)

    loop(4, (G_PROJL, grad_latent), at=(2,), unroll=2)

    def dnormed_cols(k):
        xx, cc = lax.div(k, 2), lax.rem(k, 2)
        part = nt(dquery[...], attn[0, xx, cc].reshape(256, WIDTH))
        part = part + nt(dlatent[...], latw[xx, cc, :, :, :, pl.ds(0, 512)].reshape(256, 512))
        tmp[pl.ds(0, ROWS), cols(k)] = part

    loop(4, (G_DNORMED, dnormed_cols), unroll=2)

    def back_one(k):
        rows = pl.ds(pl.multiple_of(k * 32, 32), 32)
        val = tok[x, rows].astype(F32)
        r1 = lax.rsqrt(jnp.mean(val * val, axis=1, keepdims=True) + EPSILON)
        grad = tmp[rows]
        sum_own[0:1] = sum_own[0:1] + jnp.sum(grad * val * r1, axis=0, keepdims=True)
        s = grad * gain_full[0:1, :]
        dmid[rows] = dmid[rows] + r1 * (s - val * r1 * r1 * jnp.mean(s * val, axis=1, keepdims=True))

    loop(8, (G_NORM1B, back_one), unroll=2)
    to_gtok = local(dmid, gtok_hbm, 0)
    to_gtok.start()
    gap(G_RESULT)

    def out_rows(k):
        rows = pl.ds(pl.multiple_of(k * 32, 32), 32)
        part = tmp[pl.ds(pl.multiple_of(ROWS + k * 32, 32), 32)]
        tok[x, rows] = (middle[rows] + (part + rcv_out[rows].astype(F32))).astype(BF16)

    drain("tok")
    loop(8, (G_RESULT, out_rows))
    to_out = local(tok.at[x], out_hbm, 1)
    to_out.start()
    gap(G_TAIL)
    to_gain = local(sum_own.at[:, pl.ds(pl.multiple_of((dp * 2 + lax.div(fs, 4)) * 128, 128), 128)], gain_hbm, 2)
    to_gain.start()
    for group in list(sent):
        drain(group)
    to_gtok.wait()
    to_out.wait()
    to_gain.wait()
    wait_out()


def finish_kernel(*refs):
    given, outs, bufs, casts = refs[:7], refs[7:19], refs[19:26], refs[26:36]
    in_sem, out_sem = refs[36:]
    takes = [pltpu.make_async_copy(src, dst, in_sem.at[k]) for k, (src, dst) in enumerate(zip(given, bufs))]
    gives = [pltpu.make_async_copy(src, dst, out_sem.at[k]) for k, (src, dst) in enumerate(zip([*bufs[:2], *casts], outs))]
    slow = []
    for k in (1, 0):
        for p in range(4):
            rows = pl.ds(p * 64, 64)
            slot = 4 * k + p
            come = pltpu.make_async_copy(given[k].at[rows], bufs[k].at[rows], in_sem.at[7 + slot])
            leave = pltpu.make_async_copy(bufs[k].at[rows], outs[k].at[rows], out_sem.at[12 + slot])
            come.start()
            slow.append((come, leave))
    for k in (4, 5, 6, 2, 3):
        takes[k].start()
    for come, leave in slow:
        come.wait()
        leave.start()
    _, _, at_ref, gain_ref, gg_ref, gu_ref, gd_ref = bufs
    gq_o, gl_o, gk_o, gv_o, go_o, ga_o, gf_o, gg_o, gu_o, gd_o = casts
    for k, src, dst in ((4, gg_ref, gg_o), (5, gu_ref, gu_o)):
        takes[k].wait()
        dst[:, 0:HALF] = src[0].astype(F32)
        dst[:, HALF : 2 * HALF] = src[1].astype(F32)
        gives[k + 5].start()
    takes[6].wait()
    gd = gd_ref[...].astype(F32)
    gd_o[:, 0:512] = gd[0:DOWN]
    gd_o[:, 512:WIDTH] = gd[DOWN : 2 * DOWN]
    gives[11].start()
    takes[2].wait()
    go_o[...] = at_ref[0].astype(F32)
    gq_o[...] = at_ref[1].astype(F32)
    gl_o[...] = at_ref[2, :, 0:512].astype(F32)
    gk_o[...] = at_ref[2, 0:16, 512:1024].astype(F32)
    gv_o[...] = at_ref[2, 16:32, 512:1024].astype(F32)
    takes[3].wait()
    place = lax.rem(lax.axis_index("fsdp"), 4)
    picked = sum(jnp.where(place == k, gain_ref[:, 32 * k : 32 * k + 32], 0.0) for k in range(4))
    ga_o[...] = picked[0:1]
    gf_o[...] = picked[1:2]
    for k in range(2, 9):
        gives[k].start()
    for give in [*gives[2:], *[leave for _, leave in slow]]:
        give.wait()


def kernel_on_device(
    tokens, seq_lengths, cotangent, w_query, w_latent, w_keyup, w_valup, w_output, norm_attn, norm_ffn,
    w_gate, w_up, w_down,
):
    hbm, vmem = pl.BlockSpec(memory_space=pl.ANY), pl.BlockSpec(memory_space=pltpu.VMEM)
    smem = pl.BlockSpec(memory_space=pltpu.SMEM)
    shape = jax.ShapeDtypeStruct
    outs = [
        shape((ROWS, WIDTH), BF16), shape((ROWS, WIDTH), F32), shape((3, 32, WIDTH), BF16), shape((8, 128), F32),
        shape((2, 32, HALF), BF16), shape((2, 32, HALF), BF16), shape((2 * DOWN, 512), BF16),
    ]
    V = pltpu.VMEM
    units = [(2 * DOWN, 512), *[(2, 32, width) for width in PARTS for _ in range(2)]]
    act = V((ROWS, WIDTH), BF16)
    scratch = [
        V((2, 2, 2, 4, 2, 32, WIDTH), BF16), V((2, 2, 4, 2, 32, WIDTH + 128), BF16),
        *[V((2, 4, 2, *unit), BF16) for unit in units[1:]],
        V((2, 4, 2, 2 * DOWN, 512), BF16), V((HALF, WIDTH), BF16), V((16, WIDTH), F32),
        V((2, ROWS, WIDTH), BF16), V((2, 8, 128), F32), V((2, ROWS, ROWS), F32), act, act, V((ROWS, 512), BF16), act, act, act, V((ROWS, 128), F32),
        V((ROWS, WIDTH), F32), V((2, ROWS, WIDTH), BF16), V((2, ROWS, WIDTH), BF16),
        V((512, HALF), BF16), V((512, HALF), BF16), V((512, HALF), BF16), V((ROWS + 768, WIDTH), F32),
        act, act, act,
        V((ROWS, WIDTH), F32), act, act, act, act, act, V((ROWS, 512), BF16),
        V((3, 2, 2, 4, 2, 32, WIDTH), BF16),
        *[V((2, 4, *unit), BF16) for unit in units],
        *[V((4, *unit), BF16) for unit in units],
        *[V((3, *unit), BF16) for unit in units],
        *[V(unit[1:], BF16) for unit in units[1:]],
        V((3, 2, 4, 2, 32, WIDTH), BF16), V((3, 4, 2, 32, WIDTH), BF16),
        V((3, 3, 2, 32, WIDTH), BF16), V((3, 32, WIDTH), BF16), V((8, WIDTH), F32), V((5, 8, WIDTH), F32),
        pltpu.SemaphoreType.DMA((2 * FFN + 14,)), pltpu.SemaphoreType.DMA((SLOTS.count,)), pltpu.SemaphoreType.DMA((PUT + 8 + 2 * FFN,)),
    ]
    res = pl.pallas_call(
        layer_kernel,
        out_shape=outs,
        in_specs=[hbm, smem, hbm, hbm, hbm, hbm, hbm, hbm, vmem, vmem, hbm, hbm, vmem],
        out_specs=[hbm] * len(outs),
        scratch_shapes=scratch,
        compiler_params=pltpu.CompilerParams(
            collective_id=0, has_side_effects=True, vmem_limit_bytes=63 * 2**20
        ),
    )(
        tokens, seq_lengths, cotangent, w_query, w_latent, w_keyup, w_valup, w_output, norm_attn, norm_ffn,
        w_gate, w_up, w_down,
    )
    final = [
        shape((ROWS, WIDTH), BF16), shape((ROWS, WIDTH), F32), shape((32, WIDTH), F32), shape((32, 512), F32),
        shape((16, 512), F32), shape((16, 512), F32), shape((32, WIDTH), F32), shape((1, 32), F32), shape((1, 32), F32),
        shape((32, 2 * HALF), F32), shape((32, 2 * HALF), F32), shape((DOWN, WIDTH), F32),
    ]
    out = pl.pallas_call(
        finish_kernel,
        out_shape=final,
        in_specs=[hbm] * 7,
        out_specs=[hbm] * 12,
        scratch_shapes=[
            *[V(one.shape, one.dtype) for one in [*outs, *final[2:]]],
            pltpu.SemaphoreType.DMA((15,)), pltpu.SemaphoreType.DMA((20,)),
        ],
    )(*res)
    return tuple(out[:7]) + (out[7].reshape(32), out[8].reshape(32)) + tuple(out[9:])


def solution(mesh):
    fits = dict(mesh.shape) == {"dp": 4, "fsdp": 8}
    return jax.shard_map(
        kernel_on_device if fits else on_device,
        mesh=mesh,
        in_specs=(
            P(("dp", "fsdp"), None),
            P(("dp", "fsdp")),
            P(("dp", "fsdp"), None),
            P(("dp", "fsdp"), None),
            P(("dp", "fsdp"), None),
            P(("dp", "fsdp"), None),
            P(("dp", "fsdp"), None),
            P(("dp", "fsdp"), None),
            P(("dp", "fsdp")),
            P(("dp", "fsdp")),
            P(("dp", "fsdp"), None),
            P(("dp", "fsdp"), None),
            P(("dp", "fsdp"), None),
        ),
        out_specs=(
            P(("dp", "fsdp"), None),
            P(("dp", "fsdp"), None),
            P(("dp", "fsdp"), None),
            P(("dp", "fsdp"), None),
            P(("dp", "fsdp"), None),
            P(("dp", "fsdp"), None),
            P(("dp", "fsdp"), None),
            P(("dp", "fsdp")),
            P(("dp", "fsdp")),
            P(("dp", "fsdp"), None),
            P(("dp", "fsdp"), None),
            P(("dp", "fsdp"), None),
        ),
        check_vma=False,
    )
```
